32 devices in a mesh: group: 2 (over y), expert: 4 (over x, core), dp: 4 (over z).
Axes of the slice: x: 2, y: 2, z: 4, core: 2. Of those that a mesh axis runs over, the one named last changes fastest.
Arguments:
- tokens: bfloat16 [1024, 2048], P(('group', 'expert'), 'dp'), parts along dimension 0, may hold values from -6 to 6
- expert_ids: int32 [1024, 8], P(('group', 'expert')), parts along dimension 0, may hold values from 0 to 15, all different within a row; in each aligned block of 128 rows (0 to 127, 128 to 255, ...) at most 80 rows name the same one
- combine: float32 [1024, 8], P(('group', 'expert')), parts along dimension 0, may hold values from 0.05 to 1
- gate_weight: bfloat16 [16, 2048, 768], P('expert', 'dp'), may hold values from -0.125 to 0.125
- up_weight: bfloat16 [16, 2048, 768], P('expert', 'dp'), may hold values from -0.125 to 0.125
- down_weight: bfloat16 [16, 768, 2048], P('expert', None, 'dp'), may hold values from -0.21875 to 0.21875
- out_grad: bfloat16 [1024, 2048], P(('group', 'expert'), 'dp'), parts along dimension 0, may hold values from -6 to 6
Outputs:
- layer_out: bfloat16 [1024, 2048], P(('group', 'expert'), 'dp'), parts along dimension 0
- token_grad: bfloat16 [1024, 2048], P(('group', 'expert'), 'dp'), parts along dimension 0
- gate_grad: bfloat16 [32, 2048, 768], P(('group', 'expert'), 'dp'), parts along dimension 0
- up_grad: bfloat16 [32, 2048, 768], P(('group', 'expert'), 'dp'), parts along dimension 0
- down_grad: bfloat16 [32, 768, 2048], P(('group', 'expert'), None, 'dp'), parts along dimension 0
- combine_grad: float32 [1024, 8], P(('group', 'expert')), parts along dimension 0
The draws below stay inside these ranges and needn't reach their ends.
There are 2 independent parts, one for each index of `group`. The reference program is written for one: setup_inputs(seed, part) draws one part's arguments, and reference() takes and returns one part's arrays. A program takes and returns all parts, laid end to end along the dimension named above; an argument that names none is the same for every part. Nothing has to cross between parts.
Inputs may be any that keep to these rules, and one draw needn't show every extreme that they name: `expert_ids`: each token names 8 different experts. Among the 128 tokens of one block no expert is named more than 80 times, and in some block one expert is named exactly 80 times.
All inputs are finite; a program needn't handle non-finite values.
Results may differ from the reference program's by a relative error of at most 0.019.
Values may be sent and summed in bfloat16 or wider, within the bound.
No kernel may reach another device: no remote copies, remote signals or barrier semaphores. Data moves between devices by JAX's collectives and lax.ppermute only.
A program may use at most 128 MiB of HBM per device.

```python
import math
import jax
import jax.numpy as jnp
import numpy as np
from jax import lax

D = 2048
FF = 768
TOP = 8
TOK_DEV = 128
EXPERTS = 16
CAP = 80
TOKENS = 512
N_EXPERT = 4
N_DP = 4


def level_of(key, dims, pieces, least, top_value):
    gain = 1.0
    for position, blocks in pieces:
        steps = jax.random.uniform(jax.random.fold_in(jax.random.fold_in(key, 6), position), (blocks,), jnp.float32, least / len(pieces), top_value / len(pieces))
        gain = gain * jnp.repeat(jnp.exp(steps), dims[position] // blocks).reshape((-1,) + (1,) * (len(dims) - 1 - position))
    return gain


def assign_block(own_key, own, number, rows, amount, top, bound, lean):
    ranking = jax.random.permutation(own_key, amount)
    heavy_load, usual = load_shares(amount, rows * top, bound, lean, True), load_shares(amount, rows * top, bound, lean, False)
    places = jnp.arange(amount)

    def named(lengths, offset_by):
        used = int((lengths > 0).sum())
        fixed = max(1, used // 4)
        moved = fixed + (places - fixed + offset_by * (used - fixed)) % max(1, amount - fixed)
        return jnp.zeros((amount,), jnp.int32).at[ranking[jnp.where(places < fixed, places, moved)]].set(jnp.asarray(lengths, jnp.int32))

    lengths = jnp.where(number % 4 == 0, named(heavy_load, number // 4), named(usual, number - number // 4 - 1))
    mixed = jax.random.permutation(jax.random.fold_in(own, 3), amount)
    source_of, taker = mixed[0:amount // 2 * 2:2], mixed[1:amount // 2 * 2:2]
    slack = jnp.minimum(lengths[source_of] - 1, bound - lengths[taker]) // 2
    slack = jnp.where((source_of == ranking[0]) | (taker == ranking[0]) | (lengths[taker] == 0), 0, jnp.maximum(slack, 0))
    moved = jax.random.randint(jax.random.fold_in(own, 4), (amount // 2,), 0, 1 << 20) % (slack + 1)
    lengths = lengths.at[source_of].add(-moved).at[taker].add(moved)
    items = jnp.searchsorted(jnp.cumsum(lengths), jnp.arange(rows * top), side="right").astype(jnp.int32)
    listing = items.reshape(top, rows).T
    listing = listing[jax.random.permutation(jax.random.fold_in(own, 1), rows)]
    offset_by = jax.random.randint(jax.random.fold_in(own, 2), (rows, 1), 0, top)
    return jnp.take_along_axis(listing, (jnp.arange(top)[None, :] + offset_by) % top, axis=1)


def load_shares(amount, total, most, slope, full):
    weights = [(1 << 20) // math.isqrt(grade ** slope) + 1 for grade in range(1, amount + 1)]
    largest = most if full else min(most, max(-(-total // amount), total * weights[0] // sum(weights)))
    least = 1 if total - largest >= amount - 1 else 0
    holding, spare = [largest] + [least] * (amount - 1), total - largest - least * (amount - 1)
    while spare > 0:
        free = [i for i in range(1, amount) if holding[i] < largest] or [i for i in range(1, amount) if holding[i] < most]
        mass, left = sum([weights[i] for i in free]), spare
        for i in free:
            addition = min(most - holding[i], max(1, left * weights[i] // mass), spare)
            holding[i] = holding[i] + addition
            spare = spare - addition
    return np.array(holding)


def scatter_about(stream_key, dims, width, most, cuts=(), held_as=jnp.bfloat16):
    result = jax.random.normal(stream_key, dims, jnp.float32) * width
    if len(cuts) > 0:
        result = level_of(stream_key, dims, cuts, -0.22, 0.18) * result
    return jnp.clip(result, min=-most, max=most).astype(held_as)


def setup_inputs(seed: int = 0, part: int = 0) -> dict:
    seeds = jax.random.split(jax.random.key(seed), 8)
    part_splits = jax.random.split(jax.random.fold_in(seeds[7], part), 8)
    tokens = scatter_about(part_splits[0], (TOKENS, D), 1.0, 6.0, ((0, 4), (1, 4)))
    expert_ids_keys = jax.random.split(jax.random.fold_in(part_splits[1], 1), TOKENS // TOK_DEV)
    expert_ids_turns = jax.random.permutation(jax.random.fold_in(part_splits[1], 3), TOKENS // TOK_DEV)
    expert_ids = jax.vmap(lambda own, number: assign_block(jax.random.fold_in(part_splits[1], 2), own, number, TOK_DEV, EXPERTS, TOP, CAP, 2))(expert_ids_keys, expert_ids_turns).reshape((TOKENS, TOP))
    combine = jnp.clip(jnp.exp(math.log(1.0) - 2.9957323 * jax.random.uniform(part_splits[2], (TOKENS, TOP), jnp.float32) ** level_of(part_splits[2], (TOKENS, TOP), ((0, 4),), -0.2, 0.2)), 0.05, 1.0)
    gate_weight = scatter_about(seeds[3], (EXPERTS, D, FF), D ** -0.5, 0.125, ((0, 4), (1, 4)))
    up_weight = scatter_about(seeds[4], (EXPERTS, D, FF), D ** -0.5, 0.125, ((0, 4), (1, 4)))
    down_weight = scatter_about(seeds[5], (EXPERTS, FF, D), FF ** -0.5, 0.21875, ((0, 4), (2, 4)))
    out_grad = scatter_about(part_splits[6], (TOKENS, D), 1.0, 6.0, ((0, 4), (1, 4)))
    return dict(tokens=tokens, expert_ids=expert_ids, combine=combine, gate_weight=gate_weight, up_weight=up_weight, down_weight=down_weight, out_grad=out_grad)


def rounded(value):
    return lax.optimization_barrier(value.astype(jnp.bfloat16)).astype(jnp.float32)


def shard_sum(parts):
    return jnp.sum(rounded(parts), axis=0)


def reference(tokens, expert_ids, combine, gate_weight, up_weight, down_weight, out_grad):
    local_width = D // N_DP
    pair_count = TOK_DEV * TOP
    buffer_rows = N_EXPERT * CAP
    blocked = expert_ids.reshape(N_EXPERT, pair_count)
    onehot = (blocked[:, :, None] == jnp.arange(EXPERTS, dtype=jnp.int32)[None, None, :]).astype(jnp.int32)
    before = jnp.cumsum(onehot, axis=1) - onehot
    slot_index = jnp.sum(before * onehot, axis=2).astype(jnp.int32)
    row_index = (jnp.arange(N_EXPERT, dtype=jnp.int32)[:, None] * CAP + slot_index).reshape(-1).astype(jnp.int32)
    expert_index = expert_ids.reshape(-1).astype(jnp.int32)
    token_index = (jnp.arange(TOKENS * TOP, dtype=jnp.int32) // TOP).astype(jnp.int32)
    inputs = jnp.zeros((EXPERTS, buffer_rows, D), jnp.bfloat16).at[expert_index, row_index].set(tokens[token_index])
    wide_grad = out_grad.astype(jnp.float32)
    scaled = (combine[:, :, None] * wide_grad[:, None, :]).astype(jnp.bfloat16).reshape(TOKENS * TOP, D)
    cotangent = jnp.zeros((EXPERTS, buffer_rows, D), jnp.bfloat16).at[expert_index, row_index].set(scaled)

    def one_expert(operands):
        expert_in, expert_cot, gate_matrix, up_matrix, down_matrix = operands
        split_in = expert_in.astype(jnp.float32).reshape(buffer_rows, N_DP, local_width)
        gate_total = shard_sum(jnp.einsum("rjd,jdf->jrf", split_in, gate_matrix.astype(jnp.float32).reshape(N_DP, local_width, FF)))
        up_total = shard_sum(jnp.einsum("rjd,jdf->jrf", split_in, up_matrix.astype(jnp.float32).reshape(N_DP, local_width, FF)))
        sigmoid_gate = jax.nn.sigmoid(gate_total)
        hidden = (gate_total * sigmoid_gate * up_total).astype(jnp.bfloat16)
        expert_out = jnp.dot(hidden, down_matrix, preferred_element_type=jnp.float32).astype(jnp.bfloat16)
        split_cot = expert_cot.astype(jnp.float32).reshape(buffer_rows, N_DP, local_width)
        hidden_delta = rounded(shard_sum(jnp.einsum("rjd,fjd->jrf", split_cot, down_matrix.astype(jnp.float32).reshape(FF, N_DP, local_width))))
        gate_delta = (hidden_delta * up_total * sigmoid_gate * (1.0 + gate_total * (1.0 - sigmoid_gate))).astype(jnp.bfloat16)
        up_delta = (hidden_delta * (gate_total * sigmoid_gate)).astype(jnp.bfloat16)
        down_step = jnp.dot(hidden.T, expert_cot, preferred_element_type=jnp.float32).astype(jnp.bfloat16)
        gate_step = jnp.dot(expert_in.T, gate_delta, preferred_element_type=jnp.float32).astype(jnp.bfloat16)
        up_step = jnp.dot(expert_in.T, up_delta, preferred_element_type=jnp.float32).astype(jnp.bfloat16)
        input_delta = (jnp.dot(gate_delta, gate_matrix.T, preferred_element_type=jnp.float32)
                       + jnp.dot(up_delta, up_matrix.T, preferred_element_type=jnp.float32)).astype(jnp.bfloat16)
        return expert_out, input_delta, gate_step, up_step, down_step

    results = lax.map(one_expert, (inputs, cotangent, gate_weight, up_weight, down_weight))
    expert_outs, input_deltas, gate_grad, up_grad, down_grad = results
    picked = expert_outs[expert_index, row_index].astype(jnp.float32).reshape(TOKENS, TOP, D)
    layer_out = jnp.sum(combine[:, :, None] * picked, axis=1).astype(jnp.bfloat16)
    combine_grad = jnp.sum(picked * wide_grad[:, None, :], axis=2)
    returned = input_deltas[expert_index, row_index].astype(jnp.float32).reshape(TOKENS, TOP, D)
    token_grad = jnp.sum(returned, axis=1).astype(jnp.bfloat16)
    return (layer_out, token_grad, gate_grad, up_grad, down_grad, combine_grad)
```

```python
import functools

import jax
import jax.numpy as jnp
from jax import lax
from jax.experimental import pallas as pl
from jax.experimental.pallas import tpu as pltpu
from jax.sharding import PartitionSpec as P

F32, BF16 = jnp.float32, jnp.bfloat16
VMEM_BYTES = 48 << 20


def line_pairs(n, gather, step):
    if gather:
        senders = [i for i in range(step - 1, n - 1)]
    else:
        senders = [i for i in range(0, min(step, n - 1))]
    right = [(i, i + 1) for i in senders]
    left = [(n - 1 - i, n - 2 - i) for i in senders]
    return right, left


class Line:
    def __init__(self, axis, n, stride):
        self.axis, self.n, self.stride = axis, n, stride

    def send(self, value, pairs):
        wide = [
            (a * self.stride + c, b * self.stride + c) for a, b in pairs for c in range(self.stride)
        ]
        return lax.ppermute(value, self.axis, wide)

    def gather(self, own):
        n = self.n
        if n == 2:
            both = self.send(own, [(0, 1), (1, 0)])
            return [(both, both)]
        right, left, rights, lefts = own, own, [], []
        for step in range(1, n):
            pairs_r, pairs_l = line_pairs(n, True, step)
            right, left = self.send(right, pairs_r), self.send(left, pairs_l)
            rights.append(right)
            lefts.append(left)
        return [(rights[q - 1], lefts[n - q - 1]) for q in range(1, n)]

    def scatter(self, parts, add):
        n = self.n
        if n == 2:
            return self.send(parts[1], [(0, 1), (1, 0)]), None
        right, left = parts[1], parts[n - 1]
        for step in range(1, n):
            pairs_r, pairs_l = line_pairs(n, False, step)
            right, left = self.send(right, pairs_r), self.send(left, pairs_l)
            if step < n - 1:
                right, left = add(parts[step + 1], right), add(parts[n - 1 - step], left)
        return right, left


def add_rounded(a, b):
    return (a.astype(F32) + b.astype(F32)).astype(BF16)


def dot(a, b, dims=((1,), (0,))):
    return lax.dot_general(a, b, (dims, ((), ())), preferred_element_type=F32)


def place_of(scal, q, n, chips):
    block = lax.rem(scal[0] - q + n, n)
    core = lax.rem(lax.rem(block, 2) + scal[2], 2)
    return core * chips + lax.rem(scal[1] - block // 2 + chips, chips)


def routing(scal, w_ref, expert, n, rows):
    chips, (experts_all, tokens) = w_ref.shape[0] // 2, w_ref.shape[1:]
    local = experts_all // (2 * chips)
    which = (scal[1] * 2 + scal[2]) * local + expert
    ids = lax.broadcasted_iota(jnp.int32, (experts_all, tokens), 0)
    places = [place_of(scal, q, n, chips) for q in range(n)]
    weights = jnp.concatenate(
        [jnp.sum(jnp.where(ids == which, w_ref[p], 0.0), axis=0, keepdims=True) for p in places],
        axis=0,
    )
    chosen = weights > 0.0
    earlier = lax.broadcasted_iota(jnp.int32, (tokens, tokens), 0) < lax.broadcasted_iota(
        jnp.int32, (tokens, tokens), 1
    )
    slots = dot(chosen.astype(F32).astype(BF16), earlier.astype(F32).astype(BF16))
    slots = jnp.where(chosen, slots, -1.0).astype(jnp.int32)
    row = lax.broadcasted_iota(jnp.int32, (rows, tokens), 0)
    return [(places[q], weights[q : q + 1], row == slots[q : q + 1]) for q in range(n)]


def pre_kernel(n, expert, scal, w_ref, tok_ref, og_ref, gw, uw, dw, in_ref, cot_ref, *outs):
    rows = in_ref.shape[0] // n

    @pl.when(pl.program_id(0) == 0)
    def _():
        for q, (place, weight, hit) in enumerate(routing(scal, w_ref, expert, n, rows)):
            pick = hit.astype(F32).astype(BF16)
            span = pl.ds(q * rows, rows)
            in_ref[span, :] = dot(pick, tok_ref[place]).astype(BF16)
            scale = jnp.sum(jnp.where(hit, weight, 0.0), axis=1, keepdims=True)
            cot_ref[span, :] = (dot(pick, og_ref[place]) * scale).astype(BF16)

    tile = gw.shape[2]
    gate = dot(in_ref[...], gw[0]).astype(BF16).reshape(n, rows, tile)
    up = dot(in_ref[...], uw[0]).astype(BF16).reshape(n, rows, tile)
    back = dot(cot_ref[...], dw[0], ((1,), (1,))).astype(BF16).reshape(n, rows, tile)
    for q in range(n):
        outs[q][0] = gate[q]
        outs[q][1] = up[q]
        outs[q][2] = back[q]


def mid_kernel(own, right, left, out, product):
    total = own[...].astype(F32) + right[...].astype(F32) + left[...].astype(F32)
    gate, up, back = total[0], total[1], total[2]
    sig = jax.nn.sigmoid(gate)
    hidden = (gate * sig * up).astype(BF16)
    delta = back.astype(BF16).astype(F32)
    out[0] = hidden
    out[1] = (delta * up * sig * (1.0 + gate * (1.0 - sig))).astype(BF16)
    out[2] = (delta * (gate * sig)).astype(BF16)
    prod = hidden.astype(F32) * back
    lanes = product.shape[1]
    acc = prod[:, 0:lanes]
    for k in range(1, prod.shape[1] // lanes):
        acc = acc + prod[:, k * lanes : (k + 1) * lanes]
    product[...] = acc


def load_rows(scal, n, which, pieces):
    own, rest = pieces[0], pieces[1:]
    values = [own[which]]
    for q in range(1, n):
        values.append(jnp.where(scal[0] >= q, rest[2 * q - 2][which], rest[2 * q - 1][which]))
    return jnp.concatenate(values, axis=0)


def out_kernel(n, expert, has_prev, scal, w_ref, *refs):
    if has_prev:
        prev, refs = refs[0], refs[1:]
    pieces, refs = refs[: 2 * n - 1], refs[2 * n - 1 :]
    gw, uw, dw, out, eo, idl = refs
    step = pl.program_id(0)

    @pl.when(step == 0)
    def _():
        eo[...] = jnp.zeros_like(eo)
        idl[...] = jnp.zeros_like(idl)

    eo[...] += dot(load_rows(scal, n, 0, pieces), dw[0])
    idl[...] += dot(load_rows(scal, n, 1, pieces), gw[0], ((1,), (1,))) + dot(
        load_rows(scal, n, 2, pieces), uw[0], ((1,), (1,))
    )

    @pl.when(step == pl.num_programs(0) - 1)
    def _():
        rows = eo.shape[0] // n
        for q, (place, weight, hit) in enumerate(routing(scal, w_ref, expert, n, rows)):
            pick = hit.astype(F32)
            scaled = (pick * weight).astype(BF16)
            span = pl.ds(q * rows, rows)
            layer = dot(scaled, eo[span, :].astype(BF16), ((0,), (0,)))
            token = dot(pick.astype(BF16), idl[span, :].astype(BF16), ((0,), (0,)))
            if has_prev:
                layer, token = layer + prev[place, 0], token + prev[place, 1]
            out[place, 0] = layer.astype(out.dtype)
            out[place, 1] = token.astype(out.dtype)


def grad_kernel(n, has_prev, scal, in_ref, cot_ref, *refs):
    pieces, refs = refs[: 2 * n - 1], refs[2 * n - 1 :]
    if has_prev:
        refs = refs[3:]
    gg, ug, dg = refs
    gg[0] = dot(in_ref[...], load_rows(scal, n, 1, pieces), ((0,), (0,))).astype(BF16)
    ug[0] = dot(in_ref[...], load_rows(scal, n, 2, pieces), ((0,), (0,))).astype(BF16)
    dg[0] = dot(load_rows(scal, n, 0, pieces), cot_ref[...], ((0,), (0,))).astype(BF16)


def whole_spec(shape):
    return pl.BlockSpec(tuple(shape), lambda g: (0,) * len(shape))


SMEM_SPEC = pl.BlockSpec(memory_space=pltpu.SMEM)


def call(kernel, grid, in_specs, out_specs, out_shape, flops, moved, **rest):
    return pl.pallas_call(
        kernel,
        grid=(grid,),
        in_specs=in_specs,
        out_specs=out_specs,
        out_shape=out_shape,
        compiler_params=pltpu.CompilerParams(vmem_limit_bytes=VMEM_BYTES),
        cost_estimate=pl.CostEstimate(flops=flops, bytes_accessed=moved, transcendentals=0),
        **rest,
    )


def body(tokens, expert_ids, combine, gate_weight, up_weight, down_weight, out_grad):
    peers, n = lax.axis_size("expert"), lax.axis_size("dp")
    assert peers == n
    chips = peers // 2
    local, width, hidden = gate_weight.shape
    count, choose = expert_ids.shape
    experts_all = peers * local
    capacity = count * choose * 5 // (4 * experts_all)
    rows = -(-capacity // 16) * 16
    all_rows = n * rows
    tile = 256
    grid = hidden // tile
    me = lax.axis_index("expert")
    scal = jnp.stack([lax.axis_index("dp"), me // 2, lax.rem(me, 2)]).astype(jnp.int32)

    ids_t, combine_t = expert_ids.T, combine.T
    named = ids_t[:, None, :] == jnp.arange(experts_all, dtype=jnp.int32)[None, :, None]
    dense = jnp.sum(jnp.where(named, combine_t[:, None, :], 0.0), axis=0)

    along_x, across = Line("expert", chips, 2), Line("expert", peers, 1)
    swap = [(2 * x + c, 2 * x + 1 - c) for x in range(chips) for c in range(2)]

    def gather_blocks(own):
        others = along_x.gather(own)
        here = [own] + [
            right if right is left else jnp.where(scal[1] >= q + 1, right, left)
            for q, (right, left) in enumerate(others)
        ]
        there = [across.send(piece, swap) for piece in here]
        return jnp.stack(here + there)

    w_all = gather_blocks(dense)
    tok_all = gather_blocks(tokens)
    og_all = gather_blocks(out_grad)

    mac = all_rows * width * hidden
    weight_bytes = 2 * width * hidden
    piece_shape = jax.ShapeDtypeStruct((3, rows, hidden), BF16)
    piece_spec = pl.BlockSpec((3, rows, tile), lambda g: (0, 0, g))
    slot_shape = jax.ShapeDtypeStruct((all_rows, width), BF16)
    slot_spec = whole_spec((all_rows, width))

    def weight_specs(e):
        wide = pl.BlockSpec((1, width, tile), lambda g: (e, 0, g))
        return [wide, wide, pl.BlockSpec((1, tile, width), lambda g: (e, g, 0))]

    along_z = Line("dp", n, 1)
    arrived, totals = [], []
    for e in range(local):
        inputs, cot, *parts = call(
            functools.partial(pre_kernel, n, e),
            grid,
            [SMEM_SPEC, whole_spec(w_all.shape), whole_spec(tok_all.shape), whole_spec(og_all.shape)]
            + weight_specs(e),
            [slot_spec] * 2 + [piece_spec] * n,
            [slot_shape] * 2 + [piece_shape] * n,
            6 * mac,
            3 * weight_bytes + 5 * 2 * all_rows * hidden,
        )(scal, w_all, tok_all, og_all, gate_weight, up_weight, down_weight)
        arrived.append((inputs, cot))
        totals.append((parts[0], *along_z.scatter(parts, add_rounded)))

    products, grads, partial_sums = [], None, None
    for e in range(local):
        own, product = call(
            mid_kernel,
            1,
            [whole_spec(piece_shape.shape)] * 3,
            [whole_spec(piece_shape.shape), whole_spec((rows, 128))],
            [piece_shape, jax.ShapeDtypeStruct((rows, 128), F32)],
            20 * rows * hidden,
            24 * rows * hidden,
        )(*totals[e])
        products.append(product)
        pieces = [own]
        for right, left in along_z.gather(own):
            pieces += [right, left]
        piece_specs = [piece_spec] * len(pieces)
        last = e == local - 1
        sum_shape = (2 * chips, 2, count, width)
        partial_sums = call(
            functools.partial(out_kernel, n, e, e > 0),
            grid,
            [SMEM_SPEC, whole_spec(w_all.shape)]
            + ([whole_spec(sum_shape)] if e > 0 else [])
            + piece_specs
            + weight_specs(e),
            whole_spec(sum_shape),
            jax.ShapeDtypeStruct(sum_shape, BF16 if last else F32),
            6 * mac,
            3 * weight_bytes + 9 * 2 * all_rows * hidden,
            scratch_shapes=[pltpu.VMEM((all_rows, width), F32)] * 2,
        )(
            scal,
            w_all,
            *([partial_sums] if e > 0 else []),
            *pieces,
            gate_weight,
            up_weight,
            down_weight,
        )
        inputs, cot = arrived[e]
        base = 3 + len(pieces)
        grads = call(
            functools.partial(grad_kernel, n, e > 0),
            grid,
            [SMEM_SPEC, slot_spec, slot_spec]
            + piece_specs
            + ([pl.BlockSpec(memory_space=pl.ANY)] * 3 if e > 0 else []),
            weight_specs(e),
            [
                jax.ShapeDtypeStruct(gate_weight.shape, BF16),
                jax.ShapeDtypeStruct(up_weight.shape, BF16),
                jax.ShapeDtypeStruct(down_weight.shape, BF16),
            ],
            6 * mac,
            3 * weight_bytes + 8 * 2 * all_rows * hidden,
            input_output_aliases={base + k: k for k in range(3)} if e > 0 else {},
        )(scal, inputs, cot, *pieces, *(grads if e > 0 else []))

    near, far = partial_sums[:chips], partial_sums[chips:]
    near = add_rounded(near, across.send(far, swap))
    right, left = along_x.scatter([near[q] for q in range(chips)], add_rounded)
    home = near[0].astype(F32) + right.astype(F32)
    if left is not None:
        home = home + left.astype(F32)
    home = home.astype(BF16)

    own_products = jnp.sum(jnp.stack(products), axis=2)
    all_products = lax.all_gather(own_products, ("expert", "dp"), axis=0, tiled=False)
    all_products = all_products.reshape(peers, n, local, rows)
    mine = lax.dynamic_index_in_dim(all_products, me, 1, keepdims=False).reshape(experts_all, rows)
    chosen = dense > 0.0
    earlier = (jnp.arange(count)[:, None] < jnp.arange(count)[None, :]).astype(BF16)
    slots = jnp.dot(chosen.astype(BF16), earlier, preferred_element_type=F32).astype(jnp.int32)
    at_slot = slots[:, None, :] == jnp.arange(rows, dtype=jnp.int32)[None, :, None]
    per_expert = jnp.sum(jnp.where(at_slot, mine[:, :, None], 0.0), axis=1)
    combine_grad = jnp.sum(jnp.where(named, per_expert[None], 0.0), axis=1) / combine_t
    return (home[0], home[1], *grads, combine_grad.T)


def solution(mesh):
    return jax.shard_map(
        body,
        mesh=mesh,
        in_specs=(
            P(("group", "expert"), "dp"),
            P(("group", "expert"), None),
            P(("group", "expert"), None),
            P("expert", "dp", None),
            P("expert", "dp", None),
            P("expert", None, "dp"),
            P(("group", "expert"), "dp"),
        ),
        out_specs=(
            P(("group", "expert"), "dp"),
            P(("group", "expert"), "dp"),
            P(("group", "expert"), "dp", None),
            P(("group", "expert"), "dp", None),
            P(("group", "expert"), None, "dp"),
            P(("group", "expert"), None),
        ),
        check_vma=False,
    )
```

```python
import functools

import jax
import jax.numpy as jnp
from jax import lax
from jax.experimental import pallas as pl
from jax.experimental.pallas import tpu as pltpu
from jax.sharding import PartitionSpec as P

F32, BF16 = jnp.float32, jnp.bfloat16
VMEM_BYTES = 48 << 20


def line_pairs(n, gather, step):
    if gather:
        senders = [i for i in range(step - 1, n - 1)]
    else:
        senders = [i for i in range(0, min(step, n - 1))]
    right = [(i, i + 1) for i in senders]
    left = [(n - 1 - i, n - 2 - i) for i in senders]
    return right, left


class Line:
    def __init__(self, axis, n, stride):
        self.axis, self.n, self.stride = axis, n, stride

    def send(self, value, pairs):
        wide = [
            (a * self.stride + c, b * self.stride + c) for a, b in pairs for c in range(self.stride)
        ]
        return lax.ppermute(value, self.axis, wide)

    def gather(self, own):
        n = self.n
        if n == 2:
            both = self.send(own, [(0, 1), (1, 0)])
            return [(both, both)]
        right, left, rights, lefts = own, own, [], []
        for step in range(1, n):
            pairs_r, pairs_l = line_pairs(n, True, step)
            right, left = self.send(right, pairs_r), self.send(left, pairs_l)
            rights.append(right)
            lefts.append(left)
        return [(rights[q - 1], lefts[n - q - 1]) for q in range(1, n)]

    def scatter(self, parts, add):
        n = self.n
        if n == 2:
            return self.send(parts[1], [(0, 1), (1, 0)]), None
        right, left = parts[1], parts[n - 1]
        for step in range(1, n):
            pairs_r, pairs_l = line_pairs(n, False, step)
            right, left = self.send(right, pairs_r), self.send(left, pairs_l)
            if step < n - 1:
                right, left = add(parts[step + 1], right), add(parts[n - 1 - step], left)
        return right, left


def add_rounded(a, b):
    return (a.astype(F32) + b.astype(F32)).astype(BF16)


def dot(a, b, dims=((1,), (0,))):
    return lax.dot_general(a, b, (dims, ((), ())), preferred_element_type=F32)


def routing(scal, w_refs, expert, rows):
    n = len(w_refs)
    experts_all, tokens = w_refs[0].shape
    ids = lax.broadcasted_iota(jnp.int32, (experts_all, tokens), 0)
    which = scal[2 * n] + expert
    weights = jnp.concatenate(
        [jnp.sum(jnp.where(ids == which, w[...], 0.0), axis=0, keepdims=True) for w in w_refs],
        axis=0,
    )
    chosen = weights > 0.0
    earlier = lax.broadcasted_iota(jnp.int32, (tokens, tokens), 0) < lax.broadcasted_iota(
        jnp.int32, (tokens, tokens), 1
    )
    slots = dot(chosen.astype(F32).astype(BF16), earlier.astype(F32).astype(BF16))
    slots = jnp.where(chosen, slots, -1.0).astype(jnp.int32)
    row = lax.broadcasted_iota(jnp.int32, (rows, tokens), 0)
    return [(scal[k], weights[k : k + 1], row == slots[k : k + 1]) for k in range(n)]


def span_of(position, rows):
    return pl.ds(pl.multiple_of(position * rows, rows), rows)


def pre_kernel(n, expert, deps, scal, *refs):
    refs = refs[deps:]
    w_refs, packs, refs = refs[:n], refs[n : 2 * n], refs[2 * n :]
    gw, uw, dw, in_ref, cot_ref, *outs = refs
    rows = in_ref.shape[0] // n
    half = pl.program_id(0)

    @pl.when(half == 0)
    def _():
        for k, (position, weight, hit) in enumerate(routing(scal, w_refs, expert, rows)):
            pick = hit.astype(F32).astype(BF16)
            span = span_of(position, rows)
            in_ref[span, :] = dot(pick, packs[k][0]).astype(BF16)
            scale = jnp.sum(jnp.where(hit, weight, 0.0), axis=1, keepdims=True)
            cot_ref[span, :] = (dot(pick, packs[k][1]) * scale).astype(BF16)

    gate = dot(in_ref[...], gw[0]).astype(BF16)
    up = dot(in_ref[...], uw[0]).astype(BF16)
    back = dot(cot_ref[...], dw[0], ((1,), (1,))).astype(BF16)
    for h in range(2):

        @pl.when(half == h)
        def _():
            for p in range(n):
                for k, value in enumerate((gate, up, back)):
                    outs[h * n + p][k] = value[p * rows : (p + 1) * rows]


def mid_kernel(deps, *refs):
    own, right, left, out, product = refs[deps:]
    total = own[...].astype(F32) + right[...].astype(F32) + left[...].astype(F32)
    gate, up, back = total[0], total[1], total[2]
    sig = jax.nn.sigmoid(gate)
    hidden = (gate * sig * up).astype(BF16)
    delta = back.astype(BF16).astype(F32)
    out[0] = hidden
    out[1] = (delta * up * sig * (1.0 + gate * (1.0 - sig))).astype(BF16)
    out[2] = (delta * (gate * sig)).astype(BF16)
    prod = hidden.astype(F32) * back
    lanes = product.shape[1]
    acc = prod[:, 0:lanes]
    for k in range(1, prod.shape[1] // lanes):
        acc = acc + prod[:, k * lanes : (k + 1) * lanes]
    product[...] = acc


def step_kernel(deps, select, add, scal, *refs):
    refs = list(refs[deps:])
    ins, outs = refs[: 2 * (select + add)], refs[2 * (select + add) :]
    if select:
        a, b, out = ins[0], ins[1], outs[0]
        out[...] = jnp.where(scal[scal.shape[0] - 1] > 0, a[...], b[...])
    if add:
        for k in range(add):
            a, b = ins[2 * (select + k)], ins[2 * (select + k) + 1]
            outs[select + k][...] = (a[...].astype(F32) + b[...].astype(F32)).astype(BF16)


def load_rows(scal, n, which, pieces):
    values = [pieces[0][which]]
    for q, pair in enumerate(pieces[1:], 1):
        if len(pair) == 1:
            values.append(pair[0][which])
        else:
            values.append(jnp.where(scal[n + q] > 0, pair[0][which], pair[1][which]))
    return jnp.concatenate(values, axis=0)


def split_pieces(refs, sizes):
    halves, at = [], 0
    for _ in range(2):
        pieces = [refs[at]]
        at += 1
        for size in sizes:
            pieces.append(refs[at : at + size])
            at += size
        halves.append(pieces)
    return halves, refs[at:]


def out_kernel(n, expert, has_prev, sizes, scal, *refs):
    w_refs, refs = refs[:n], refs[n:]
    if has_prev:
        prev, refs = refs[:2], refs[2:]
    halves, refs = split_pieces(refs, sizes)
    gw, uw, dw, near, far, token, eo, idl = refs
    step = pl.program_id(0)

    for h in range(2):

        @pl.when(step == h)
        def _():
            layer = dot(load_rows(scal, n, 0, halves[h]), dw[0])
            back = dot(load_rows(scal, n, 1, halves[h]), gw[0], ((1,), (1,))) + dot(
                load_rows(scal, n, 2, halves[h]), uw[0], ((1,), (1,))
            )
            eo[...] = layer if h == 0 else eo[...] + layer
            idl[...] = back if h == 0 else idl[...] + back

    @pl.when(step == 1)
    def _():
        rows = eo.shape[0] // n
        for k, (position, weight, hit) in enumerate(routing(scal, w_refs, expert, rows)):
            pick = hit.astype(F32)
            scaled = (pick * weight).astype(BF16)
            span = span_of(position, rows)
            layer = dot(scaled, eo[span, :].astype(BF16), ((0,), (0,)))
            back = dot(pick.astype(BF16), idl[span, :].astype(BF16), ((0,), (0,)))
            which, place = (near, k) if k < n // 2 else (far, k - n // 2)
            if has_prev:
                before = prev[0 if k < n // 2 else 1]
                layer, back = layer + before[place, 0], back + before[place, 1]
            which[place, 0] = layer.astype(which.dtype)
            which[place, 1] = back.astype(which.dtype)
        token[...] = jnp.zeros_like(token)


def grad_kernel(n, has_prev, sizes, scal, in_ref, cot_ref, *refs):
    halves, refs = split_pieces(refs, sizes)
    if has_prev:
        refs = refs[3:]
    gg, ug, dg, token = refs
    step = pl.program_id(0)
    token[...] = jnp.zeros_like(token)
    for h in range(2):

        @pl.when(step == h)
        def _():
            gg[0] = dot(in_ref[...], load_rows(scal, n, 1, halves[h]), ((0,), (0,))).astype(BF16)
            ug[0] = dot(in_ref[...], load_rows(scal, n, 2, halves[h]), ((0,), (0,))).astype(BF16)
            dg[0] = dot(load_rows(scal, n, 0, halves[h]), cot_ref[...], ((0,), (0,))).astype(BF16)


def home_kernel(n, local, sizes, scal, *refs):
    w_refs, own, refs = refs[:n], refs[n], refs[n + 1 :]
    pairs = []
    for size in sizes:
        pairs.append(refs[:size])
        refs = refs[size:]
    near, far, held = refs
    held[0] = own[...]
    for q, pair in enumerate(pairs, 1):
        held[q] = (
            pair[0][...]
            if len(pair) == 1
            else jnp.where(scal[n + q] > 0, pair[0][...], pair[1][...])
        )
    experts_all, tokens = w_refs[0].shape
    ids = lax.broadcasted_iota(jnp.int32, (experts_all, tokens), 0)
    sums = [jnp.zeros((experts_all, tokens), F32) for _ in range(n)]
    for e in range(local):
        for k, (position, _, hit) in enumerate(routing(scal, w_refs, e, own.shape[0])):
            column = held[position][:, e : e + 1]
            value = jnp.sum(jnp.where(hit, column, 0.0), axis=0, keepdims=True)
            sums[k] = sums[k] + jnp.where(ids == scal[2 * n] + e, value, 0.0)
    for k in range(n):
        if k < n // 2:
            near[k] = sums[k]
        else:
            far[k - n // 2] = sums[k]


def whole_spec(shape):
    return pl.BlockSpec(tuple(shape), lambda g: (0,) * len(shape))


def spec_of(array):
    return whole_spec(array.shape)


def like(shape, dtype=BF16):
    return jax.ShapeDtypeStruct(tuple(shape), dtype)


SMEM_SPEC = pl.BlockSpec(memory_space=pltpu.SMEM)
ANY_SPEC = pl.BlockSpec(memory_space=pl.ANY)
TOKEN = (8, 128)


def call(kernel, grid, in_specs, out_specs, out_shape, flops, moved, **rest):
    return pl.pallas_call(
        kernel,
        grid=(grid,),
        in_specs=in_specs,
        out_specs=out_specs,
        out_shape=out_shape,
        compiler_params=pltpu.CompilerParams(vmem_limit_bytes=VMEM_BYTES),
        cost_estimate=pl.CostEstimate(flops=flops, bytes_accessed=moved, transcendentals=0),
        **rest,
    )


def body(tokens, expert_ids, combine, gate_weight, up_weight, down_weight, out_grad):
    peers, n = lax.axis_size("expert"), lax.axis_size("dp")
    assert peers == n
    chips = peers // 2
    local, width, hidden = gate_weight.shape
    count, choose = expert_ids.shape
    experts_all = peers * local
    capacity = count * choose * 5 // (4 * experts_all)
    rows = -(-capacity // 16) * 16
    all_rows = n * rows
    tile = hidden // 2
    swaps = n == 4

    me, here = lax.axis_index("expert"), lax.axis_index("dp")
    at_end = (here == 0) | (here == n - 1)
    table = []
    for place in range(n):
        block = 2 * lax.rem(me // 2 - place % chips + chips, chips) + lax.rem(
            lax.rem(me, 2) + place // chips, 2
        )
        if swaps:
            across_middle = jnp.where((block == 0) | (block == 3), 3, 2)
            position = jnp.where(
                block == here, 0, jnp.where(block // 2 == here // 2, 1, across_middle)
            )
        else:
            position = lax.rem(here - block + n, n)
        table.append(position)
    flags = [at_end if swaps else here >= q for q in range(n)]
    scal = jnp.stack(
        [jnp.asarray(v).astype(jnp.int32) for v in table + flags + [me * local, at_end]]
    )

    ids_t, combine_t = expert_ids.T, combine.T
    named = ids_t[:, None, :] == jnp.arange(experts_all, dtype=jnp.int32)[None, :, None]
    dense = jnp.sum(jnp.where(named, combine_t[:, None, :], 0.0), axis=0)

    along_x, across = Line("expert", chips, 2), Line("expert", peers, 1)
    swap = [(2 * x + c, 2 * x + 1 - c) for x in range(chips) for c in range(2)]

    def gather_blocks(own):
        found = [own] + [
            right if right is left else jnp.where(me // 2 >= q, right, left)
            for q, (right, left) in enumerate(along_x.gather(own), 1)
        ]
        return found + [across.send(piece, swap) for piece in found]

    packs = gather_blocks(jnp.stack([tokens, out_grad]))
    w_all = gather_blocks(dense)
    w_specs, pack_specs = [spec_of(w) for w in w_all], [spec_of(p) for p in packs]

    mac = all_rows * width * hidden
    weight_bytes = 2 * width * hidden
    piece_shape = (3, rows, tile)
    piece_bytes = 2 * 3 * rows * tile
    slot_shape = (all_rows, width)

    def weight_specs(e):
        wide = pl.BlockSpec((1, width, tile), lambda g: (e, 0, g))
        return [wide, wide, pl.BlockSpec((1, tile, width), lambda g: (e, g, 0))]

    def pre(e, deps):
        inputs, cot, *parts = call(
            functools.partial(pre_kernel, n, e, len(deps)),
            2,
            [SMEM_SPEC] + [ANY_SPEC] * len(deps) + w_specs + pack_specs + weight_specs(e),
            [whole_spec(slot_shape)] * 2 + [whole_spec(piece_shape)] * (2 * n),
            [like(slot_shape)] * 2 + [like(piece_shape)] * (2 * n),
            6 * mac,
            3 * weight_bytes + 2 * n * piece_bytes,
        )(scal, *deps, *w_all, *packs, gate_weight, up_weight, down_weight)
        return (inputs, cot), [parts[:n], parts[n:]]

    def mid(own, right, left, deps):
        return call(
            functools.partial(mid_kernel, len(deps)),
            1,
            [ANY_SPEC] * len(deps) + [whole_spec(piece_shape)] * 3,
            [whole_spec(piece_shape), whole_spec((rows, 128))],
            [like(piece_shape), like((rows, 128), F32)],
            20 * rows * tile,
            4 * piece_bytes,
        )(*deps, own, right, left)

    def step(select, adds, deps=()):
        pairs = ([select] if select is not None else []) + list(adds)
        flat = [x for pair in pairs for x in pair]
        return call(
            functools.partial(step_kernel, len(deps), int(select is not None), len(adds)),
            1,
            [SMEM_SPEC] + [ANY_SPEC] * len(deps) + [whole_spec(piece_shape)] * len(flat),
            [whole_spec(piece_shape)] * len(pairs),
            [like(piece_shape)] * len(pairs),
            3 * rows * tile * len(pairs),
            3 * piece_bytes * len(pairs),
        )(scal, *deps, *flat)

    def flatten(halves):
        return [x for pieces in halves for group in pieces for x in group]

    def sizes_of(pieces):
        return [len(group) for group in pieces[1:]]

    def out(e, halves, prev):
        flat = flatten(halves)
        sum_shape = (chips, 2, count, width)
        return call(
            functools.partial(out_kernel, n, e, e > 0, sizes_of(halves[0])),
            2,
            [SMEM_SPEC]
            + w_specs
            + ([whole_spec(sum_shape)] * 2 if e > 0 else [])
            + [whole_spec(piece_shape)] * len(flat)
            + weight_specs(e),
            [whole_spec(sum_shape)] * 2 + [whole_spec(TOKEN)],
            [like(sum_shape, BF16 if e == local - 1 else F32)] * 2 + [like(TOKEN, F32)],
            6 * mac,
            3 * weight_bytes + len(flat) * piece_bytes,
            scratch_shapes=[pltpu.VMEM(slot_shape, F32)] * 2,
        )(scal, *w_all, *prev, *flat, gate_weight, up_weight, down_weight)

    def grad(e, slots, halves, prev):
        flat = flatten(halves)
        base = 3 + len(flat)
        return call(
            functools.partial(grad_kernel, n, e > 0, sizes_of(halves[0])),
            2,
            [SMEM_SPEC]
            + [whole_spec(slot_shape)] * 2
            + [whole_spec(piece_shape)] * len(flat)
            + ([ANY_SPEC] * 3 if e > 0 else []),
            weight_specs(e) + [whole_spec(TOKEN)],
            [like(w.shape) for w in (gate_weight, up_weight, down_weight)] + [like(TOKEN, F32)],
            6 * mac,
            3 * weight_bytes + len(flat) * piece_bytes,
            input_output_aliases={base + k: k for k in range(3)} if e > 0 else {},
        )(scal, *slots, *flat, *prev)

    along_z = Line("dp", n, 1)

    def outer(value):
        return along_z.send(value, [(0, 1), (1, 0), (2, 3), (3, 2)])

    def inner(value):
        return along_z.send(value, [(1, 2), (2, 1)])

    products, sums, grads = [], [], []

    def finish(e, slots, halves):
        nonlocal sums, grads
        *sums, token_a = out(e, halves, sums)
        *grads, token_b = grad(e, slots, halves, grads)
        return token_a, token_b

    if swaps:
        tokens_of, flight, arrived, deps = None, [None, None], None, []
        for e in range(local):
            slots, parts = pre(e, deps)
            deps, halves = [], []
            for h in range(2):
                x, last = parts[h], flight[h]
                if last is None:
                    a1 = outer(x[3])
                    send_a2, (send_b2,) = x[2], step(None, [(x[3], a1)])
                else:
                    y, got_a, got_b, wait = last
                    (send_a1,) = step((x[3], got_b), [], wait)
                    a1, b1 = outer(send_a1), inner(got_a)
                    send_a2, send_b2 = step((x[2], b1), [(x[3], a1)])
                a2, b2 = outer(send_a2), inner(send_b2)
                if last is not None:
                    halves.append([(y,), (got_a,), (a1, got_b), (a2, b1)])
                send_a3, send_b3 = step(None, [(x[1], b2), (x[2], a2)])
                a3, b3 = outer(send_a3), inner(send_b3)
                parts[h] = (x[0], a3, b3)
            wait_mid, wait_next = [], []
            if e > 0:
                token_a, token_b = finish(e - 1, arrived, halves)
                wait_mid, wait_next = [token_a], [token_b]
            for h in range(2):
                y, product = mid(*parts[h], wait_mid if h == 1 else [])
                products.append(product)
                flight[h] = (y, outer(y), inner(y), wait_next if h == 1 else [])
            deps = [parts[1][1]] if e > 0 else [parts[0][1]]
            arrived = slots
        halves = []
        for h in range(2):
            y, got_a, got_b, _ = flight[h]
            a1, b1 = outer(got_b), inner(got_a)
            a2 = outer(b1)
            halves.append([(y,), (got_a,), (a1, got_b), (a2, b1)])
        finish(local - 1, arrived, halves)
    else:
        begun = []
        for e in range(local):
            slots, parts = pre(e, [])
            begun.append((slots, [(x[0], *along_z.scatter(x, add_rounded)) for x in parts]))
        for e in range(local):
            halves = []
            for h in range(2):
                y, product = mid(*begun[e][1][h], [])
                products.append(product)
                halves.append([(y,)] + along_z.gather(y))
            finish(e, begun[e][0], halves)

    own = jnp.stack(
        [jnp.sum(products[2 * e] + products[2 * e + 1], axis=1) for e in range(local)], axis=1
    )
    if swaps:
        got_a, got_b = outer(own), inner(own)
        a1, b1 = outer(got_b), inner(got_a)
        pairs = [(got_a,), (a1, got_b), (outer(b1), b1)]
    else:
        pairs = along_z.gather(own)
    flat = [x for pair in pairs for x in pair]
    dense_shape = (chips, experts_all, count)
    near_p, far_p = call(
        functools.partial(home_kernel, n, local, [len(pair) for pair in pairs]),
        1,
        [SMEM_SPEC] + w_specs + [spec_of(own)] * (1 + len(flat)),
        [whole_spec(dense_shape)] * 2,
        [like(dense_shape, F32)] * 2,
        local * all_rows * count * 4,
        4 * experts_all * count * n,
        scratch_shapes=[pltpu.VMEM((n, rows, local), F32)],
    )(scal, *w_all, own, *flat)

    def send_home(near, far, add):
        near = add(near, across.send(far, swap))
        right, left = along_x.scatter([near[q] for q in range(chips)], add)
        home = near[0].astype(F32) + right.astype(F32)
        return home if left is None else home + left.astype(F32)

    per_expert = send_home(near_p, far_p, lambda a, b: a + b)
    combine_grad = jnp.sum(jnp.where(named, per_expert[None], 0.0), axis=1) / combine_t
    home = send_home(*sums, add_rounded)
    return (home[0].astype(BF16), home[1].astype(BF16), *grads, combine_grad.T)


def solution(mesh):
    return jax.shard_map(
        body,
        mesh=mesh,
        in_specs=(
            P(("group", "expert"), "dp"),
            P(("group", "expert"), None),
            P(("group", "expert"), None),
            P("expert", "dp", None),
            P("expert", "dp", None),
            P("expert", None, "dp"),
            P(("group", "expert"), "dp"),
        ),
        out_specs=(
            P(("group", "expert"), "dp"),
            P(("group", "expert"), "dp"),
            P(("group", "expert"), "dp", None),
            P(("group", "expert"), "dp", None),
            P(("group", "expert"), None, "dp"),
            P(("group", "expert"), None),
        ),
        check_vma=False,
    )
```

```python
import functools

import jax
import jax.numpy as jnp
from jax import lax
from jax.experimental import pallas as pl
from jax.experimental.pallas import tpu as pltpu
from jax.sharding import PartitionSpec as P

F32, BF16 = jnp.float32, jnp.bfloat16
VMEM_BYTES = 26 << 20


def line_pairs(n, gather, step):
    if gather:
        senders = [i for i in range(step - 1, n - 1)]
    else:
        senders = [i for i in range(0, min(step, n - 1))]
    right = [(i, i + 1) for i in senders]
    left = [(n - 1 - i, n - 2 - i) for i in senders]
    return right, left


class Line:
    def __init__(self, axis, n, stride):
        self.axis, self.n, self.stride = axis, n, stride

    def send(self, value, pairs):
        wide = [
            (a * self.stride + c, b * self.stride + c) for a, b in pairs for c in range(self.stride)
        ]
        return lax.ppermute(value, self.axis, wide)

    def gather(self, own):
        n = self.n
        if n == 2:
            both = self.send(own, [(0, 1), (1, 0)])
            return [(both, both)]
        right, left, rights, lefts = own, own, [], []
        for step in range(1, n):
            pairs_r, pairs_l = line_pairs(n, True, step)
            right, left = self.send(right, pairs_r), self.send(left, pairs_l)
            rights.append(right)
            lefts.append(left)
        return [(rights[q - 1], lefts[n - q - 1]) for q in range(1, n)]

    def scatter(self, parts, add):
        n = self.n
        if n == 2:
            return self.send(parts[1], [(0, 1), (1, 0)]), None
        right, left = parts[1], parts[n - 1]
        for step in range(1, n):
            pairs_r, pairs_l = line_pairs(n, False, step)
            right, left = self.send(right, pairs_r), self.send(left, pairs_l)
            if step < n - 1:
                right, left = add(parts[step + 1], right), add(parts[n - 1 - step], left)
        return right, left


def add_rounded(a, b):
    return (a.astype(F32) + b.astype(F32)).astype(BF16)


def dot(a, b, dims=((1,), (0,))):
    return lax.dot_general(a, b, (dims, ((), ())), preferred_element_type=F32)


def routing(scal, w_refs, expert, rows):
    n = len(w_refs)
    experts_all, tokens = w_refs[0].shape
    ids = lax.broadcasted_iota(jnp.int32, (experts_all, tokens), 0)
    which = scal[2 * n] + expert
    weights = jnp.concatenate(
        [jnp.sum(jnp.where(ids == which, w[...], 0.0), axis=0, keepdims=True) for w in w_refs],
        axis=0,
    )
    chosen = weights > 0.0
    earlier = lax.broadcasted_iota(jnp.int32, (tokens, tokens), 0) < lax.broadcasted_iota(
        jnp.int32, (tokens, tokens), 1
    )
    slots = dot(chosen.astype(F32).astype(BF16), earlier.astype(F32).astype(BF16))
    slots = jnp.where(chosen, slots, -1.0).astype(jnp.int32)
    row = lax.broadcasted_iota(jnp.int32, (rows, tokens), 0)
    return [(scal[k], weights[k : k + 1], row == slots[k : k + 1]) for k in range(n)]


def span_of(position, rows):
    return pl.ds(pl.multiple_of(position * rows, rows), rows)


def pre_kernel(n, expert, deps, scal, *refs):
    refs = refs[deps:]
    w_refs, packs, refs = refs[:n], refs[n : 2 * n], refs[2 * n :]
    gw, uw, dw, in_ref, cot_ref, *outs = refs
    rows = in_ref.shape[0] // n
    half = pl.program_id(0)

    @pl.when(half == 0)
    def _():
        for k, (position, weight, hit) in enumerate(routing(scal, w_refs, expert, rows)):
            pick = hit.astype(F32).astype(BF16)
            span = span_of(position, rows)
            in_ref[span, :] = dot(pick, packs[k][0]).astype(BF16)
            scale = jnp.sum(jnp.where(hit, weight, 0.0), axis=1, keepdims=True)
            cot_ref[span, :] = (dot(pick, packs[k][1]) * scale).astype(BF16)

    gate = dot(in_ref[...], gw[0]).astype(BF16)
    up = dot(in_ref[...], uw[0]).astype(BF16)
    back = dot(cot_ref[...], dw[0], ((1,), (1,))).astype(BF16)
    for h in range(2):

        @pl.when(half == h)
        def _():
            for p in range(n):
                for k, value in enumerate((gate, up, back)):
                    outs[h * n + p][pl.ds(k * rows, rows), :] = value[p * rows : (p + 1) * rows]


def thirds(value):
    high = value.astype(BF16)
    rest = value - high.astype(F32)
    middle = rest.astype(BF16)
    return high, middle, (rest - middle.astype(F32)).astype(BF16)


def mid_kernel(deps, others, *refs):
    own, right, left, *rest = refs[deps:]
    earlier, (out, product) = rest[:others], rest[others:]
    rows, tile = own.shape[0] // 3, own.shape[1]
    total = own[...].astype(F32) + right[...].astype(F32) + left[...].astype(F32)
    gate, up, back = (total[k * rows : (k + 1) * rows] for k in range(3))
    sig = jax.nn.sigmoid(gate)
    hidden = (gate * sig * up).astype(BF16)
    delta = back.astype(BF16).astype(F32)
    out[0:rows, :] = hidden
    out[rows : 2 * rows, :] = (delta * up * sig * (1.0 + gate * (1.0 - sig))).astype(BF16)
    out[2 * rows : 3 * rows, :] = (delta * (gate * sig)).astype(BF16)
    prod = hidden.astype(F32) * back
    lanes = product.shape[1]
    acc = prod[:, 0:lanes]
    for k in range(1, tile // lanes):
        acc = acc + prod[:, k * lanes : (k + 1) * lanes]
    product[...] = acc
    if others:
        partial = [ref[...] for ref in earlier] + [acc]
        ones, fill = jnp.ones((8, lanes), BF16), jnp.zeros((lanes - rows, lanes), F32)
        lines = []
        for e in range(len(partial) // 2):
            wide = jnp.concatenate([partial[2 * e] + partial[2 * e + 1], fill], axis=0)
            total = sum(dot(ones, part, ((1,), (1,))) for part in thirds(wide))[0:1]
            lines += [part.astype(F32) for part in thirds(total)]
        extra = out.shape[0] - 3 * rows
        lines.append(jnp.zeros((extra - len(lines), lanes), F32))
        out[3 * rows :, :] = jnp.zeros((extra, tile), BF16)
        out[3 * rows :, 0:lanes] = jnp.concatenate(lines, axis=0).astype(BF16)


def part_of(scal, n, q, group, start, size):
    span = pl.ds(start, size)
    if len(group) == 1:
        return group[0][span, :]
    return jnp.where(scal[n + q] > 0, group[0][span, :], group[1][span, :])


def load_rows(scal, n, which, pieces):
    rows = pieces[0][0].shape[0] // 48 * 16
    return jnp.concatenate(
        [part_of(scal, n, q, group, which * rows, rows) for q, group in enumerate(pieces)], axis=0
    )


def split_pieces(refs, sizes):
    halves, at = [], 0
    for _ in range(2):
        pieces = [refs[at : at + 1]]
        at += 1
        for size in sizes:
            pieces.append(refs[at : at + size])
            at += size
        halves.append(pieces)
    return halves, refs[at:]


def out_kernel(n, expert, has_prev, last, sizes, deps, scal, *refs):
    refs = refs[deps:]
    w_refs, refs = refs[:n], refs[n:]
    if has_prev:
        prev, refs = refs[:2], refs[2:]
    halves, refs = split_pieces(refs, sizes)
    gw, uw, dw, near, far, token, *refs = refs
    if last:
        near_p, far_p, *refs, held = refs
    eo, idl = refs
    step = pl.program_id(0)

    for h in range(2):

        @pl.when(step == h)
        def _():
            layer = dot(load_rows(scal, n, 0, halves[h]), dw[0])
            back = dot(load_rows(scal, n, 1, halves[h]), gw[0], ((1,), (1,))) + dot(
                load_rows(scal, n, 2, halves[h]), uw[0], ((1,), (1,))
            )
            eo[...] = layer if h == 0 else eo[...] + layer
            idl[...] = back if h == 0 else idl[...] + back

    @pl.when(step == 1)
    def _():
        rows = eo.shape[0] // n
        for k, (position, weight, hit) in enumerate(routing(scal, w_refs, expert, rows)):
            pick = hit.astype(F32)
            scaled = (pick * weight).astype(BF16)
            span = span_of(position, rows)
            layer = dot(scaled, eo[span, :].astype(BF16), ((0,), (0,)))
            back = dot(pick.astype(BF16), idl[span, :].astype(BF16), ((0,), (0,)))
            which, place = (near, k) if k < n // 2 else (far, k - n // 2)
            if has_prev:
                before = prev[0 if k < n // 2 else 1]
                layer, back = layer + before[place, 0], back + before[place, 1]
            which[place, 0] = layer.astype(which.dtype)
            which[place, 1] = back.astype(which.dtype)
        token[...] = jnp.zeros_like(token)
        if last:
            send_products(scal, w_refs, expert + 1, halves[1], held, near_p, far_p)


def grad_kernel(n, has_prev, sizes, scal, in_ref, cot_ref, *refs):
    halves, refs = split_pieces(refs, sizes)
    if has_prev:
        refs = refs[3:]
    gg, ug, dg, token = refs
    step = pl.program_id(0)
    token[...] = jnp.zeros_like(token)
    for h in range(2):

        @pl.when(step == h)
        def _():
            gg[0] = dot(in_ref[...], load_rows(scal, n, 1, halves[h]), ((0,), (0,))).astype(BF16)
            ug[0] = dot(in_ref[...], load_rows(scal, n, 2, halves[h]), ((0,), (0,))).astype(BF16)
            dg[0] = dot(load_rows(scal, n, 0, halves[h]), cot_ref[...], ((0,), (0,))).astype(BF16)


def send_products(scal, w_refs, local, pieces, held, near, far):
    n, (_, extra, lanes) = len(w_refs), held.shape
    first = pieces[0][0].shape[0] - extra
    for q, group in enumerate(pieces):
        held[q] = part_of(scal, n, q, group, first, extra)[:, 0:lanes]
    experts_all, tokens = w_refs[0].shape
    ids = lax.broadcasted_iota(jnp.int32, (experts_all, tokens), 0)
    sums = [jnp.zeros((experts_all, tokens), F32) for _ in range(n)]
    for e in range(local):
        for k, (position, _, hit) in enumerate(routing(scal, w_refs, e, lanes)):
            found = dot(held[position], hit.astype(F32).astype(BF16))
            value = found[3 * e : 3 * e + 1] + found[3 * e + 1 : 3 * e + 2] + found[3 * e + 2 : 3 * e + 3]
            sums[k] = sums[k] + jnp.where(ids == scal[2 * n] + e, value, 0.0)
    for k in range(n):
        if k < n // 2:
            near[k] = sums[k]
        else:
            far[k - n // 2] = sums[k]


def pack_kernel(ids, combine, tokens, grads, pack, dense):
    pack[0] = tokens[...]
    pack[1] = grads[...]
    expert = lax.broadcasted_iota(jnp.int32, dense.shape, 0)
    total = jnp.zeros(dense.shape, F32)
    for k in range(ids.shape[0]):
        total = total + jnp.where(expert == ids[k : k + 1, :], combine[k : k + 1, :], 0.0)
    dense[...] = total


def whole_spec(shape):
    return pl.BlockSpec(tuple(shape), lambda g: (0,) * len(shape))


def spec_of(array):
    return whole_spec(array.shape)


def like(shape, dtype=BF16):
    return jax.ShapeDtypeStruct(tuple(shape), dtype)


SMEM_SPEC = pl.BlockSpec(memory_space=pltpu.SMEM)
ANY_SPEC = pl.BlockSpec(memory_space=pl.ANY)
TOKEN = (8, 128)


def call(kernel, grid, in_specs, out_specs, out_shape, flops, moved, **rest):
    return pl.pallas_call(
        kernel,
        grid=(grid,),
        in_specs=in_specs,
        out_specs=out_specs,
        out_shape=out_shape,
        compiler_params=pltpu.CompilerParams(vmem_limit_bytes=VMEM_BYTES),
        cost_estimate=pl.CostEstimate(flops=flops, bytes_accessed=moved, transcendentals=0),
        **rest,
    )


def body(tokens, expert_ids, combine, gate_weight, up_weight, down_weight, out_grad):
    peers, n = lax.axis_size("expert"), lax.axis_size("dp")
    assert peers == n
    chips = peers // 2
    local, width, hidden = gate_weight.shape
    count, choose = expert_ids.shape
    experts_all = peers * local
    capacity = count * choose * 5 // (4 * experts_all)
    rows = -(-capacity // 16) * 16
    all_rows = n * rows
    tile = hidden // 2
    swaps = n == 4

    me, here = lax.axis_index("expert"), lax.axis_index("dp")
    at_end = (here == 0) | (here == n - 1)
    table = []
    for place in range(n):
        block = 2 * lax.rem(me // 2 - place % chips + chips, chips) + lax.rem(
            lax.rem(me, 2) + place // chips, 2
        )
        if swaps:
            across_middle = jnp.where((block == 0) | (block == 3), 3, 2)
            position = jnp.where(
                block == here, 0, jnp.where(block // 2 == here // 2, 1, across_middle)
            )
        else:
            position = lax.rem(here - block + n, n)
        table.append(position)
    flags = [at_end if swaps else here >= q for q in range(n)]
    scal = jnp.stack(
        [jnp.asarray(v).astype(jnp.int32) for v in table + flags + [me * local, at_end]]
    )

    ids_t, combine_t = expert_ids.T, combine.T
    named = ids_t[:, None, :] == jnp.arange(experts_all, dtype=jnp.int32)[None, :, None]
    pack, dense = call(
        pack_kernel,
        1,
        [spec_of(ids_t), spec_of(combine_t), spec_of(tokens), spec_of(out_grad)],
        [whole_spec((2, count, width)), whole_spec((experts_all, count))],
        [like((2, count, width)), like((experts_all, count), F32)],
        choose * experts_all * count,
        8 * count * width,
    )(ids_t, combine_t, tokens, out_grad)

    along_x, across = Line("expert", chips, 2), Line("expert", peers, 1)
    swap = [(2 * x + c, 2 * x + 1 - c) for x in range(chips) for c in range(2)]

    def gather_blocks(own):
        found = [own] + [
            right if right is left else jnp.where(me // 2 >= q, right, left)
            for q, (right, left) in enumerate(along_x.gather(own), 1)
        ]
        return found + [across.send(piece, swap) for piece in found]

    w_all = gather_blocks(dense)
    packs = gather_blocks(pack)
    w_specs, pack_specs = [spec_of(w) for w in w_all], [spec_of(p) for p in packs]

    mac = all_rows * width * hidden
    weight_bytes = 2 * width * hidden
    piece_shape = (3 * rows, tile)
    extra = -(-3 * local // 16) * 16
    wide_shape = (3 * rows + extra, tile)
    piece_bytes = 2 * 3 * rows * tile
    slot_shape = (all_rows, width)

    def weight_specs(e):
        wide = pl.BlockSpec((1, width, tile), lambda g: (e, 0, g))
        return [wide, wide, pl.BlockSpec((1, tile, width), lambda g: (e, g, 0))]

    def pre(e, deps):
        inputs, cot, *parts = call(
            functools.partial(pre_kernel, n, e, len(deps)),
            2,
            [SMEM_SPEC] + [ANY_SPEC] * len(deps) + w_specs + pack_specs + weight_specs(e),
            [whole_spec(slot_shape)] * 2 + [whole_spec(piece_shape)] * (2 * n),
            [like(slot_shape)] * 2 + [like(piece_shape)] * (2 * n),
            6 * mac,
            3 * weight_bytes + 2 * n * piece_bytes,
        )(scal, *deps, *w_all, *packs, gate_weight, up_weight, down_weight)
        return (inputs, cot), [parts[:n], parts[n:]]

    def mid(e, h, totals, products, deps=()):
        others = products if e == local - 1 and h == 1 else []
        shape = wide_shape if others else piece_shape
        return call(
            functools.partial(mid_kernel, len(deps), len(others)),
            1,
            [ANY_SPEC] * len(deps)
            + [whole_spec(piece_shape)] * 3
            + [whole_spec((rows, 128))] * len(others),
            [whole_spec(shape), whole_spec((rows, 128))],
            [like(shape), like((rows, 128), F32)],
            20 * rows * tile,
            4 * piece_bytes,
        )(*deps, *totals, *others)

    def flatten(halves):
        return [x for pieces in halves for group in pieces for x in group]

    def sizes_of(pieces):
        return [len(group) for group in pieces[1:]]

    def out(e, halves, prev, deps):
        flat = flatten(halves)
        last = e == local - 1
        dense_shape = (chips, experts_all, count)
        sum_shape = (chips, 2, count, width)
        return call(
            functools.partial(out_kernel, n, e, e > 0, last, sizes_of(halves[0]), len(deps)),
            2,
            [SMEM_SPEC]
            + [ANY_SPEC] * len(deps)
            + w_specs
            + ([whole_spec(sum_shape)] * 2 if e > 0 else [])
            + [spec_of(x) for x in flat]
            + weight_specs(e),
            [whole_spec(sum_shape)] * 2
            + [whole_spec(TOKEN)]
            + ([whole_spec(dense_shape)] * 2 if last else []),
            [like(sum_shape, BF16 if last else F32)] * 2
            + [like(TOKEN, F32)]
            + ([like(dense_shape, F32)] * 2 if last else []),
            6 * mac,
            3 * weight_bytes + len(flat) * piece_bytes,
            scratch_shapes=[pltpu.VMEM(slot_shape, F32)] * 2
            + ([pltpu.VMEM((n, extra, 128), BF16)] if last else []),
        )(scal, *deps, *w_all, *prev, *flat, gate_weight, up_weight, down_weight)

    def grad(e, slots, halves, prev):
        flat = flatten(halves)
        base = 3 + len(flat)
        return call(
            functools.partial(grad_kernel, n, e > 0, sizes_of(halves[0])),
            2,
            [SMEM_SPEC]
            + [whole_spec(slot_shape)] * 2
            + [spec_of(x) for x in flat]
            + ([ANY_SPEC] * 3 if e > 0 else []),
            weight_specs(e) + [whole_spec(TOKEN)],
            [like(w.shape) for w in (gate_weight, up_weight, down_weight)] + [like(TOKEN, F32)],
            6 * mac,
            3 * weight_bytes + len(flat) * piece_bytes,
            input_output_aliases={base + k: k for k in range(3)} if e > 0 else {},
        )(scal, *slots, *flat, *prev)

    along_z = Line("dp", n, 1)

    def outer(value):
        return along_z.send(value, [(0, 1), (1, 0), (2, 3), (3, 2)])

    def inner(value):
        return along_z.send(value, [(1, 2), (2, 1), (0, 0), (3, 3)])

    def unless_end(value):
        return jnp.where(at_end, jnp.zeros_like(value), value)

    products, sums, grads, home_sums = [], [], [], []

    def finish(e, slots, halves, deps=()):
        nonlocal sums, grads, home_sums
        near, far, token_a, *home_sums = out(e, halves, sums, deps)
        *grads, token_b = grad(e, slots, halves, grads)
        sums = [near, far]
        return token_a, token_b

    if swaps:
        flight, arrived, deps, token_b = [None, None], None, [], None
        for e in range(local):
            slots, parts = pre(e, deps)
            halves, totals = [], []
            for h in range(2):
                x, last = parts[h], flight[h]
                if last is None:
                    a1, send_a2 = outer(x[3]), x[2]
                else:
                    y, got_a, got_b = last
                    a1, b1 = outer(jnp.where(at_end, x[3], got_b)), inner(got_a)
                    send_a2 = jnp.where(at_end, x[2], b1)
                a2, b2 = outer(send_a2), inner(unless_end(add_rounded(x[3], a1)))
                if last is not None:
                    halves.append([(y,), (got_a,), (a1, got_b), (a2, b1)])
                a3 = outer(add_rounded(x[1], b2))
                b3 = inner(unless_end(add_rounded(x[2], a2)))
                totals.append((x[0], a3, b3))
            token_a = None
            if e > 0:
                token_a, token_b = finish(e - 1, arrived, halves)
            for h in range(2):
                wait = [token_a] if e > 0 and h == 1 else []
                y, product = mid(e, h, totals[h], products, wait)
                products.append(product)
                flight[h] = (y, outer(y), inner(y))
            deps = [totals[0][1]] if e == 0 else [token_b]
            arrived = slots
        halves = []
        for h in range(2):
            y, got_a, got_b = flight[h]
            a1, b1 = outer(got_b), inner(got_a)
            a2 = outer(b1)
            halves.append([(y,), (got_a,), (a1, got_b), (a2, b1)])
        finish(local - 1, arrived, halves, [token_b])
    else:
        begun = []
        for e in range(local):
            slots, parts = pre(e, [])
            begun.append((slots, [(x[0], *along_z.scatter(x, add_rounded)) for x in parts]))
        for e in range(local):
            halves = []
            for h in range(2):
                y, product = mid(e, h, begun[e][1][h], products)
                products.append(product)
                halves.append([(y,)] + along_z.gather(y))
            finish(e, begun[e][0], halves)

    def send_home(near, far, add):
        near = add(near, across.send(far, swap))
        right, left = along_x.scatter([near[q] for q in range(chips)], add)
        home = near[0].astype(F32) + right.astype(F32)
        return home if left is None else home + left.astype(F32)

    per_expert = send_home(*home_sums, lambda a, b: a + b)
    combine_grad = jnp.sum(jnp.where(named, per_expert[None], 0.0), axis=1) / combine_t
    home = send_home(*sums, add_rounded)
    return (home[0].astype(BF16), home[1].astype(BF16), *grads, combine_grad.T)


def solution(mesh):
    return jax.shard_map(
        body,
        mesh=mesh,
        in_specs=(
            P(("group", "expert"), "dp"),
            P(("group", "expert"), None),
            P(("group", "expert"), None),
            P("expert", "dp", None),
            P("expert", "dp", None),
            P("expert", None, "dp"),
            P(("group", "expert"), "dp"),
        ),
        out_specs=(
            P(("group", "expert"), "dp"),
            P(("group", "expert"), "dp"),
            P(("group", "expert"), "dp", None),
            P(("group", "expert"), "dp", None),
            P(("group", "expert"), None, "dp"),
            P(("group", "expert"), None),
        ),
        check_vma=False,
    )
```

```python
import functools

import jax
import jax.numpy as jnp
from jax import lax
from jax.experimental import pallas as pl
from jax.experimental.pallas import tpu as pltpu
from jax.sharding import PartitionSpec as P

F32, BF16 = jnp.float32, jnp.bfloat16
VMEM_BYTES = 26 << 20


def line_pairs(n, gather, step):
    if gather:
        senders = [i for i in range(step - 1, n - 1)]
    else:
        senders = [i for i in range(0, min(step, n - 1))]
    right = [(i, i + 1) for i in senders]
    left = [(n - 1 - i, n - 2 - i) for i in senders]
    return right, left


class Line:
    def __init__(self, axis, n, stride):
        self.axis, self.n, self.stride = axis, n, stride

    def send(self, value, pairs):
        wide = [
            (a * self.stride + c, b * self.stride + c) for a, b in pairs for c in range(self.stride)
        ]
        return lax.ppermute(value, self.axis, wide)

    def gather(self, own):
        n = self.n
        if n == 2:
            both = self.send(own, [(0, 1), (1, 0)])
            return [(both, both)]
        right, left, rights, lefts = own, own, [], []
        for step in range(1, n):
            pairs_r, pairs_l = line_pairs(n, True, step)
            right, left = self.send(right, pairs_r), self.send(left, pairs_l)
            rights.append(right)
            lefts.append(left)
        return [(rights[q - 1], lefts[n - q - 1]) for q in range(1, n)]

    def scatter(self, parts, add):
        n = self.n
        if n == 2:
            return self.send(parts[1], [(0, 1), (1, 0)]), None
        right, left = parts[1], parts[n - 1]
        for step in range(1, n):
            pairs_r, pairs_l = line_pairs(n, False, step)
            right, left = self.send(right, pairs_r), self.send(left, pairs_l)
            if step < n - 1:
                right, left = add(parts[step + 1], right), add(parts[n - 1 - step], left)
        return right, left


def add_rounded(a, b):
    return (a.astype(F32) + b.astype(F32)).astype(BF16)


def dot(a, b, dims=((1,), (0,))):
    return lax.dot_general(a, b, (dims, ((), ())), preferred_element_type=F32)


def routing(scal, w_refs, expert, rows):
    n = len(w_refs)
    experts_all, tokens = w_refs[0].shape
    ids = lax.broadcasted_iota(jnp.int32, (experts_all, tokens), 0)
    which = scal[2 * n] + expert
    weights = jnp.concatenate(
        [jnp.sum(jnp.where(ids == which, w[...], 0.0), axis=0, keepdims=True) for w in w_refs],
        axis=0,
    )
    chosen = weights > 0.0
    earlier = lax.broadcasted_iota(jnp.int32, (tokens, tokens), 0) < lax.broadcasted_iota(
        jnp.int32, (tokens, tokens), 1
    )
    slots = dot(chosen.astype(F32).astype(BF16), earlier.astype(F32).astype(BF16))
    slots = jnp.where(chosen, slots, -1.0).astype(jnp.int32)
    row = lax.broadcasted_iota(jnp.int32, (rows, tokens), 0)
    return [(scal[k], weights[k : k + 1], row == slots[k : k + 1]) for k in range(n)]


def span_of(position, rows):
    return pl.ds(pl.multiple_of(position * rows, rows), rows)


def weight_copies(expert, weights, held, sems):
    halves = []
    for h in range(2):
        copies = []
        for k, (source, target) in enumerate(zip(weights, held)):
            size = target.shape[0 if k == 2 else 1] // 2
            span = pl.ds(h * size, size)
            src, dst = (
                (source.at[expert, span, :], target.at[span, :])
                if k == 2
                else (source.at[expert, :, span], target.at[:, span])
            )
            copies.append(pltpu.make_async_copy(src, dst, sems.at[h, k]))
        halves.append(copies)
    return halves


def pre_kernel(n, expert, deps, scal, *refs):
    refs = refs[deps:]
    w_refs, toks, ogs, refs = refs[:n], refs[n : 2 * n], refs[2 * n : 3 * n], refs[3 * n :]
    weights, (in_ref, cot_ref, *refs) = refs[:3], refs[3:]
    outs, (token, gw, uw, dw, sems) = refs[: 2 * n], refs[2 * n :]
    rows, tile = in_ref.shape[0] // n, gw.shape[1] // 2
    copies = weight_copies(expert, weights, (gw, uw, dw), sems)
    for group in copies:
        for copy in group:
            copy.start()
    token[...] = jnp.zeros_like(token)
    for k, (position, weight, hit) in enumerate(routing(scal, w_refs, expert, rows)):
        pick = hit.astype(F32).astype(BF16)
        span = span_of(position, rows)
        in_ref[span, :] = dot(pick, toks[k][...]).astype(BF16)
        scale = jnp.sum(jnp.where(hit, weight, 0.0), axis=1, keepdims=True)
        cot_ref[span, :] = (dot(pick, ogs[k][...]) * scale).astype(BF16)
    for h in range(2):
        for copy in copies[h]:
            copy.wait()
        part = slice(h * tile, (h + 1) * tile)
        gate = dot(in_ref[...], gw[:, part]).astype(BF16)
        up = dot(in_ref[...], uw[:, part]).astype(BF16)
        back = dot(cot_ref[...], dw[part, :], ((1,), (1,))).astype(BF16)
        for p in range(n):
            for k, value in enumerate((gate, up, back)):
                outs[h * n + p][pl.ds(k * rows, rows), :] = value[p * rows : (p + 1) * rows]


def thirds(value):
    high = value.astype(BF16)
    rest = value - high.astype(F32)
    middle = rest.astype(BF16)
    return high, middle, (rest - middle.astype(F32)).astype(BF16)


def mid_kernel(deps, others, *refs):
    own, right, left, *rest = refs[deps:]
    earlier, (out, product) = rest[:others], rest[others:]
    rows, tile = own.shape[0] // 3, own.shape[1]
    total = own[...].astype(F32) + right[...].astype(F32) + left[...].astype(F32)
    gate, up, back = (total[k * rows : (k + 1) * rows] for k in range(3))
    sig = jax.nn.sigmoid(gate)
    hidden = (gate * sig * up).astype(BF16)
    delta = back.astype(BF16).astype(F32)
    out[0:rows, :] = hidden
    out[rows : 2 * rows, :] = (delta * up * sig * (1.0 + gate * (1.0 - sig))).astype(BF16)
    out[2 * rows : 3 * rows, :] = (delta * (gate * sig)).astype(BF16)
    prod = hidden.astype(F32) * back
    lanes = product.shape[1]
    acc = prod[:, 0:lanes]
    for k in range(1, tile // lanes):
        acc = acc + prod[:, k * lanes : (k + 1) * lanes]
    product[...] = acc
    if others:
        partial = [ref[...] for ref in earlier] + [acc]
        ones, fill = jnp.ones((8, lanes), BF16), jnp.zeros((lanes - rows, lanes), F32)
        lines = []
        for e in range(len(partial) // 2):
            wide = jnp.concatenate([partial[2 * e] + partial[2 * e + 1], fill], axis=0)
            total = sum(dot(ones, part, ((1,), (1,))) for part in thirds(wide))[0:1]
            lines += [part.astype(F32) for part in thirds(total)]
        extra = out.shape[0] - 3 * rows
        lines.append(jnp.zeros((extra - len(lines), lanes), F32))
        out[3 * rows :, :] = jnp.zeros((extra, tile), BF16)
        out[3 * rows :, 0:lanes] = jnp.concatenate(lines, axis=0).astype(BF16)


def part_of(scal, n, q, group, start, size):
    span = pl.ds(start, size)
    if len(group) == 1:
        return group[0][span, :]
    return jnp.where(scal[n + q] > 0, group[0][span, :], group[1][span, :])


def load_rows(scal, n, which, pieces):
    rows = pieces[0][0].shape[0] // 48 * 16
    return jnp.concatenate(
        [part_of(scal, n, q, group, which * rows, rows) for q, group in enumerate(pieces)], axis=0
    )


def split_pieces(refs, sizes):
    halves, at = [], 0
    for _ in range(2):
        pieces = [refs[at : at + 1]]
        at += 1
        for size in sizes:
            pieces.append(refs[at : at + size])
            at += size
        halves.append(pieces)
    return halves, refs[at:]


def out_kernel(n, expert, has_prev, last, sizes, deps, scal, *refs):
    refs = refs[deps:]
    w_refs, refs = refs[:n], refs[n:]
    if has_prev:
        prev, refs = refs[:2], refs[2:]
    halves, refs = split_pieces(refs, sizes)
    weights, (near, far, token, *refs) = refs[:3], refs[3:]
    if last:
        near_p, far_p, *refs, held = refs
    gw, uw, dw, sems, eo_ref, idl_ref = refs
    copies = weight_copies(expert, weights, (gw, uw, dw), sems)
    for group in copies:
        for copy in group:
            copy.start()
    token[...] = jnp.zeros_like(token)
    routes = routing(scal, w_refs, expert, halves[0][0][0].shape[0] // 48 * 16)
    if last:
        send_products(scal, w_refs, expert + 1, halves[1], held, near_p, far_p)
    tile = gw.shape[1] // 2
    eo, idl = 0.0, 0.0
    for h in range(2):
        for copy in copies[h]:
            copy.wait()
        part = slice(h * tile, (h + 1) * tile)
        eo = eo + dot(load_rows(scal, n, 0, halves[h]), dw[part, :])
        idl = idl + dot(load_rows(scal, n, 1, halves[h]), gw[:, part], ((1,), (1,)))
        idl = idl + dot(load_rows(scal, n, 2, halves[h]), uw[:, part], ((1,), (1,)))
    rows = eo.shape[0] // n
    eo_ref[...], idl_ref[...] = eo.astype(BF16), idl.astype(BF16)
    for k, (position, weight, hit) in enumerate(routes):
        pick = hit.astype(F32)
        scaled = (pick * weight).astype(BF16)
        span = span_of(position, rows)
        layer = dot(scaled, eo_ref[span, :], ((0,), (0,)))
        back = dot(pick.astype(BF16), idl_ref[span, :], ((0,), (0,)))
        which, place = (near, k) if k < n // 2 else (far, k - n // 2)
        if has_prev:
            before = prev[0 if k < n // 2 else 1]
            layer, back = layer + before[place, 0], back + before[place, 1]
        which[place, 0] = layer.astype(which.dtype)
        which[place, 1] = back.astype(which.dtype)


def grad_kernel(n, has_prev, sizes, deps, scal, in_ref, cot_ref, *refs):
    refs = refs[deps:]
    halves, refs = split_pieces(refs, sizes)
    if has_prev:
        refs = refs[3:]
    gg, ug, dg, token = refs
    step = pl.program_id(0)
    token[...] = jnp.zeros_like(token)
    for h in range(2):

        @pl.when(step == h)
        def _():
            gg[0] = dot(in_ref[...], load_rows(scal, n, 1, halves[h]), ((0,), (0,))).astype(BF16)
            ug[0] = dot(in_ref[...], load_rows(scal, n, 2, halves[h]), ((0,), (0,))).astype(BF16)
            dg[0] = dot(load_rows(scal, n, 0, halves[h]), cot_ref[...], ((0,), (0,))).astype(BF16)


def send_products(scal, w_refs, local, pieces, held, near, far):
    n, (_, extra, lanes) = len(w_refs), held.shape
    first = pieces[0][0].shape[0] - extra
    for q, group in enumerate(pieces):
        held[q] = part_of(scal, n, q, group, first, extra)[:, 0:lanes]
    experts_all, tokens = w_refs[0].shape
    ids = lax.broadcasted_iota(jnp.int32, (experts_all, tokens), 0)
    sums = [jnp.zeros((experts_all, tokens), F32) for _ in range(n)]
    for e in range(local):
        for k, (position, _, hit) in enumerate(routing(scal, w_refs, e, lanes)):
            found = dot(held[position], hit.astype(F32).astype(BF16))
            value = found[3 * e : 3 * e + 1] + found[3 * e + 1 : 3 * e + 2] + found[3 * e + 2 : 3 * e + 3]
            sums[k] = sums[k] + jnp.where(ids == scal[2 * n] + e, value, 0.0)
    for k in range(n):
        if k < n // 2:
            near[k] = sums[k]
        else:
            far[k - n // 2] = sums[k]


def whole_spec(shape):
    return pl.BlockSpec(tuple(shape), lambda g: (0,) * len(shape))


def spec_of(array):
    return whole_spec(array.shape)


def like(shape, dtype=BF16):
    return jax.ShapeDtypeStruct(tuple(shape), dtype)


SMEM_SPEC = pl.BlockSpec(memory_space=pltpu.SMEM)
ANY_SPEC = pl.BlockSpec(memory_space=pl.ANY)
HBM_SPEC = pl.BlockSpec(memory_space=pltpu.HBM)
TOKEN = (8, 128)


def call(kernel, grid, in_specs, out_specs, out_shape, flops, moved, **rest):
    return pl.pallas_call(
        kernel,
        grid=(grid,),
        in_specs=in_specs,
        out_specs=out_specs,
        out_shape=out_shape,
        compiler_params=pltpu.CompilerParams(vmem_limit_bytes=VMEM_BYTES),
        cost_estimate=pl.CostEstimate(flops=flops, bytes_accessed=moved, transcendentals=0),
        **rest,
    )


def body(tokens, expert_ids, combine, gate_weight, up_weight, down_weight, out_grad):
    peers, n = lax.axis_size("expert"), lax.axis_size("dp")
    assert peers == n
    chips = peers // 2
    local, width, hidden = gate_weight.shape
    count, choose = expert_ids.shape
    experts_all = peers * local
    capacity = count * choose * 5 // (4 * experts_all)
    rows = -(-capacity // 16) * 16
    all_rows = n * rows
    tile = hidden // 2
    swaps = n == 4

    me, here = lax.axis_index("expert"), lax.axis_index("dp")
    at_end = (here == 0) | (here == n - 1)
    table = []
    for place in range(n):
        block = 2 * lax.rem(me // 2 - place % chips + chips, chips) + lax.rem(
            lax.rem(me, 2) + place // chips, 2
        )
        if swaps:
            across_middle = jnp.where((block == 0) | (block == 3), 3, 2)
            position = jnp.where(
                block == here, 0, jnp.where(block // 2 == here // 2, 1, across_middle)
            )
        else:
            position = lax.rem(here - block + n, n)
        table.append(position)
    flags = [at_end if swaps else here >= q for q in range(n)]
    scal = jnp.stack(
        [jnp.asarray(v).astype(jnp.int32) for v in table + flags + [me * local, at_end]]
    )

    ids_t, combine_t = expert_ids.T, combine.T
    named = ids_t[:, None, :] == jnp.arange(experts_all, dtype=jnp.int32)[None, :, None]
    dense = jnp.sum(jnp.where(named, combine_t[:, None, :], 0.0), axis=0)

    along_x, across = Line("expert", chips, 2), Line("expert", peers, 1)
    swap = [(2 * x + c, 2 * x + 1 - c) for x in range(chips) for c in range(2)]

    def gather_blocks(own):
        found = [own] + [
            right if right is left else jnp.where(me // 2 >= q, right, left)
            for q, (right, left) in enumerate(along_x.gather(own), 1)
        ]
        return found + [across.send(piece, swap) for piece in found]

    tok_all, og_all, w_all = gather_blocks(tokens), gather_blocks(out_grad), gather_blocks(dense)
    w_specs, block_specs = [spec_of(w) for w in w_all], [spec_of(x) for x in tok_all + og_all]

    mac = all_rows * width * hidden
    weight_bytes = 2 * width * hidden
    piece_shape = (3 * rows, tile)
    extra = -(-3 * local // 16) * 16
    wide_shape = (3 * rows + extra, tile)
    piece_bytes = 2 * 3 * rows * tile
    slot_shape = (all_rows, width)

    weights = (gate_weight, up_weight, down_weight)
    held_weights = [pltpu.VMEM(w.shape[1:], BF16) for w in weights] + [
        pltpu.SemaphoreType.DMA((2, 3))
    ]

    def grad_specs(e):
        wide = pl.BlockSpec((1, width, tile), lambda g: (e, 0, g))
        return [wide, wide, pl.BlockSpec((1, tile, width), lambda g: (e, g, 0))]

    def pre(e, deps):
        inputs, cot, *parts, token = call(
            functools.partial(pre_kernel, n, e, len(deps)),
            1,
            [SMEM_SPEC] + [ANY_SPEC] * len(deps) + w_specs + block_specs + [HBM_SPEC] * 3,
            [whole_spec(slot_shape)] * 2 + [whole_spec(piece_shape)] * (2 * n) + [whole_spec(TOKEN)],
            [like(slot_shape)] * 2 + [like(piece_shape)] * (2 * n) + [like(TOKEN, F32)],
            6 * mac,
            3 * weight_bytes + 2 * n * piece_bytes,
            scratch_shapes=held_weights,
        )(scal, *deps, *w_all, *tok_all, *og_all, *weights)
        return (inputs, cot), [parts[:n], parts[n:]], token

    def mid(e, h, totals, products, deps=()):
        others = products if e == local - 1 and h == 1 else []
        shape = wide_shape if others else piece_shape
        return call(
            functools.partial(mid_kernel, len(deps), len(others)),
            1,
            [ANY_SPEC] * len(deps)
            + [whole_spec(piece_shape)] * 3
            + [whole_spec((rows, 128))] * len(others),
            [whole_spec(shape), whole_spec((rows, 128))],
            [like(shape), like((rows, 128), F32)],
            20 * rows * tile,
            4 * piece_bytes,
        )(*deps, *totals, *others)

    def flatten(halves):
        return [x for pieces in halves for group in pieces for x in group]

    def sizes_of(pieces):
        return [len(group) for group in pieces[1:]]

    def out(e, halves, prev, deps):
        flat = flatten(halves)
        last = e == local - 1
        dense_shape = (chips, experts_all, count)
        sum_shape = (chips, 2, count, width)
        return call(
            functools.partial(out_kernel, n, e, e > 0, last, sizes_of(halves[0]), len(deps)),
            1,
            [SMEM_SPEC]
            + [ANY_SPEC] * len(deps)
            + w_specs
            + ([whole_spec(sum_shape)] * 2 if e > 0 else [])
            + [spec_of(x) for x in flat]
            + [HBM_SPEC] * 3,
            [whole_spec(sum_shape)] * 2
            + [whole_spec(TOKEN)]
            + ([whole_spec(dense_shape)] * 2 if last else []),
            [like(sum_shape, BF16 if last else F32)] * 2
            + [like(TOKEN, F32)]
            + ([like(dense_shape, F32)] * 2 if last else []),
            6 * mac,
            3 * weight_bytes + len(flat) * piece_bytes,
            scratch_shapes=held_weights
            + [pltpu.VMEM(slot_shape, BF16)] * 2
            + ([pltpu.VMEM((n, extra, 128), BF16)] if last else []),
        )(scal, *deps, *w_all, *prev, *flat, *weights)

    def grad(e, slots, halves, prev, deps):
        flat = flatten(halves)
        base = 3 + len(deps) + len(flat)
        return call(
            functools.partial(grad_kernel, n, e > 0, sizes_of(halves[0]), len(deps)),
            2,
            [SMEM_SPEC]
            + [whole_spec(slot_shape)] * 2
            + [ANY_SPEC] * len(deps)
            + [spec_of(x) for x in flat]
            + ([ANY_SPEC] * 3 if e > 0 else []),
            grad_specs(e) + [whole_spec(TOKEN)],
            [like(w.shape) for w in weights] + [like(TOKEN, F32)],
            6 * mac,
            3 * weight_bytes + len(flat) * piece_bytes,
            input_output_aliases={base + k: k for k in range(3)} if e > 0 else {},
        )(scal, *slots, *deps, *flat, *prev)

    along_z = Line("dp", n, 1)

    def outer(value):
        return along_z.send(value, [(0, 1), (1, 0), (2, 3), (3, 2)])

    def inner(value):
        return along_z.send(value, [(1, 2), (2, 1), (0, 0), (3, 3)])

    def after(token):
        return at_end if token is None else at_end & (token[0, 0] == 0.0)

    def unless(end, value):
        return jnp.where(end, jnp.zeros_like(value), value)

    products, sums, grads = [], [], []

    def send_home(near, far, add):
        near = add(near, across.send(far, swap))
        right, left = along_x.scatter([near[q] for q in range(chips)], add)
        home = near[0].astype(F32) + right.astype(F32)
        return near, home if left is None else home + left.astype(F32)

    if swaps:
        flight, arrived = [None, None], None
        slots, parts, pre_token = pre(0, [])
        grad_token = None
        for e in range(local):
            more = e < local - 1
            first, second, totals, halves = [], [], [], []
            for h in range(2):
                x = parts[h]
                if e == 0:
                    first.append((outer(x[3]), None))
                else:
                    y, got_a, got_b = flight[h]
                    end = after(grad_token if h == 0 else None)
                    first.append((outer(jnp.where(end, x[3], got_b)), inner(got_a)))
            if more:
                begun = pre(e + 1, [first[0][0]] if e == 0 else [flight[1][2]])
            for h in range(2):
                x, (a1, b1) = parts[h], first[h]
                end = after(begun[2] if more and h == int(e == 0) else None)
                send_a2 = x[2] if e == 0 else jnp.where(end, x[2], b1)
                second.append((outer(send_a2), inner(unless(end, add_rounded(x[3], a1)))))
                if e > 0:
                    y, got_a, got_b = flight[h]
                    halves.append([(y,), (got_a,), (a1, got_b), (second[h][0], b1)])
            for h in range(2):
                x, (a2, b2) = parts[h], second[h]
                a3 = outer(add_rounded(x[1], b2))
                b3 = inner(unless(at_end, add_rounded(x[2], a2)))
                totals.append((x[0], a3, b3))
            wait = []
            if e > 0:
                *sums, out_token = out(e - 1, halves, sums, [])
                wait = [out_token]
            for h in range(2):
                y, product = mid(e, h, totals[h], products, wait if h == 0 else [])
                products.append(product)
                flight[h] = (y, outer(y), inner(y))
            if e > 0:
                *grads, grad_token = grad(e - 1, arrived, halves, grads, [flight[1][0]])
            arrived = slots
            if more:
                slots, parts, _ = begun
        halves = []
        for h in range(2):
            y, got_a, got_b = flight[h]
            a1, b1 = outer(got_b), inner(got_a)
            a2 = outer(b1)
            halves.append([(y,), (got_a,), (a1, got_b), (a2, b1)])
        wait = [grad_token]
    else:
        begun = []
        for e in range(local):
            slots, parts, _ = pre(e, [])
            begun.append((slots, [(x[0], *along_z.scatter(x, add_rounded)) for x in parts]))
        for e in range(local):
            halves, arrived, wait = [], begun[e][0], []
            for h in range(2):
                y, product = mid(e, h, begun[e][1][h], products)
                products.append(product)
                halves.append([(y,)] + along_z.gather(y))
            if e < local - 1:
                *sums, _ = out(e, halves, sums, [])
                *grads, _ = grad(e, arrived, halves, grads, [])

    near, far, _, near_p, far_p = out(local - 1, halves, sums, wait)
    hop, home = send_home(near, far, add_rounded)
    _, per_expert = send_home(near_p, far_p, lambda a, b: a + b)
    *grads, _ = grad(local - 1, arrived, halves, grads, [hop])
    combine_grad = jnp.sum(jnp.where(named, per_expert[None], 0.0), axis=1) / combine_t
    return (home[0].astype(BF16), home[1].astype(BF16), *grads, combine_grad.T)


def solution(mesh):
    return jax.shard_map(
        body,
        mesh=mesh,
        in_specs=(
            P(("group", "expert"), "dp"),
            P(("group", "expert"), None),
            P(("group", "expert"), None),
            P("expert", "dp", None),
            P("expert", "dp", None),
            P("expert", None, "dp"),
            P(("group", "expert"), "dp"),
        ),
        out_specs=(
            P(("group", "expert"), "dp"),
            P(("group", "expert"), "dp"),
            P(("group", "expert"), "dp", None),
            P(("group", "expert"), "dp", None),
            P(("group", "expert"), None, "dp"),
            P(("group", "expert"), None),
        ),
        check_vma=False,
    )
```

```python
import functools

import jax
import jax.numpy as jnp
from jax import lax
from jax.experimental import pallas as pl
from jax.experimental.pallas import tpu as pltpu
from jax.sharding import PartitionSpec as P

F32, BF16 = jnp.float32, jnp.bfloat16
VMEM_BYTES = 20 << 20


def line_pairs(n, gather, step):
    if gather:
        senders = [i for i in range(step - 1, n - 1)]
    else:
        senders = [i for i in range(0, min(step, n - 1))]
    right = [(i, i + 1) for i in senders]
    left = [(n - 1 - i, n - 2 - i) for i in senders]
    return right, left


class Line:
    def __init__(self, axis, n, stride):
        self.axis, self.n, self.stride = axis, n, stride

    def send(self, value, pairs):
        wide = [
            (a * self.stride + c, b * self.stride + c) for a, b in pairs for c in range(self.stride)
        ]
        return lax.ppermute(value, self.axis, wide)

    def gather(self, own):
        n = self.n
        if n == 2:
            both = self.send(own, [(0, 1), (1, 0)])
            return [(both, both)]
        right, left, rights, lefts = own, own, [], []
        for step in range(1, n):
            pairs_r, pairs_l = line_pairs(n, True, step)
            right, left = self.send(right, pairs_r), self.send(left, pairs_l)
            rights.append(right)
            lefts.append(left)
        return [(rights[q - 1], lefts[n - q - 1]) for q in range(1, n)]

    def scatter(self, parts, add):
        n = self.n
        if n == 2:
            return self.send(parts[1], [(0, 1), (1, 0)]), None
        right, left = parts[1], parts[n - 1]
        for step in range(1, n):
            pairs_r, pairs_l = line_pairs(n, False, step)
            right, left = self.send(right, pairs_r), self.send(left, pairs_l)
            if step < n - 1:
                right, left = add(parts[step + 1], right), add(parts[n - 1 - step], left)
        return right, left


def add_rounded(a, b):
    return (a.astype(F32) + b.astype(F32)).astype(BF16)


def dot(a, b, dims=((1,), (0,))):
    return lax.dot_general(a, b, (dims, ((), ())), preferred_element_type=F32)


def routing(scal, names, scales, expert, rows):
    n = len(names)
    tokens = names[0].shape[1]
    which = scal[2 * n] + expert
    hits = [ids[...] == which for ids in names]
    weights = [
        jnp.sum(jnp.where(hit, scale[...], 0.0), axis=0, keepdims=True)
        for hit, scale in zip(hits, scales)
    ]
    chosen = jnp.concatenate(
        [jnp.sum(jnp.where(hit, 1.0, 0.0), axis=0, keepdims=True) for hit in hits], axis=0
    )
    earlier = lax.broadcasted_iota(jnp.int32, (tokens, tokens), 0) < lax.broadcasted_iota(
        jnp.int32, (tokens, tokens), 1
    )
    slots = dot(chosen.astype(BF16), earlier.astype(F32).astype(BF16))
    slots = jnp.where(chosen > 0.0, slots, -1.0).astype(jnp.int32)
    row = lax.broadcasted_iota(jnp.int32, (rows, tokens), 0)
    return [(scal[k], weights[k], row == slots[k : k + 1]) for k in range(n)]


def span_of(position, rows):
    return pl.ds(pl.multiple_of(position * rows, rows), rows)


def weight_copies(expert, weights, held, sems):
    halves = []
    for h in range(2):
        copies = []
        for k, (source, target) in enumerate(zip(weights, held)):
            size = target.shape[0 if k == 2 else 1] // 2
            span = pl.ds(h * size, size)
            src, dst = (
                (source.at[expert, span, :], target.at[span, :])
                if k == 2
                else (source.at[expert, :, span], target.at[:, span])
            )
            copies.append(pltpu.make_async_copy(src, dst, sems.at[h, k]))
        halves.append(copies)
    return halves


def pre_kernel(n, expert, deps, scal, *refs):
    refs = refs[deps:]
    names, scales, toks, ogs, refs = *(refs[k * n : (k + 1) * n] for k in range(4)), refs[4 * n :]
    weights, (in_ref, cot_ref, *refs) = refs[:3], refs[3:]
    outs, (token, gw, uw, dw, sems) = refs[: 2 * n], refs[2 * n :]
    rows, tile = in_ref.shape[0] // n, gw.shape[1] // 2
    copies = weight_copies(expert, weights, (gw, uw, dw), sems)
    for group in copies:
        for copy in group:
            copy.start()
    token[...] = jnp.zeros_like(token)
    for k, (position, weight, hit) in enumerate(routing(scal, names, scales, expert, rows)):
        pick = hit.astype(F32).astype(BF16)
        span = span_of(position, rows)
        in_ref[span, :] = dot(pick, toks[k][...]).astype(BF16)
        scale = jnp.sum(jnp.where(hit, weight, 0.0), axis=1, keepdims=True)
        cot_ref[span, :] = (dot(pick, ogs[k][...]) * scale).astype(BF16)
    for h in range(2):
        for copy in copies[h]:
            copy.wait()
        part = slice(h * tile, (h + 1) * tile)
        gate = dot(in_ref[...], gw[:, part]).astype(BF16)
        up = dot(in_ref[...], uw[:, part]).astype(BF16)
        back = dot(cot_ref[...], dw[part, :], ((1,), (1,))).astype(BF16)
        for p in range(n):
            for k, value in enumerate((gate, up, back)):
                outs[h * n + p][pl.ds(k * rows, rows), :] = value[p * rows : (p + 1) * rows]


def thirds(value):
    high = value.astype(BF16)
    rest = value - high.astype(F32)
    middle = rest.astype(BF16)
    return high, middle, (rest - middle.astype(F32)).astype(BF16)


def mid_kernel(deps, others, *refs):
    own, right, left, *rest = refs[deps:]
    earlier, (out, product) = rest[:others], rest[others:]
    rows, tile = own.shape[0] // 3, own.shape[1]
    total = own[...].astype(F32) + right[...].astype(F32) + left[...].astype(F32)
    gate, up, back = (total[k * rows : (k + 1) * rows] for k in range(3))
    sig = jax.nn.sigmoid(gate)
    hidden = (gate * sig * up).astype(BF16)
    delta = back.astype(BF16).astype(F32)
    out[0:rows, :] = hidden
    out[rows : 2 * rows, :] = (delta * up * sig * (1.0 + gate * (1.0 - sig))).astype(BF16)
    out[2 * rows : 3 * rows, :] = (delta * (gate * sig)).astype(BF16)
    prod = hidden.astype(F32) * back
    lanes = product.shape[1]
    acc = prod[:, 0:lanes]
    for k in range(1, tile // lanes):
        acc = acc + prod[:, k * lanes : (k + 1) * lanes]
    product[...] = acc
    if others:
        partial = [ref[...] for ref in earlier] + [acc]
        ones, fill = jnp.ones((8, lanes), BF16), jnp.zeros((lanes - rows, lanes), F32)
        lines = []
        for e in range(len(partial) // 2):
            wide = jnp.concatenate([partial[2 * e] + partial[2 * e + 1], fill], axis=0)
            total = sum(dot(ones, part, ((1,), (1,))) for part in thirds(wide))[0:1]
            lines += [part.astype(F32) for part in thirds(total)]
        extra = out.shape[0] - 3 * rows
        lines.append(jnp.zeros((extra - len(lines), lanes), F32))
        out[3 * rows :, :] = jnp.zeros((extra, tile), BF16)
        out[3 * rows :, 0:lanes] = jnp.concatenate(lines, axis=0).astype(BF16)


def add_kernel(deps, *refs):
    a, b, out = refs[deps:]
    out[...] = (a[...].astype(F32) + b[...].astype(F32)).astype(BF16)


def part_of(scal, n, q, group, start, size):
    span = pl.ds(start, size)
    if len(group) == 1:
        return group[0][span, :]
    return jnp.where(scal[n + q] > 0, group[0][span, :], group[1][span, :])


def load_rows(scal, n, which, pieces):
    rows = pieces[0][0].shape[0] // 48 * 16
    return jnp.concatenate(
        [part_of(scal, n, q, group, which * rows, rows) for q, group in enumerate(pieces)], axis=0
    )


def split_pieces(refs, sizes):
    halves, at = [], 0
    for _ in range(2):
        pieces = [refs[at : at + 1]]
        at += 1
        for size in sizes:
            pieces.append(refs[at : at + size])
            at += size
        halves.append(pieces)
    return halves, refs[at:]


def out_kernel(n, expert, has_prev, last, sizes, deps, scal, *refs):
    refs = refs[deps:]
    names, scales, refs = refs[:n], refs[n : 2 * n], refs[2 * n :]
    if has_prev:
        prev, refs = refs[:2], refs[2:]
    halves, refs = split_pieces(refs, sizes)
    weights, (near, far, token, *refs) = refs[:3], refs[3:]
    if last:
        near_p, far_p, *refs, held = refs
    gw, uw, dw, sems, eo_ref, idl_ref = refs
    copies = weight_copies(expert, weights, (gw, uw, dw), sems)
    for group in copies:
        for copy in group:
            copy.start()
    token[...] = jnp.zeros_like(token)
    routes = routing(scal, names, scales, expert, halves[0][0][0].shape[0] // 48 * 16)
    if last:
        send_products(scal, names, scales, expert + 1, halves[1], held, near_p, far_p)
    tile = gw.shape[1] // 2
    eo, idl = 0.0, 0.0
    for h in range(2):
        for copy in copies[h]:
            copy.wait()
        part = slice(h * tile, (h + 1) * tile)
        eo = eo + dot(load_rows(scal, n, 0, halves[h]), dw[part, :])
        idl = idl + dot(load_rows(scal, n, 1, halves[h]), gw[:, part], ((1,), (1,)))
        idl = idl + dot(load_rows(scal, n, 2, halves[h]), uw[:, part], ((1,), (1,)))
    rows = eo.shape[0] // n
    eo_ref[...], idl_ref[...] = eo.astype(BF16), idl.astype(BF16)
    for k, (position, weight, hit) in enumerate(routes):
        pick = hit.astype(F32)
        scaled = (pick * weight).astype(BF16)
        span = span_of(position, rows)
        layer = dot(scaled, eo_ref[span, :], ((0,), (0,)))
        back = dot(pick.astype(BF16), idl_ref[span, :], ((0,), (0,)))
        which, place = (near, k) if k < n // 2 else (far, k - n // 2)
        if has_prev:
            before = prev[0 if k < n // 2 else 1]
            layer, back = layer + before[place, 0], back + before[place, 1]
        which[place, 0] = layer.astype(which.dtype)
        which[place, 1] = back.astype(which.dtype)


def grad_kernel(n, has_prev, sizes, deps, scal, in_ref, cot_ref, *refs):
    refs = refs[deps:]
    halves, refs = split_pieces(refs, sizes)
    if has_prev:
        refs = refs[3:]
    gg, ug, dg, token = refs
    step = pl.program_id(0)
    token[...] = jnp.zeros_like(token)
    for h in range(2):

        @pl.when(step == h)
        def _():
            gg[0] = dot(in_ref[...], load_rows(scal, n, 1, halves[h]), ((0,), (0,))).astype(BF16)
            ug[0] = dot(in_ref[...], load_rows(scal, n, 2, halves[h]), ((0,), (0,))).astype(BF16)
            dg[0] = dot(load_rows(scal, n, 0, halves[h]), cot_ref[...], ((0,), (0,))).astype(BF16)


def send_products(scal, names, scales, local, pieces, held, near, far):
    n, (_, extra, lanes) = len(names), held.shape
    first = pieces[0][0].shape[0] - extra
    for q, group in enumerate(pieces):
        held[q] = part_of(scal, n, q, group, first, extra)[:, 0:lanes]
    experts_all, tokens = near.shape[1:]
    ids = lax.broadcasted_iota(jnp.int32, (experts_all, tokens), 0)
    sums = [jnp.zeros((experts_all, tokens), F32) for _ in range(n)]
    for e in range(local):
        for k, (position, _, hit) in enumerate(routing(scal, names, scales, e, lanes)):
            found = dot(held[position], hit.astype(F32).astype(BF16))
            value = found[3 * e : 3 * e + 1] + found[3 * e + 1 : 3 * e + 2] + found[3 * e + 2 : 3 * e + 3]
            sums[k] = sums[k] + jnp.where(ids == scal[2 * n] + e, value, 0.0)
    for k in range(n):
        if k < n // 2:
            near[k] = sums[k]
        else:
            far[k - n // 2] = sums[k]


def in_hbm(array):
    return pltpu.with_memory_space_constraint(array, pltpu.HBM)


def whole_spec(shape):
    return pl.BlockSpec(tuple(shape), lambda g: (0,) * len(shape))


def spec_of(array):
    return whole_spec(array.shape)


def like(shape, dtype=BF16):
    return jax.ShapeDtypeStruct(tuple(shape), dtype)


SMEM_SPEC = pl.BlockSpec(memory_space=pltpu.SMEM)
ANY_SPEC = pl.BlockSpec(memory_space=pl.ANY)
HBM_SPEC = pl.BlockSpec(memory_space=pltpu.HBM)
TOKEN = (8, 128)


def call(kernel, grid, in_specs, out_specs, out_shape, flops, moved, **rest):
    return pl.pallas_call(
        kernel,
        grid=(grid,),
        in_specs=in_specs,
        out_specs=out_specs,
        out_shape=out_shape,
        compiler_params=pltpu.CompilerParams(vmem_limit_bytes=VMEM_BYTES),
        cost_estimate=pl.CostEstimate(flops=flops, bytes_accessed=moved, transcendentals=0),
        **rest,
    )


def body(tokens, expert_ids, combine, gate_weight, up_weight, down_weight, out_grad):
    peers, n = lax.axis_size("expert"), lax.axis_size("dp")
    assert peers == n
    chips = peers // 2
    local, width, hidden = gate_weight.shape
    count, choose = expert_ids.shape
    experts_all = peers * local
    capacity = count * choose * 5 // (4 * experts_all)
    rows = -(-capacity // 16) * 16
    all_rows = n * rows
    tile = hidden // 2
    swaps = n == 4

    me, here = lax.axis_index("expert"), lax.axis_index("dp")
    at_end = (here == 0) | (here == n - 1)
    table = []
    for place in range(n):
        block = 2 * lax.rem(me // 2 - place % chips + chips, chips) + lax.rem(
            lax.rem(me, 2) + place // chips, 2
        )
        if swaps:
            across_middle = jnp.where((block == 0) | (block == 3), 3, 2)
            position = jnp.where(
                block == here, 0, jnp.where(block // 2 == here // 2, 1, across_middle)
            )
        else:
            position = lax.rem(here - block + n, n)
        table.append(position)
    flags = [at_end if swaps else here >= q for q in range(n)]
    scal = jnp.stack(
        [jnp.asarray(v).astype(jnp.int32) for v in table + flags + [me * local, at_end]]
    )

    ids_t, combine_t = expert_ids.T, combine.T
    named = ids_t[:, None, :] == jnp.arange(experts_all, dtype=jnp.int32)[None, :, None]

    along_x, across = Line("expert", chips, 2), Line("expert", peers, 1)
    swap = [(2 * x + c, 2 * x + 1 - c) for x in range(chips) for c in range(2)]

    def gather_blocks(own):
        found = [own] + [
            right if right is left else jnp.where(me // 2 >= q, right, left)
            for q, (right, left) in enumerate(along_x.gather(own), 1)
        ]
        return found + [across.send(piece, swap) for piece in found]

    routes = gather_blocks(ids_t) + gather_blocks(combine_t)
    blocks = gather_blocks(tokens) + gather_blocks(out_grad)
    for held in (routes, blocks):
        held[0], held[n] = in_hbm(held[0]), in_hbm(held[n])
    route_specs, block_specs = [spec_of(x) for x in routes], [spec_of(x) for x in blocks]

    mac = all_rows * width * hidden
    weight_bytes = 2 * width * hidden
    piece_shape = (3 * rows, tile)
    extra = -(-3 * local // 16) * 16
    wide_shape = (3 * rows + extra, tile)
    piece_bytes = 2 * 3 * rows * tile
    slot_shape = (all_rows, width)

    weights = [in_hbm(w) for w in (gate_weight, up_weight, down_weight)]
    held_weights = [pltpu.VMEM(w.shape[1:], BF16) for w in weights] + [
        pltpu.SemaphoreType.DMA((2, 3))
    ]

    def grad_specs(e):
        wide = pl.BlockSpec((1, width, tile), lambda g: (e, 0, g))
        return [wide, wide, pl.BlockSpec((1, tile, width), lambda g: (e, g, 0))]

    def pre(e, deps):
        inputs, cot, *parts, token = call(
            functools.partial(pre_kernel, n, e, len(deps)),
            1,
            [SMEM_SPEC] + [ANY_SPEC] * len(deps) + route_specs + block_specs + [HBM_SPEC] * 3,
            [whole_spec(slot_shape)] * 2 + [whole_spec(piece_shape)] * (2 * n) + [whole_spec(TOKEN)],
            [like(slot_shape)] * 2 + [like(piece_shape)] * (2 * n) + [like(TOKEN, F32)],
            6 * mac,
            3 * weight_bytes + 2 * n * piece_bytes,
            scratch_shapes=held_weights,
        )(scal, *deps, *routes, *blocks, *weights)
        return (inputs, cot), [parts[:n], parts[n:]], token

    def mid(e, h, totals, products, deps=()):
        others = products if e == local - 1 and h == 1 else []
        shape = wide_shape if others else piece_shape
        return call(
            functools.partial(mid_kernel, len(deps), len(others)),
            1,
            [ANY_SPEC] * len(deps)
            + [whole_spec(piece_shape)] * 3
            + [whole_spec((rows, 128))] * len(others),
            [whole_spec(shape), whole_spec((rows, 128))],
            [like(shape), like((rows, 128), F32)],
            20 * rows * tile,
            4 * piece_bytes,
        )(*deps, *totals, *others)

    def add(a, b, deps):
        return call(
            functools.partial(add_kernel, len(deps)),
            1,
            [ANY_SPEC] * len(deps) + [whole_spec(piece_shape)] * 2,
            whole_spec(piece_shape),
            like(piece_shape),
            3 * rows * tile,
            3 * piece_bytes,
        )(*deps, a, b)

    def flatten(halves):
        return [x for pieces in halves for group in pieces for x in group]

    def sizes_of(pieces):
        return [len(group) for group in pieces[1:]]

    def out(e, halves, prev, deps):
        flat = flatten(halves)
        last = e == local - 1
        dense_shape = (chips, experts_all, count)
        sum_shape = (chips, 2, count, width)
        return call(
            functools.partial(out_kernel, n, e, e > 0, last, sizes_of(halves[0]), len(deps)),
            1,
            [SMEM_SPEC]
            + [ANY_SPEC] * len(deps)
            + route_specs
            + ([whole_spec(sum_shape)] * 2 if e > 0 else [])
            + [spec_of(x) for x in flat]
            + [HBM_SPEC] * 3,
            [whole_spec(sum_shape)] * 2
            + [whole_spec(TOKEN)]
            + ([whole_spec(dense_shape)] * 2 if last else []),
            [like(sum_shape, BF16 if last else F32)] * 2
            + [like(TOKEN, F32)]
            + ([like(dense_shape, F32)] * 2 if last else []),
            6 * mac,
            3 * weight_bytes + len(flat) * piece_bytes,
            scratch_shapes=held_weights
            + [pltpu.VMEM(slot_shape, BF16)] * 2
            + ([pltpu.VMEM((n, extra, 128), BF16)] if last else []),
        )(scal, *deps, *routes, *prev, *flat, *weights)

    def grad(e, slots, halves, prev, deps):
        flat = flatten(halves)
        base = 3 + len(deps) + len(flat)
        return call(
            functools.partial(grad_kernel, n, e > 0, sizes_of(halves[0]), len(deps)),
            2,
            [SMEM_SPEC]
            + [whole_spec(slot_shape)] * 2
            + [ANY_SPEC] * len(deps)
            + [spec_of(x) for x in flat]
            + ([ANY_SPEC] * 3 if e > 0 else []),
            grad_specs(e) + [whole_spec(TOKEN)],
            [like(w.shape) for w in weights] + [like(TOKEN, F32)],
            6 * mac,
            3 * weight_bytes + len(flat) * piece_bytes,
            input_output_aliases={base + k: k for k in range(3)} if e > 0 else {},
        )(scal, *slots, *deps, *flat, *prev)

    along_z = Line("dp", n, 1)

    def outer(value):
        return along_z.send(value, [(0, 1), (1, 0), (2, 3), (3, 2)])

    def inner(value):
        return along_z.send(value, [(1, 2), (2, 1), (0, 0), (3, 3)])

    def unless_end(value):
        return jnp.where(at_end, jnp.zeros_like(value), value)

    products, sums, grads = [], [], []

    def send_home(near, far, add):
        near = add(near, across.send(far, swap))
        right, left = along_x.scatter([near[q] for q in range(chips)], add)
        home = near[0].astype(F32) + right.astype(F32)
        return near, home if left is None else home + left.astype(F32)

    if swaps:
        flight, arrived = [None, None], None
        slots, parts, _ = pre(0, [])
        grad_token = None
        for e in range(local):
            more = e < local - 1
            first, second, totals, halves = [], [], [], []
            for h in range(2):
                x = parts[h]
                if e == 0:
                    first.append((outer(x[3]), None))
                else:
                    y, got_a, got_b = flight[h]
                    first.append((outer(jnp.where(at_end, x[3], got_b)), inner(got_a)))
            if more:
                begun = pre(e + 1, [first[0][0]] if e == 0 else [flight[1][2]])
            for h in range(2):
                x, (a1, b1) = parts[h], first[h]
                tokens_seen = [begun[2]] if more and h == 1 else []
                if grad_token is not None and h == 0:
                    tokens_seen = [grad_token]
                send_a2 = x[2] if e == 0 else jnp.where(at_end, x[2], b1)
                second.append((outer(send_a2), inner(add(x[3], a1, tokens_seen))))
                if e > 0:
                    y, got_a, got_b = flight[h]
                    halves.append([(y,), (got_a,), (a1, got_b), (second[h][0], b1)])
            for h in range(2):
                x, (a2, b2) = parts[h], second[h]
                a3 = outer(jnp.where(at_end, x[1], add_rounded(x[1], b2)))
                b3 = inner(unless_end(add_rounded(x[2], a2)))
                totals.append((x[0], a3, b3))
            wait = []
            if e > 0:
                *sums, out_token = out(e - 1, halves, sums, [])
                wait = [out_token]
            for h in range(2):
                y, product = mid(e, h, totals[h], products, wait if h == 0 else [])
                products.append(product)
                flight[h] = (y, outer(y), inner(y))
            if e > 0:
                *grads, grad_token = grad(e - 1, arrived, halves, grads, [flight[1][0]])
            arrived = slots
            if more:
                slots, parts, _ = begun
        halves = []
        for h in range(2):
            y, got_a, got_b = flight[h]
            a1, b1 = outer(got_b), inner(got_a)
            a2 = outer(b1)
            halves.append([(y,), (got_a,), (a1, got_b), (a2, b1)])
        wait = [grad_token]
    else:
        begun = []
        for e in range(local):
            slots, parts, _ = pre(e, [])
            begun.append((slots, [(x[0], *along_z.scatter(x, add_rounded)) for x in parts]))
        for e in range(local):
            halves, arrived, wait = [], begun[e][0], []
            for h in range(2):
                y, product = mid(e, h, begun[e][1][h], products)
                products.append(product)
                halves.append([(y,)] + along_z.gather(y))
            if e < local - 1:
                *sums, _ = out(e, halves, sums, [])
                *grads, _ = grad(e, arrived, halves, grads, [])

    near, far, _, near_p, far_p = out(local - 1, halves, sums, wait)
    hop, home = send_home(near, far, add_rounded)
    _, per_expert = send_home(near_p, far_p, lambda a, b: a + b)
    *grads, _ = grad(local - 1, arrived, halves, grads, [hop])
    combine_grad = jnp.sum(jnp.where(named, per_expert[None], 0.0), axis=1) / combine_t
    return (home[0].astype(BF16), home[1].astype(BF16), *grads, combine_grad.T)


def solution(mesh):
    return jax.shard_map(
        body,
        mesh=mesh,
        in_specs=(
            P(("group", "expert"), "dp"),
            P(("group", "expert"), None),
            P(("group", "expert"), None),
            P("expert", "dp", None),
            P("expert", "dp", None),
            P("expert", None, "dp"),
            P(("group", "expert"), "dp"),
        ),
        out_specs=(
            P(("group", "expert"), "dp"),
            P(("group", "expert"), "dp"),
            P(("group", "expert"), "dp", None),
            P(("group", "expert"), "dp", None),
            P(("group", "expert"), None, "dp"),
            P(("group", "expert"), None),
        ),
        check_vma=False,
    )
```

```python
import functools

import jax
import jax.numpy as jnp
from jax import lax
from jax.experimental import pallas as pl
from jax.experimental.pallas import tpu as pltpu
from jax.sharding import PartitionSpec as P

F32, BF16 = jnp.float32, jnp.bfloat16
VMEM_BYTES = 20 << 20


def line_pairs(n, gather, step):
    if gather:
        senders = [i for i in range(step - 1, n - 1)]
    else:
        senders = [i for i in range(0, min(step, n - 1))]
    right = [(i, i + 1) for i in senders]
    left = [(n - 1 - i, n - 2 - i) for i in senders]
    return right, left


class Line:
    def __init__(self, axis, n, stride):
        self.axis, self.n, self.stride = axis, n, stride

    def send(self, value, pairs):
        wide = [
            (a * self.stride + c, b * self.stride + c) for a, b in pairs for c in range(self.stride)
        ]
        return lax.ppermute(value, self.axis, wide)

    def gather(self, own):
        n = self.n
        if n == 2:
            both = self.send(own, [(0, 1), (1, 0)])
            return [(both, both)]
        right, left, rights, lefts = own, own, [], []
        for step in range(1, n):
            pairs_r, pairs_l = line_pairs(n, True, step)
            right, left = self.send(right, pairs_r), self.send(left, pairs_l)
            rights.append(right)
            lefts.append(left)
        return [(rights[q - 1], lefts[n - q - 1]) for q in range(1, n)]

    def scatter(self, parts, add):
        n = self.n
        if n == 2:
            return self.send(parts[1], [(0, 1), (1, 0)]), None
        right, left = parts[1], parts[n - 1]
        for step in range(1, n):
            pairs_r, pairs_l = line_pairs(n, False, step)
            right, left = self.send(right, pairs_r), self.send(left, pairs_l)
            if step < n - 1:
                right, left = add(parts[step + 1], right), add(parts[n - 1 - step], left)
        return right, left


def add_rounded(a, b):
    return (a.astype(F32) + b.astype(F32)).astype(BF16)


def dot(a, b, dims=((1,), (0,))):
    return lax.dot_general(a, b, (dims, ((), ())), preferred_element_type=F32)


def routing(scal, routes, expert, rows):
    n = len(routes)
    choose, tokens = routes[0].shape[0] // 2, routes[0].shape[1]
    which = (scal[2 * n] + expert).astype(F32)
    hits = [route[0:choose, :] == which for route in routes]
    weights = [
        jnp.sum(jnp.where(hit, route[choose:, :], 0.0), axis=0, keepdims=True)
        for hit, route in zip(hits, routes)
    ]
    chosen = jnp.concatenate(
        [jnp.sum(jnp.where(hit, 1.0, 0.0), axis=0, keepdims=True) for hit in hits], axis=0
    )
    earlier = lax.broadcasted_iota(jnp.int32, (tokens, tokens), 0) < lax.broadcasted_iota(
        jnp.int32, (tokens, tokens), 1
    )
    slots = dot(chosen.astype(BF16), earlier.astype(F32).astype(BF16))
    slots = jnp.where(chosen > 0.0, slots, -1.0).astype(jnp.int32)
    row = lax.broadcasted_iota(jnp.int32, (rows, tokens), 0)
    return [(scal[k], weights[k], row == slots[k : k + 1]) for k in range(n)]


def span_of(position, rows):
    return pl.ds(pl.multiple_of(position * rows, rows), rows)


def weight_copies(expert, weights, held, sems):
    halves = []
    for h in range(2):
        copies = []
        for k, (source, target) in enumerate(zip(weights, held)):
            size = target.shape[0 if k == 2 else 1] // 2
            span = pl.ds(h * size, size)
            src, dst = (
                (source.at[expert, span, :], target.at[span, :])
                if k == 2
                else (source.at[expert, :, span], target.at[:, span])
            )
            copies.append(pltpu.make_async_copy(src, dst, sems.at[h, k]))
        halves.append(copies)
    return halves


def pre_kernel(n, expert, deps, scal, *refs):
    refs = refs[deps:]
    routes, packs, refs = refs[:n], refs[n : 2 * n], refs[2 * n :]
    weights, (in_ref, cot_ref, *refs) = refs[:3], refs[3:]
    outs, (token, gw, uw, dw, sems) = refs[: 2 * n], refs[2 * n :]
    rows, tile = in_ref.shape[0] // n, gw.shape[1] // 2
    copies = weight_copies(expert, weights, (gw, uw, dw), sems)
    for group in copies:
        for copy in group:
            copy.start()
    token[...] = jnp.zeros_like(token)
    for k, (position, weight, hit) in enumerate(routing(scal, routes, expert, rows)):
        pick = hit.astype(F32).astype(BF16)
        span = span_of(position, rows)
        in_ref[span, :] = dot(pick, packs[k][0]).astype(BF16)
        scale = jnp.sum(jnp.where(hit, weight, 0.0), axis=1, keepdims=True)
        cot_ref[span, :] = (dot(pick, packs[k][1]) * scale).astype(BF16)
    for h in range(2):
        for copy in copies[h]:
            copy.wait()
        part = slice(h * tile, (h + 1) * tile)
        gate = dot(in_ref[...], gw[:, part]).astype(BF16)
        up = dot(in_ref[...], uw[:, part]).astype(BF16)
        back = dot(cot_ref[...], dw[part, :], ((1,), (1,))).astype(BF16)
        for p in range(n):
            for k, value in enumerate((gate, up, back)):
                outs[h * n + p][pl.ds(k * rows, rows), :] = value[p * rows : (p + 1) * rows]


def thirds(value):
    high = value.astype(BF16)
    rest = value - high.astype(F32)
    middle = rest.astype(BF16)
    return high, middle, (rest - middle.astype(F32)).astype(BF16)


def mid_kernel(deps, others, *refs):
    own, right, left, *rest = refs[deps:]
    earlier, (out, product) = rest[:others], rest[others:]
    rows, tile = own.shape[0] // 3, own.shape[1]
    total = own[...].astype(F32) + right[...].astype(F32) + left[...].astype(F32)
    gate, up, back = (total[k * rows : (k + 1) * rows] for k in range(3))
    sig = jax.nn.sigmoid(gate)
    hidden = (gate * sig * up).astype(BF16)
    delta = back.astype(BF16).astype(F32)
    out[0:rows, :] = hidden
    out[rows : 2 * rows, :] = (delta * up * sig * (1.0 + gate * (1.0 - sig))).astype(BF16)
    out[2 * rows : 3 * rows, :] = (delta * (gate * sig)).astype(BF16)
    prod = hidden.astype(F32) * back
    lanes = product.shape[1]
    acc = prod[:, 0:lanes]
    for k in range(1, tile // lanes):
        acc = acc + prod[:, k * lanes : (k + 1) * lanes]
    product[...] = acc
    if others:
        partial = [ref[...] for ref in earlier] + [acc]
        ones, fill = jnp.ones((8, lanes), BF16), jnp.zeros((lanes - rows, lanes), F32)
        lines = []
        for e in range(len(partial) // 2):
            wide = jnp.concatenate([partial[2 * e] + partial[2 * e + 1], fill], axis=0)
            total = sum(dot(ones, part, ((1,), (1,))) for part in thirds(wide))[0:1]
            lines += [part.astype(F32) for part in thirds(total)]
        extra = out.shape[0] - 3 * rows
        lines.append(jnp.zeros((extra - len(lines), lanes), F32))
        out[3 * rows :, :] = jnp.zeros((extra, tile), BF16)
        out[3 * rows :, 0:lanes] = jnp.concatenate(lines, axis=0).astype(BF16)


def pack_kernel(ids, combine, tokens, grads, pack, route):
    pack[0] = tokens[...]
    pack[1] = grads[...]
    route[0 : ids.shape[0], :] = ids[...].astype(F32)
    route[ids.shape[0] :, :] = combine[...]


def add_kernel(deps, *refs):
    a, b, out = refs[deps:]
    out[...] = (a[...].astype(F32) + b[...].astype(F32)).astype(out.dtype)


def part_of(scal, n, q, group, start, size):
    span = pl.ds(start, size)
    if len(group) == 1:
        return group[0][span, :]
    return jnp.where(scal[n + q] > 0, group[0][span, :], group[1][span, :])


def load_rows(scal, n, which, pieces):
    rows = pieces[0][0].shape[0] // 48 * 16
    return jnp.concatenate(
        [part_of(scal, n, q, group, which * rows, rows) for q, group in enumerate(pieces)], axis=0
    )


def split_pieces(refs, sizes):
    halves, at = [], 0
    for _ in range(2):
        pieces = [refs[at : at + 1]]
        at += 1
        for size in sizes:
            pieces.append(refs[at : at + size])
            at += size
        halves.append(pieces)
    return halves, refs[at:]


def out_kernel(n, expert, has_prev, last, sizes, deps, scal, *refs):
    refs = refs[deps:]
    routes, refs = refs[:n], refs[n:]
    if has_prev:
        prev, refs = refs[:2], refs[2:]
    halves, refs = split_pieces(refs, sizes)
    weights, (near, far, token, *refs) = refs[:3], refs[3:]
    if last:
        near_p, far_p, *refs, held = refs
    gw, uw, dw, sems, eo_ref, idl_ref = refs
    copies = weight_copies(expert, weights, (gw, uw, dw), sems)
    for group in copies:
        for copy in group:
            copy.start()
    token[...] = jnp.zeros_like(token)
    spots = routing(scal, routes, expert, halves[0][0][0].shape[0] // 48 * 16)
    if last:
        send_products(scal, routes, expert + 1, halves[1], held, near_p, far_p)
    tile = gw.shape[1] // 2
    eo, idl = 0.0, 0.0
    for h in range(2):
        for copy in copies[h]:
            copy.wait()
        part = slice(h * tile, (h + 1) * tile)
        eo = eo + dot(load_rows(scal, n, 0, halves[h]), dw[part, :])
        idl = idl + dot(load_rows(scal, n, 1, halves[h]), gw[:, part], ((1,), (1,)))
        idl = idl + dot(load_rows(scal, n, 2, halves[h]), uw[:, part], ((1,), (1,)))
    rows = eo.shape[0] // n
    eo_ref[...], idl_ref[...] = eo.astype(BF16), idl.astype(BF16)
    for k, (position, weight, hit) in enumerate(spots):
        pick = hit.astype(F32)
        scaled = (pick * weight).astype(BF16)
        span = span_of(position, rows)
        layer = dot(scaled, eo_ref[span, :], ((0,), (0,)))
        back = dot(pick.astype(BF16), idl_ref[span, :], ((0,), (0,)))
        which, place = (near, k) if k < n // 2 else (far, k - n // 2)
        if has_prev:
            before = prev[0 if k < n // 2 else 1]
            layer, back = layer + before[place, 0], back + before[place, 1]
        which[place, 0] = layer.astype(which.dtype)
        which[place, 1] = back.astype(which.dtype)


def grad_kernel(n, has_prev, sizes, deps, scal, in_ref, cot_ref, *refs):
    refs = refs[deps:]
    halves, refs = split_pieces(refs, sizes)
    if has_prev:
        refs = refs[3:]
    gg, ug, dg, token = refs
    step = pl.program_id(0)
    token[...] = jnp.zeros_like(token)
    for h in range(2):

        @pl.when(step == h)
        def _():
            gg[0] = dot(in_ref[...], load_rows(scal, n, 1, halves[h]), ((0,), (0,))).astype(BF16)
            ug[0] = dot(in_ref[...], load_rows(scal, n, 2, halves[h]), ((0,), (0,))).astype(BF16)
            dg[0] = dot(load_rows(scal, n, 0, halves[h]), cot_ref[...], ((0,), (0,))).astype(BF16)


def send_products(scal, routes, local, pieces, held, near, far):
    n, (_, extra, lanes) = len(routes), held.shape
    first = pieces[0][0].shape[0] - extra
    for q, group in enumerate(pieces):
        held[q] = part_of(scal, n, q, group, first, extra)[:, 0:lanes]
    experts_all, tokens = near.shape[1:]
    ids = lax.broadcasted_iota(jnp.int32, (experts_all, tokens), 0)
    sums = [jnp.zeros((experts_all, tokens), F32) for _ in range(n)]
    for e in range(local):
        for k, (position, _, hit) in enumerate(routing(scal, routes, e, lanes)):
            found = dot(held[position], hit.astype(F32).astype(BF16))
            value = found[3 * e : 3 * e + 1] + found[3 * e + 1 : 3 * e + 2] + found[3 * e + 2 : 3 * e + 3]
            sums[k] = sums[k] + jnp.where(ids == scal[2 * n] + e, value, 0.0)
    for k in range(n):
        if k < n // 2:
            near[k] = sums[k]
        else:
            far[k - n // 2] = sums[k]


def in_hbm(array):
    return pltpu.with_memory_space_constraint(array, pltpu.HBM)


def whole_spec(shape):
    return pl.BlockSpec(tuple(shape), lambda g: (0,) * len(shape))


def spec_of(array):
    return whole_spec(array.shape)


def like(shape, dtype=BF16):
    return jax.ShapeDtypeStruct(tuple(shape), dtype)


SMEM_SPEC = pl.BlockSpec(memory_space=pltpu.SMEM)
ANY_SPEC = pl.BlockSpec(memory_space=pl.ANY)
HBM_SPEC = pl.BlockSpec(memory_space=pltpu.HBM)
TOKEN = (8, 128)


def call(kernel, grid, in_specs, out_specs, out_shape, flops, moved, **rest):
    return pl.pallas_call(
        kernel,
        grid=(grid,),
        in_specs=in_specs,
        out_specs=out_specs,
        out_shape=out_shape,
        compiler_params=pltpu.CompilerParams(vmem_limit_bytes=VMEM_BYTES),
        cost_estimate=pl.CostEstimate(flops=flops, bytes_accessed=moved, transcendentals=0),
        **rest,
    )


def body(tokens, expert_ids, combine, gate_weight, up_weight, down_weight, out_grad):
    peers, n = lax.axis_size("expert"), lax.axis_size("dp")
    assert peers == n
    chips = peers // 2
    local, width, hidden = gate_weight.shape
    count, choose = expert_ids.shape
    experts_all = peers * local
    capacity = count * choose * 5 // (4 * experts_all)
    rows = -(-capacity // 16) * 16
    all_rows = n * rows
    tile = hidden // 2
    swaps = n == 4

    me, here = lax.axis_index("expert"), lax.axis_index("dp")
    at_end = (here == 0) | (here == n - 1)
    table = []
    for place in range(n):
        block = 2 * lax.rem(me // 2 - place % chips + chips, chips) + lax.rem(
            lax.rem(me, 2) + place // chips, 2
        )
        if swaps:
            across_middle = jnp.where((block == 0) | (block == 3), 3, 2)
            position = jnp.where(
                block == here, 0, jnp.where(block // 2 == here // 2, 1, across_middle)
            )
        else:
            position = lax.rem(here - block + n, n)
        table.append(position)
    flags = [at_end if swaps else here >= q for q in range(n)]
    scal = jnp.stack(
        [jnp.asarray(v).astype(jnp.int32) for v in table + flags + [me * local, at_end]]
    )

    ids_t, combine_t = expert_ids.T, combine.T
    named = ids_t[:, None, :] == jnp.arange(experts_all, dtype=jnp.int32)[None, :, None]

    along_x, across = Line("expert", chips, 2), Line("expert", peers, 1)
    swap = [(2 * x + c, 2 * x + 1 - c) for x in range(chips) for c in range(2)]

    def gather_blocks(own):
        found = [own] + [
            right if right is left else jnp.where(me // 2 >= q, right, left)
            for q, (right, left) in enumerate(along_x.gather(own), 1)
        ]
        return found + [across.send(piece, swap) for piece in found]

    pack, route = call(
        pack_kernel,
        1,
        [spec_of(ids_t), spec_of(combine_t), spec_of(tokens), spec_of(out_grad)],
        [whole_spec((2, count, width)), whole_spec((2 * choose, count))],
        [like((2, count, width)), like((2 * choose, count), F32)],
        count * width,
        8 * count * width,
    )(*(in_hbm(x) for x in (ids_t, combine_t, tokens, out_grad)))
    routes, packs = gather_blocks(route), gather_blocks(pack)
    route_specs, pack_specs = [spec_of(x) for x in routes], [spec_of(x) for x in packs]

    mac = all_rows * width * hidden
    weight_bytes = 2 * width * hidden
    piece_shape = (3 * rows, tile)
    extra = -(-3 * local // 16) * 16
    wide_shape = (3 * rows + extra, tile)
    piece_bytes = 2 * 3 * rows * tile
    slot_shape = (all_rows, width)

    weights = [in_hbm(w) for w in (gate_weight, up_weight, down_weight)]
    held_weights = [pltpu.VMEM(w.shape[1:], BF16) for w in weights] + [
        pltpu.SemaphoreType.DMA((2, 3))
    ]

    def grad_specs(e):
        wide = pl.BlockSpec((1, width, tile), lambda g: (e, 0, g))
        return [wide, wide, pl.BlockSpec((1, tile, width), lambda g: (e, g, 0))]

    def pre(e, deps):
        inputs, cot, *parts, token = call(
            functools.partial(pre_kernel, n, e, len(deps)),
            1,
            [SMEM_SPEC] + [ANY_SPEC] * len(deps) + route_specs + pack_specs + [HBM_SPEC] * 3,
            [whole_spec(slot_shape)] * 2 + [whole_spec(piece_shape)] * (2 * n) + [whole_spec(TOKEN)],
            [like(slot_shape)] * 2 + [like(piece_shape)] * (2 * n) + [like(TOKEN, F32)],
            6 * mac,
            3 * weight_bytes + 2 * n * piece_bytes,
            scratch_shapes=held_weights,
        )(scal, *deps, *routes, *packs, *weights)
        return (inputs, cot), [parts[:n], parts[n:]], token

    def mid(e, h, totals, products, deps=()):
        others = products if e == local - 1 and h == 1 else []
        shape = wide_shape if others else piece_shape
        return call(
            functools.partial(mid_kernel, len(deps), len(others)),
            1,
            [ANY_SPEC] * len(deps)
            + [whole_spec(piece_shape)] * 3
            + [whole_spec((rows, 128))] * len(others),
            [whole_spec(shape), whole_spec((rows, 128))],
            [like(shape), like((rows, 128), F32)],
            20 * rows * tile,
            4 * piece_bytes,
        )(*deps, *totals, *others)

    def add(a, b, deps):
        return call(
            functools.partial(add_kernel, len(deps)),
            1,
            [ANY_SPEC] * len(deps) + [spec_of(a)] * 2,
            spec_of(a),
            like(a.shape, a.dtype),
            a.size,
            3 * a.size * a.dtype.itemsize,
        )(*deps, a, b)

    def flatten(halves):
        return [x for pieces in halves for group in pieces for x in group]

    def sizes_of(pieces):
        return [len(group) for group in pieces[1:]]

    def out(e, halves, prev, deps):
        flat = flatten(halves)
        last = e == local - 1
        dense_shape = (chips, experts_all, count)
        sum_shape = (chips, 2, count, width)
        return call(
            functools.partial(out_kernel, n, e, e > 0, last, sizes_of(halves[0]), len(deps)),
            1,
            [SMEM_SPEC]
            + [ANY_SPEC] * len(deps)
            + route_specs
            + ([whole_spec(sum_shape)] * 2 if e > 0 else [])
            + [spec_of(x) for x in flat]
            + [HBM_SPEC] * 3,
            [whole_spec(sum_shape)] * 2
            + [whole_spec(TOKEN)]
            + ([whole_spec(dense_shape)] * 2 if last else []),
            [like(sum_shape, BF16 if last else F32)] * 2
            + [like(TOKEN, F32)]
            + ([like(dense_shape, F32)] * 2 if last else []),
            6 * mac,
            3 * weight_bytes + len(flat) * piece_bytes,
            scratch_shapes=held_weights
            + [pltpu.VMEM(slot_shape, BF16)] * 2
            + ([pltpu.VMEM((n, extra, 128), BF16)] if last else []),
        )(scal, *deps, *routes, *prev, *flat, *weights)

    def grad(e, slots, halves, prev, deps):
        flat = flatten(halves)
        base = 3 + len(deps) + len(flat)
        return call(
            functools.partial(grad_kernel, n, e > 0, sizes_of(halves[0]), len(deps)),
            2,
            [SMEM_SPEC]
            + [whole_spec(slot_shape)] * 2
            + [ANY_SPEC] * len(deps)
            + [spec_of(x) for x in flat]
            + ([ANY_SPEC] * 3 if e > 0 else []),
            grad_specs(e) + [whole_spec(TOKEN)],
            [like(w.shape) for w in weights] + [like(TOKEN, F32)],
            6 * mac,
            3 * weight_bytes + len(flat) * piece_bytes,
            input_output_aliases={base + k: k for k in range(3)} if e > 0 else {},
        )(scal, *slots, *deps, *flat, *prev)

    along_z = Line("dp", n, 1)

    def outer(value):
        return along_z.send(value, [(0, 1), (1, 0), (2, 3), (3, 2)])

    def inner(value):
        pairs = []
        for p in range(peers):
            pairs += [(p * n + 1, p * n + 2), (p * n + 2, p * n + 1)]
            pairs += [(p * n + end, (p ^ 1) * n + end) for end in (0, n - 1)]
        return lax.ppermute(value, ("expert", "dp"), pairs)

    def unless_end(value):
        return jnp.where(at_end, jnp.zeros_like(value), value)

    products, sums, grads = [], [], []

    def send_home(near, far, add):
        near = add(near, across.send(far, swap))
        right, left = along_x.scatter([near[q] for q in range(chips)], add)
        home = near[0].astype(F32) + right.astype(F32)
        return near, home if left is None else home + left.astype(F32)

    if swaps:
        flight, arrived = [None, None], None
        slots, parts, _ = pre(0, [])
        grad_token = None
        for e in range(local):
            more = e < local - 1
            first, second, totals, halves = [], [], [], []
            for h in range(2):
                x = parts[h]
                if e == 0:
                    first.append((outer(x[3]), None))
                else:
                    y, got_a, got_b = flight[h]
                    first.append((outer(jnp.where(at_end, x[3], got_b)), inner(got_a)))
            if more:
                begun = pre(e + 1, [first[0][0]] if e == 0 else [flight[1][2]])
            for h in range(2):
                x, (a1, b1) = parts[h], first[h]
                tokens_seen = [begun[2]] if more and h == 1 else []
                if grad_token is not None and h == 0:
                    tokens_seen = [grad_token]
                send_a2 = x[2] if e == 0 else jnp.where(at_end, x[2], b1)
                second.append((outer(send_a2), inner(add(x[3], a1, tokens_seen))))
                if e > 0:
                    y, got_a, got_b = flight[h]
                    halves.append([(y,), (got_a,), (a1, got_b), (second[h][0], b1)])
            for h in range(2):
                x, (a2, b2) = parts[h], second[h]
                a3 = outer(jnp.where(at_end, x[1], add_rounded(x[1], b2)))
                b3 = inner(unless_end(add_rounded(x[2], a2)))
                totals.append((x[0], a3, b3))
            wait = []
            if e > 0:
                *sums, out_token = out(e - 1, halves, sums, [])
                wait = [out_token]
            for h in range(2):
                y, product = mid(e, h, totals[h], products, wait if h == 0 else [])
                products.append(product)
                flight[h] = (y, outer(y), inner(y))
            if e > 0:
                *grads, grad_token = grad(e - 1, arrived, halves, grads, [flight[1][0]])
            arrived = slots
            if more:
                slots, parts, _ = begun
        halves = []
        for h in range(2):
            y, got_a, got_b = flight[h]
            a1, b1 = outer(got_b), inner(got_a)
            a2 = outer(b1)
            halves.append([(y,), (got_a,), (a1, got_b), (a2, b1)])
        wait = [grad_token]
    else:
        begun = []
        for e in range(local):
            slots, parts, _ = pre(e, [])
            begun.append((slots, [(x[0], *along_z.scatter(x, add_rounded)) for x in parts]))
        for e in range(local):
            halves, arrived, wait = [], begun[e][0], []
            for h in range(2):
                y, product = mid(e, h, begun[e][1][h], products)
                products.append(product)
                halves.append([(y,)] + along_z.gather(y))
            if e < local - 1:
                *sums, _ = out(e, halves, sums, [])
                *grads, _ = grad(e, arrived, halves, grads, [])

    near, far, _, near_p, far_p = out(local - 1, halves, sums, wait)
    hop, home = send_home(near, far, add_rounded)
    _, per_expert = send_home(near_p, far_p, lambda a, b: add(a, b, [hop]))
    *grads, _ = grad(local - 1, arrived, halves, grads, [hop])
    combine_grad = jnp.sum(jnp.where(named, per_expert[None], 0.0), axis=1) / combine_t
    return (home[0].astype(BF16), home[1].astype(BF16), *grads, combine_grad.T)


def solution(mesh):
    return jax.shard_map(
        body,
        mesh=mesh,
        in_specs=(
            P(("group", "expert"), "dp"),
            P(("group", "expert"), None),
            P(("group", "expert"), None),
            P("expert", "dp", None),
            P("expert", "dp", None),
            P("expert", None, "dp"),
            P(("group", "expert"), "dp"),
        ),
        out_specs=(
            P(("group", "expert"), "dp"),
            P(("group", "expert"), "dp"),
            P(("group", "expert"), "dp", None),
            P(("group", "expert"), "dp", None),
            P(("group", "expert"), None, "dp"),
            P(("group", "expert"), None),
        ),
        check_vma=False,
    )
```

```python
import functools

import jax
import jax.numpy as jnp
from jax import lax
from jax.experimental import pallas as pl
from jax.experimental.pallas import tpu as pltpu
from jax.sharding import PartitionSpec as P

F32, BF16 = jnp.float32, jnp.bfloat16
VMEM_BYTES = 20 << 20


def line_pairs(n, gather, step):
    if gather:
        senders = [i for i in range(step - 1, n - 1)]
    else:
        senders = [i for i in range(0, min(step, n - 1))]
    right = [(i, i + 1) for i in senders]
    left = [(n - 1 - i, n - 2 - i) for i in senders]
    return right, left


class Line:
    def __init__(self, axis, n, stride):
        self.axis, self.n, self.stride = axis, n, stride

    def send(self, value, pairs):
        wide = [
            (a * self.stride + c, b * self.stride + c) for a, b in pairs for c in range(self.stride)
        ]
        return lax.ppermute(value, self.axis, wide)

    def gather(self, own):
        n = self.n
        if n == 2:
            both = self.send(own, [(0, 1), (1, 0)])
            return [(both, both)]
        right, left, rights, lefts = own, own, [], []
        for step in range(1, n):
            pairs_r, pairs_l = line_pairs(n, True, step)
            right, left = self.send(right, pairs_r), self.send(left, pairs_l)
            rights.append(right)
            lefts.append(left)
        return [(rights[q - 1], lefts[n - q - 1]) for q in range(1, n)]

    def scatter(self, parts, add):
        n = self.n
        if n == 2:
            return self.send(parts[1], [(0, 1), (1, 0)]), None
        right, left = parts[1], parts[n - 1]
        for step in range(1, n):
            pairs_r, pairs_l = line_pairs(n, False, step)
            right, left = self.send(right, pairs_r), self.send(left, pairs_l)
            if step < n - 1:
                right, left = add(parts[step + 1], right), add(parts[n - 1 - step], left)
        return right, left


def add_rounded(a, b):
    return (a.astype(F32) + b.astype(F32)).astype(BF16)


def dot(a, b, dims=((1,), (0,))):
    return lax.dot_general(a, b, (dims, ((), ())), preferred_element_type=F32)


def routing(scal, routes, expert, rows):
    n = len(routes)
    choose, tokens = routes[0].shape[0] // 2, routes[0].shape[1]
    which = (scal[2 * n] + expert).astype(F32)
    routes = [route[...] for route in routes]
    hits = [route[0:choose] == which for route in routes]
    weights = [
        jnp.sum(jnp.where(hit, route[choose:], 0.0), axis=0, keepdims=True)
        for hit, route in zip(hits, routes)
    ]
    chosen = jnp.concatenate(
        [jnp.sum(jnp.where(hit, 1.0, 0.0), axis=0, keepdims=True) for hit in hits], axis=0
    )
    earlier = lax.broadcasted_iota(jnp.int32, (tokens, tokens), 0) < lax.broadcasted_iota(
        jnp.int32, (tokens, tokens), 1
    )
    slots = dot(chosen.astype(BF16), earlier.astype(F32).astype(BF16))
    slots = jnp.where(chosen > 0.0, slots, -1.0).astype(jnp.int32)
    row = lax.broadcasted_iota(jnp.int32, (rows, tokens), 0)
    return [(scal[k], weights[k], row == slots[k : k + 1]) for k in range(n)]


def span_of(position, rows):
    return pl.ds(pl.multiple_of(position * rows, rows), rows)


def weight_copies(expert, half, weights, held, sems):
    copies = []
    for k, (source, target) in enumerate(zip(weights, held)):
        size = target.shape[0 if k == 2 else 1]
        span = pl.ds(half * size, size)
        src = source.at[expert, span, :] if k == 2 else source.at[expert, :, span]
        copies.append(pltpu.make_async_copy(src, target, sems.at[k]))
    for copy in copies:
        copy.start()
    return copies


def route_blocks(choose, count, width):
    wide = max(1, width // count)
    return [(16 * (b // wide), count * (b % wide)) for b in range(4 * choose // 16)]


def pack_kernel(ids, combine, tokens, grads, pack):
    count, width = tokens.shape
    choose = ids.shape[0]
    pack[0:count, :] = tokens[...]
    pack[count : 2 * count, :] = grads[...]
    lines = [ids[...].astype(F32)] + [part.astype(F32) for part in thirds(combine[...])]
    lines = jnp.concatenate(lines, axis=0).astype(BF16)
    blocks = route_blocks(choose, count, width)
    pack[2 * count :, :] = jnp.zeros((pack.shape[0] - 2 * count, width), BF16)
    for b, (row, lane) in enumerate(blocks):
        pack[2 * count + row : 2 * count + row + 16, lane : lane + count] = lines[16 * b : 16 * b + 16]


def unpack_route(pack, choose, count):
    lines = [
        pack[2 * count + row : 2 * count + row + 16, lane : lane + count]
        for row, lane in route_blocks(choose, count, pack.shape[1])
    ]
    lines = jnp.concatenate(lines, axis=0).astype(F32)
    ids, high, middle, low = (lines[k * choose : (k + 1) * choose] for k in range(4))
    return jnp.concatenate([ids, (high + middle) + low], axis=0)


def store_parts(outs, arrays):
    n = len(outs)
    for p in range(n):
        rows = arrays[0].shape[0] // n
        for k, value in enumerate(arrays):
            outs[p][pl.ds(k * rows, rows), :] = value[p * rows : (p + 1) * rows]


def fill_kernel(n, expert, choose, deps, scal, *refs):
    refs = refs[deps:]
    packs, weights, (in_ref, cot_ref, *refs) = refs[:n], refs[n : n + 3], refs[n + 3 :]
    outs, (token, routes, gw, uw, dw, sems) = refs[:n], refs[n:]
    copies = weight_copies(expert, 0, weights, (gw, uw, dw), sems)
    token[...] = jnp.zeros_like(token)
    rows, count = in_ref.shape[0] // n, routes.shape[2]
    found = [unpack_route(pack, choose, count) for pack in packs]
    for k in range(n):
        routes[k] = found[k]
    for k, (position, weight, hit) in enumerate(routing(scal, found, expert, rows)):
        pick = hit.astype(F32).astype(BF16)
        span = span_of(position, rows)
        in_ref[span, :] = dot(pick, packs[k][0:count, :]).astype(BF16)
        scale = jnp.sum(jnp.where(hit, weight, 0.0), axis=1, keepdims=True)
        cot_ref[span, :] = (dot(pick, packs[k][count : 2 * count, :]) * scale).astype(BF16)
    for copy in copies:
        copy.wait()
    gate, up = dot(in_ref[...], gw[...]), dot(in_ref[...], uw[...])
    back = dot(cot_ref[...], dw[...], ((1,), (1,)))
    store_parts(outs, [x.astype(BF16) for x in (gate, up, back)])


def more_kernel(n, expert, deps, *refs):
    in_ref, cot_ref, *refs = refs[deps:]
    weights, outs, (token, gw, uw, dw, sems) = refs[:3], refs[3 : 3 + n], refs[3 + n :]
    copies = weight_copies(expert, 1, weights, (gw, uw, dw), sems)
    token[...] = jnp.zeros_like(token)
    for copy in copies:
        copy.wait()
    gate, up = dot(in_ref[...], gw[...]), dot(in_ref[...], uw[...])
    back = dot(cot_ref[...], dw[...], ((1,), (1,)))
    store_parts(outs, [x.astype(BF16) for x in (gate, up, back)])


def thirds(value):
    high = value.astype(BF16)
    rest = value - high.astype(F32)
    middle = rest.astype(BF16)
    return high, middle, (rest - middle.astype(F32)).astype(BF16)


def mid_kernel(deps, others, *refs):
    own, right, left, *rest = refs[deps:]
    earlier, (out, product) = rest[:others], rest[others:]
    rows, tile = own.shape[0] // 3, own.shape[1]
    total = own[...].astype(F32) + right[...].astype(F32) + left[...].astype(F32)
    gate, up, back = (total[k * rows : (k + 1) * rows] for k in range(3))
    sig = jax.nn.sigmoid(gate)
    hidden = (gate * sig * up).astype(BF16)
    delta = back.astype(BF16).astype(F32)
    out[0:rows, :] = hidden
    out[rows : 2 * rows, :] = (delta * up * sig * (1.0 + gate * (1.0 - sig))).astype(BF16)
    out[2 * rows : 3 * rows, :] = (delta * (gate * sig)).astype(BF16)
    prod = hidden.astype(F32) * back
    lanes = product.shape[1]
    acc = prod[:, 0:lanes]
    for k in range(1, tile // lanes):
        acc = acc + prod[:, k * lanes : (k + 1) * lanes]
    product[...] = acc
    if others:
        partial = [ref[...] for ref in earlier] + [acc]
        ones, fill = jnp.ones((8, lanes), BF16), jnp.zeros((lanes - rows, lanes), F32)
        lines = []
        for e in range(len(partial) // 2):
            wide = jnp.concatenate([partial[2 * e] + partial[2 * e + 1], fill], axis=0)
            total = sum(dot(ones, part, ((1,), (1,))) for part in thirds(wide))[0:1]
            lines += [part.astype(F32) for part in thirds(total)]
        extra = out.shape[0] - 3 * rows
        lines.append(jnp.zeros((extra - len(lines), lanes), F32))
        out[3 * rows :, :] = jnp.zeros((extra, tile), BF16)
        out[3 * rows :, 0:lanes] = jnp.concatenate(lines, axis=0).astype(BF16)


def add_kernel(deps, *refs):
    a, b, out = refs[deps:]
    out[...] = (a[...].astype(F32) + b[...].astype(F32)).astype(out.dtype)


def part_of(scal, n, q, group, start, size):
    span = pl.ds(start, size)
    if len(group) == 1:
        return group[0][span, :]
    return jnp.where(scal[n + q] > 0, group[0][span, :], group[1][span, :])


def load_rows(scal, n, which, pieces):
    rows = pieces[0][0].shape[0] // 48 * 16
    return jnp.concatenate(
        [part_of(scal, n, q, group, which * rows, rows) for q, group in enumerate(pieces)], axis=0
    )


def split_pieces(refs, sizes):
    pieces, at = [refs[0:1]], 1
    for size in sizes:
        pieces.append(refs[at : at + size])
        at += size
    return pieces, refs[at:]


def terms(scal, n, pieces, copies, gw, uw, dw):
    hidden, gate, up = (load_rows(scal, n, k, pieces) for k in range(3))
    for copy in copies:
        copy.wait()
    back = dot(gate, gw[...], ((1,), (1,))) + dot(up, uw[...], ((1,), (1,)))
    return dot(hidden, dw[...]), back


def half_kernel(n, expert, sizes, deps, scal, *refs):
    pieces, refs = split_pieces(refs[deps:], sizes)
    weights, (eo, idl, token, gw, uw, dw, sems) = refs[:3], refs[3:]
    copies = weight_copies(expert, 0, weights, (gw, uw, dw), sems)
    token[...] = jnp.zeros_like(token)
    eo[...], idl[...] = terms(scal, n, pieces, copies, gw, uw, dw)


def out_kernel(n, expert, has_prev, last, sizes, deps, scal, *refs):
    refs = refs[deps:]
    routes, eo, idl, refs = refs[0], refs[1], refs[2], refs[3:]
    routes = [routes.at[k] for k in range(n)]
    if has_prev:
        prev, refs = refs[:2], refs[2:]
    pieces, refs = split_pieces(refs, sizes)
    weights, (near, far, token, *refs) = refs[:3], refs[3:]
    if last:
        near_p, far_p, *refs, held = refs
    gw, uw, dw, sems, eo_ref, idl_ref = refs
    copies = weight_copies(expert, 1, weights, (gw, uw, dw), sems)
    token[...] = jnp.zeros_like(token)
    rows = eo.shape[0] // n
    spots = routing(scal, routes, expert, rows)
    if last:
        send_products(scal, routes, expert + 1, pieces, held, near_p, far_p)
    layer, back = terms(scal, n, pieces, copies, gw, uw, dw)
    eo_ref[...], idl_ref[...] = (eo[...] + layer).astype(BF16), (idl[...] + back).astype(BF16)
    for k, (position, weight, hit) in enumerate(spots):
        pick = hit.astype(F32)
        scaled = (pick * weight).astype(BF16)
        span = span_of(position, rows)
        layer = dot(scaled, eo_ref[span, :], ((0,), (0,)))
        back = dot(pick.astype(BF16), idl_ref[span, :], ((0,), (0,)))
        which, place = (near, k) if k < n // 2 else (far, k - n // 2)
        if has_prev:
            before = prev[0 if k < n // 2 else 1]
            layer, back = layer + before[place, 0], back + before[place, 1]
        which[place, 0] = layer.astype(which.dtype)
        which[place, 1] = back.astype(which.dtype)


def grad_kernel(n, has_prev, sizes, deps, scal, in_ref, cot_ref, *refs):
    pieces, refs = split_pieces(refs[deps:], sizes)
    if has_prev:
        refs = refs[3:]
    gg, ug, dg, token = refs
    token[...] = jnp.zeros_like(token)
    gg[0] = dot(in_ref[...], load_rows(scal, n, 1, pieces), ((0,), (0,))).astype(BF16)
    ug[0] = dot(in_ref[...], load_rows(scal, n, 2, pieces), ((0,), (0,))).astype(BF16)
    dg[0] = dot(load_rows(scal, n, 0, pieces), cot_ref[...], ((0,), (0,))).astype(BF16)


def send_products(scal, routes, local, pieces, held, near, far):
    n, (_, extra, lanes) = len(routes), held.shape
    first = pieces[0][0].shape[0] - extra
    for q, group in enumerate(pieces):
        held[q] = part_of(scal, n, q, group, first, extra)[:, 0:lanes]
    experts_all, tokens = near.shape[1:]
    ids = lax.broadcasted_iota(jnp.int32, (experts_all, tokens), 0)
    sums = [jnp.zeros((experts_all, tokens), F32) for _ in range(n)]
    for e in range(local):
        for k, (position, _, hit) in enumerate(routing(scal, routes, e, lanes)):
            found = dot(held[position], hit.astype(F32).astype(BF16))
            value = found[3 * e : 3 * e + 1] + found[3 * e + 1 : 3 * e + 2] + found[3 * e + 2 : 3 * e + 3]
            sums[k] = sums[k] + jnp.where(ids == scal[2 * n] + e, value, 0.0)
    for k in range(n):
        if k < n // 2:
            near[k] = sums[k]
        else:
            far[k - n // 2] = sums[k]


def in_hbm(array):
    return pltpu.with_memory_space_constraint(array, pltpu.HBM)


def whole_spec(shape):
    return pl.BlockSpec(tuple(shape), lambda g: (0,) * len(shape))


def spec_of(array):
    return whole_spec(array.shape)


def like(shape, dtype=BF16):
    return jax.ShapeDtypeStruct(tuple(shape), dtype)


SMEM_SPEC = pl.BlockSpec(memory_space=pltpu.SMEM)
ANY_SPEC = pl.BlockSpec(memory_space=pl.ANY)
HBM_SPEC = pl.BlockSpec(memory_space=pltpu.HBM)
TOKEN = (8, 128)


def call(kernel, grid, in_specs, out_specs, out_shape, flops, moved, **rest):
    return pl.pallas_call(
        kernel,
        grid=(grid,),
        in_specs=in_specs,
        out_specs=out_specs,
        out_shape=out_shape,
        compiler_params=pltpu.CompilerParams(vmem_limit_bytes=VMEM_BYTES),
        cost_estimate=pl.CostEstimate(flops=flops, bytes_accessed=moved, transcendentals=0),
        **rest,
    )


def body(tokens, expert_ids, combine, gate_weight, up_weight, down_weight, out_grad):
    peers, n = lax.axis_size("expert"), lax.axis_size("dp")
    assert peers == n
    chips = peers // 2
    local, width, hidden = gate_weight.shape
    count, choose = expert_ids.shape
    experts_all = peers * local
    capacity = count * choose * 5 // (4 * experts_all)
    rows = -(-capacity // 16) * 16
    all_rows = n * rows
    tile = hidden // 2
    swaps = n == 4

    me, here = lax.axis_index("expert"), lax.axis_index("dp")
    at_end = (here == 0) | (here == n - 1)
    table = []
    for place in range(n):
        block = 2 * lax.rem(me // 2 - place % chips + chips, chips) + lax.rem(
            lax.rem(me, 2) + place // chips, 2
        )
        if swaps:
            across_middle = jnp.where((block == 0) | (block == 3), 3, 2)
            position = jnp.where(
                block == here, 0, jnp.where(block // 2 == here // 2, 1, across_middle)
            )
        else:
            position = lax.rem(here - block + n, n)
        table.append(position)
    flags = [at_end if swaps else here >= q for q in range(n)]
    scal = jnp.stack(
        [jnp.asarray(v).astype(jnp.int32) for v in table + flags + [me * local, at_end]]
    )

    ids_t, combine_t = expert_ids.T, combine.T
    named = ids_t[:, None, :] == jnp.arange(experts_all, dtype=jnp.int32)[None, :, None]

    along_x, across = Line("expert", chips, 2), Line("expert", peers, 1)
    swap = [(2 * x + c, 2 * x + 1 - c) for x in range(chips) for c in range(2)]

    def gather_blocks(own):
        found = [own] + [
            right if right is left else jnp.where(me // 2 >= q, right, left)
            for q, (right, left) in enumerate(along_x.gather(own), 1)
        ]
        return found + [across.send(piece, swap) for piece in found]

    route_rows = 16 + max(row for row, _ in route_blocks(choose, count, width))
    pack_shape = (2 * count + route_rows, width)
    pack = call(
        pack_kernel,
        1,
        [spec_of(ids_t), spec_of(combine_t), spec_of(tokens), spec_of(out_grad)],
        whole_spec(pack_shape),
        like(pack_shape),
        count * width,
        8 * count * width,
    )(*(in_hbm(x) for x in (ids_t, combine_t, tokens, out_grad)))
    packs = gather_blocks(pack)
    route_shape = (n, 2 * choose, count)

    mac = all_rows * width * hidden
    weight_bytes = 2 * width * hidden
    piece_shape = (3 * rows, tile)
    extra = -(-3 * local // 16) * 16
    wide_shape = (3 * rows + extra, tile)
    piece_bytes = 2 * 3 * rows * tile
    slot_shape = (all_rows, width)

    weights = [in_hbm(w) for w in (gate_weight, up_weight, down_weight)]
    held_weights = [pltpu.VMEM(shape, BF16) for shape in ((width, tile), (width, tile), (tile, width))]
    held_weights += [pltpu.SemaphoreType.DMA((3,))]

    def fill(e, deps):
        inputs, cot, *parts, token, routes = call(
            functools.partial(fill_kernel, n, e, choose, len(deps)),
            1,
            [SMEM_SPEC] + [ANY_SPEC] * len(deps) + [spec_of(x) for x in packs] + [HBM_SPEC] * 3,
            [whole_spec(slot_shape)] * 2
            + [whole_spec(piece_shape)] * n
            + [whole_spec(TOKEN), whole_spec(route_shape)],
            [like(slot_shape)] * 2
            + [like(piece_shape)] * n
            + [like(TOKEN, F32), like(route_shape, F32)],
            3 * mac,
            2 * weight_bytes + n * piece_bytes,
            scratch_shapes=held_weights,
        )(scal, *deps, *packs, *weights)
        return (inputs, cot), parts, token, routes

    def more(e, slots, deps):
        *parts, token = call(
            functools.partial(more_kernel, n, e, len(deps)),
            1,
            [ANY_SPEC] * len(deps) + [whole_spec(slot_shape)] * 2 + [HBM_SPEC] * 3,
            [whole_spec(piece_shape)] * n + [whole_spec(TOKEN)],
            [like(piece_shape)] * n + [like(TOKEN, F32)],
            3 * mac,
            2 * weight_bytes + n * piece_bytes,
            scratch_shapes=held_weights,
        )(*deps, *slots, *weights)
        return parts, token

    def mid(e, h, totals, products, deps=()):
        others = products if e == local - 1 and h == 1 else []
        shape = wide_shape if others else piece_shape
        return call(
            functools.partial(mid_kernel, len(deps), len(others)),
            1,
            [ANY_SPEC] * len(deps)
            + [whole_spec(piece_shape)] * 3
            + [whole_spec((rows, 128))] * len(others),
            [whole_spec(shape), whole_spec((rows, 128))],
            [like(shape), like((rows, 128), F32)],
            20 * rows * tile,
            4 * piece_bytes,
        )(*deps, *totals, *others)

    def add(a, b, deps):
        return call(
            functools.partial(add_kernel, len(deps)),
            1,
            [ANY_SPEC] * len(deps) + [spec_of(a)] * 2,
            spec_of(a),
            like(a.shape, a.dtype),
            a.size,
            3 * a.size * a.dtype.itemsize,
        )(*deps, a, b)

    def half(e, pieces, deps):
        flat = [x for group in pieces for x in group]
        return call(
            functools.partial(half_kernel, n, e, [len(g) for g in pieces[1:]], len(deps)),
            1,
            [SMEM_SPEC] + [ANY_SPEC] * len(deps) + [spec_of(x) for x in flat] + [HBM_SPEC] * 3,
            [whole_spec(slot_shape)] * 2 + [whole_spec(TOKEN)],
            [like(slot_shape, F32)] * 2 + [like(TOKEN, F32)],
            3 * mac,
            2 * weight_bytes + len(flat) * piece_bytes,
            scratch_shapes=held_weights,
        )(scal, *deps, *flat, *weights)

    def out(e, begun, pieces, prev, deps):
        flat = [x for group in pieces for x in group]
        last = e == local - 1
        dense_shape, sum_shape = (chips, experts_all, count), (chips, 2, count, width)
        return call(
            functools.partial(
                out_kernel, n, e, e > 0, last, [len(g) for g in pieces[1:]], len(deps)
            ),
            1,
            [SMEM_SPEC]
            + [ANY_SPEC] * len(deps)
            + [whole_spec(route_shape)]
            + [whole_spec(slot_shape)] * 2
            + ([whole_spec(sum_shape)] * 2 if e > 0 else [])
            + [spec_of(x) for x in flat]
            + [HBM_SPEC] * 3,
            [whole_spec(sum_shape)] * 2
            + [whole_spec(TOKEN)]
            + ([whole_spec(dense_shape)] * 2 if last else []),
            [like(sum_shape, BF16 if last else F32)] * 2
            + [like(TOKEN, F32)]
            + ([like(dense_shape, F32)] * 2 if last else []),
            3 * mac,
            2 * weight_bytes + len(flat) * piece_bytes,
            scratch_shapes=held_weights
            + [pltpu.VMEM(slot_shape, BF16)] * 2
            + ([pltpu.VMEM((n, extra, 128), BF16)] if last else []),
        )(scal, *deps, routes, *begun, *prev, *flat, *weights)

    def grad(e, h, slots, pieces, prev, deps):
        flat = [x for group in pieces for x in group]
        base = 3 + len(deps) + len(flat)
        wide = pl.BlockSpec((1, width, tile), lambda g: (e, 0, h))
        return call(
            functools.partial(
                grad_kernel, n, len(prev) > 0, [len(g) for g in pieces[1:]], len(deps)
            ),
            1,
            [SMEM_SPEC]
            + [whole_spec(slot_shape)] * 2
            + [ANY_SPEC] * len(deps)
            + [spec_of(x) for x in flat]
            + [ANY_SPEC] * len(prev),
            [wide, wide, pl.BlockSpec((1, tile, width), lambda g: (e, h, 0)), whole_spec(TOKEN)],
            [like(w.shape) for w in weights] + [like(TOKEN, F32)],
            3 * mac,
            2 * weight_bytes + len(flat) * piece_bytes,
            input_output_aliases={base + k: k for k in range(len(prev))},
        )(scal, *slots, *deps, *flat, *prev)

    along_z = Line("dp", n, 1)

    def outer(value):
        return along_z.send(value, [(0, 1), (1, 0), (2, 3), (3, 2)])

    def inner(value):
        pairs = []
        for p in range(peers):
            pairs += [(p * n + 1, p * n + 2), (p * n + 2, p * n + 1)]
            pairs += [(p * n + end, (p ^ 1) * n + end) for end in (0, n - 1)]
        return lax.ppermute(value, ("expert", "dp"), pairs)

    def unless_end(value):
        return jnp.where(at_end, jnp.zeros_like(value), value)

    products, sums, grads = [], [], []

    def send_home(near, far, add):
        near = add(near, across.send(far, swap))
        right, left = along_x.scatter([near[q] for q in range(chips)], add)
        home = near[0].astype(F32) + right.astype(F32)
        return near, home if left is None else home + left.astype(F32)

    if swaps:
        flight, arrived = [None, None], None
        slots, x0, _, routes = fill(0, [])
        parts, grad_token = [x0, more(0, slots, [])[0]], None
        for e in range(local):
            first, second, totals, halves = [], [], [], []
            following, seen = e < local - 1, [[], []]
            for h in range(2):
                x = parts[h]
                if e == 0:
                    first.append((outer(x[3]), None))
                else:
                    y, got_a, got_b = flight[h]
                    first.append((outer(jnp.where(at_end, x[3], got_b)), inner(got_a)))
            if following:
                next_slots, next0, token_0, _ = fill(e + 1, [] if e == 0 else [flight[0][2]])
                next1, token_1 = more(e + 1, next_slots, [first[0][0] if e == 0 else flight[1][2]])
                seen = [[token_0], [token_1]]
            if grad_token is not None:
                seen[0].append(grad_token)
            for h in range(2):
                x, (a1, b1) = parts[h], first[h]
                send_a2 = x[2] if e == 0 else jnp.where(at_end, x[2], b1)
                second.append((outer(send_a2), inner(add(x[3], a1, seen[h]))))
                if e > 0:
                    y, got_a, got_b = flight[h]
                    halves.append([(y,), (got_a,), (a1, got_b), (second[h][0], b1)])
            waits = [[], []]
            if e > 0:
                *begun, half_token = half(e - 1, halves[0], [])
                *sums, out_token = out(e - 1, begun, halves[1], sums, [])
                waits[0] = [out_token]
            for h in range(2):
                x, (a2, b2) = parts[h], second[h]
                both = add(x[1], b2, [half_token]) if e > 0 and h == 1 else add_rounded(x[1], b2)
                a3 = outer(jnp.where(at_end, x[1], both))
                b3 = inner(unless_end(add_rounded(x[2], a2)))
                totals.append((x[0], a3, b3))
            for h in range(2):
                y, product = mid(e, h, totals[h], products, waits[h])
                products.append(product)
                flight[h] = (y, outer(y), inner(y))
                if e > 0:
                    *grads, grad_token = grad(e - 1, h, arrived, halves[h], grads, [y])
                    if h == 0:
                        waits[1] = [grad_token]
            arrived = slots
            if following:
                slots, parts = next_slots, [next0, next1]
        halves = []
        for h in range(2):
            y, got_a, got_b = flight[h]
            a1, b1 = outer(got_b), inner(got_a)
            a2 = outer(b1)
            halves.append([(y,), (got_a,), (a1, got_b), (a2, b1)])
        wait = [grad_token]
    else:
        started = []
        for e in range(local):
            slots, x0, _, routes = fill(e, [])
            parts = [x0, more(e, slots, [])[0]]
            started.append((slots, [(x[0], *along_z.scatter(x, add_rounded)) for x in parts]))
        for e in range(local):
            halves, arrived, wait = [], started[e][0], []
            for h in range(2):
                y, product = mid(e, h, started[e][1][h], products)
                products.append(product)
                halves.append([(y,)] + along_z.gather(y))
            if e < local - 1:
                *begun, _ = half(e, halves[0], [])
                *sums, _ = out(e, begun, halves[1], sums, [])
                for h in range(2):
                    *grads, _ = grad(e, h, arrived, halves[h], grads, [])

    *begun, _ = half(local - 1, halves[0], wait)
    near, far, _, near_p, far_p = out(local - 1, begun, halves[1], sums, [])
    hop, home = send_home(near, far, add_rounded)
    _, per_expert = send_home(near_p, far_p, lambda a, b: add(a, b, [hop]))
    for h in range(2):
        *grads, _ = grad(local - 1, h, arrived, halves[h], grads, [hop])
    combine_grad = jnp.sum(jnp.where(named, per_expert[None], 0.0), axis=1) / combine_t
    return (home[0].astype(BF16), home[1].astype(BF16), *grads, combine_grad.T)


def solution(mesh):
    return jax.shard_map(
        body,
        mesh=mesh,
        in_specs=(
            P(("group", "expert"), "dp"),
            P(("group", "expert"), None),
            P(("group", "expert"), None),
            P("expert", "dp", None),
            P("expert", "dp", None),
            P("expert", None, "dp"),
            P(("group", "expert"), "dp"),
        ),
        out_specs=(
            P(("group", "expert"), "dp"),
            P(("group", "expert"), "dp"),
            P(("group", "expert"), "dp", None),
            P(("group", "expert"), "dp", None),
            P(("group", "expert"), None, "dp"),
            P(("group", "expert"), None),
        ),
        check_vma=False,
    )
```

```python
import functools

import jax
import jax.numpy as jnp
from jax import lax
from jax.experimental import pallas as pl
from jax.experimental.pallas import tpu as pltpu
from jax.sharding import PartitionSpec as P

F32, BF16 = jnp.float32, jnp.bfloat16
VMEM_BYTES = 20 << 20


def line_pairs(n, gather, step):
    if gather:
        senders = [i for i in range(step - 1, n - 1)]
    else:
        senders = [i for i in range(0, min(step, n - 1))]
    right = [(i, i + 1) for i in senders]
    left = [(n - 1 - i, n - 2 - i) for i in senders]
    return right, left


class Line:
    def __init__(self, axis, n, stride):
        self.axis, self.n, self.stride = axis, n, stride

    def send(self, value, pairs):
        wide = [
            (a * self.stride + c, b * self.stride + c) for a, b in pairs for c in range(self.stride)
        ]
        return lax.ppermute(value, self.axis, wide)

    def gather(self, own):
        n = self.n
        if n == 2:
            both = self.send(own, [(0, 1), (1, 0)])
            return [(both, both)]
        right, left, rights, lefts = own, own, [], []
        for step in range(1, n):
            pairs_r, pairs_l = line_pairs(n, True, step)
            right, left = self.send(right, pairs_r), self.send(left, pairs_l)
            rights.append(right)
            lefts.append(left)
        return [(rights[q - 1], lefts[n - q - 1]) for q in range(1, n)]

    def scatter(self, parts, add):
        n = self.n
        if n == 2:
            return self.send(parts[1], [(0, 1), (1, 0)]), None
        right, left = parts[1], parts[n - 1]
        for step in range(1, n):
            pairs_r, pairs_l = line_pairs(n, False, step)
            right, left = self.send(right, pairs_r), self.send(left, pairs_l)
            if step < n - 1:
                right, left = add(parts[step + 1], right), add(parts[n - 1 - step], left)
        return right, left


def add_rounded(a, b):
    return (a.astype(F32) + b.astype(F32)).astype(BF16)


def dot(a, b, dims=((1,), (0,))):
    return lax.dot_general(a, b, (dims, ((), ())), preferred_element_type=F32)


def routing(scal, routes, expert, rows):
    n = len(routes)
    choose, tokens = routes[0].shape[0] // 2, routes[0].shape[1]
    which = (scal[2 * n] + expert).astype(F32)
    routes = [route[...] for route in routes]
    hits = [route[0:choose] == which for route in routes]
    weights = [
        jnp.sum(jnp.where(hit, route[choose:], 0.0), axis=0, keepdims=True)
        for hit, route in zip(hits, routes)
    ]
    chosen = jnp.concatenate(
        [jnp.sum(jnp.where(hit, 1.0, 0.0), axis=0, keepdims=True) for hit in hits], axis=0
    )
    earlier = lax.broadcasted_iota(jnp.int32, (tokens, tokens), 0) < lax.broadcasted_iota(
        jnp.int32, (tokens, tokens), 1
    )
    slots = dot(chosen.astype(BF16), earlier.astype(F32).astype(BF16))
    slots = jnp.where(chosen > 0.0, slots, -1.0).astype(jnp.int32)
    row = lax.broadcasted_iota(jnp.int32, (rows, tokens), 0)
    return [(scal[k], weights[k], row == slots[k : k + 1]) for k in range(n)]


def span_of(position, rows):
    return pl.ds(pl.multiple_of(position * rows, rows), rows)


def weight_copies(expert, half, weights, held, sems):
    copies = []
    for k, (source, target) in enumerate(zip(weights, held)):
        size = target.shape[0 if k == 2 else 1]
        span = pl.ds(half * size, size)
        src = source.at[expert, span, :] if k == 2 else source.at[expert, :, span]
        copies.append(pltpu.make_async_copy(src, target, sems.at[k]))
    for copy in copies:
        copy.start()
    return copies


def route_blocks(choose, count, width):
    wide = max(1, width // count)
    return [(16 * (b // wide), count * (b % wide)) for b in range(4 * choose // 16)]


def pack_kernel(ids, combine, tokens, grads, pack):
    count, width = tokens.shape
    choose = ids.shape[0]
    pack[0:count, :] = tokens[...]
    pack[count : 2 * count, :] = grads[...]
    lines = [ids[...].astype(F32)] + [part.astype(F32) for part in thirds(combine[...])]
    lines = jnp.concatenate(lines, axis=0).astype(BF16)
    blocks = route_blocks(choose, count, width)
    pack[2 * count :, :] = jnp.zeros((pack.shape[0] - 2 * count, width), BF16)
    for b, (row, lane) in enumerate(blocks):
        pack[2 * count + row : 2 * count + row + 16, lane : lane + count] = lines[16 * b : 16 * b + 16]


def unpack_route(pack, choose, count):
    lines = [
        pack[2 * count + row : 2 * count + row + 16, lane : lane + count]
        for row, lane in route_blocks(choose, count, pack.shape[1])
    ]
    lines = jnp.concatenate(lines, axis=0).astype(F32)
    ids, high, middle, low = (lines[k * choose : (k + 1) * choose] for k in range(4))
    return jnp.concatenate([ids, (high + middle) + low], axis=0)


def store_parts(outs, arrays):
    n = len(outs)
    for p in range(n):
        rows = arrays[0].shape[0] // n
        for k, value in enumerate(arrays):
            outs[p][pl.ds(k * rows, rows), :] = value[p * rows : (p + 1) * rows]


def fill_kernel(n, expert, choose, deps, scal, *refs):
    refs = refs[deps:]
    packs, weights, (in_ref, cot_ref, *refs) = refs[:n], refs[n : n + 3], refs[n + 3 :]
    outs, (token, routes, gw, uw, dw, sems) = refs[:n], refs[n:]
    copies = weight_copies(expert, 0, weights, (gw, uw, dw), sems)
    token[...] = jnp.zeros_like(token)
    rows, count = in_ref.shape[0] // n, routes.shape[2]
    found = [unpack_route(pack, choose, count) for pack in packs]
    for k in range(n):
        routes[k] = found[k]
    for k, (position, weight, hit) in enumerate(routing(scal, found, expert, rows)):
        pick = hit.astype(F32).astype(BF16)
        span = span_of(position, rows)
        in_ref[span, :] = dot(pick, packs[k][0:count, :]).astype(BF16)
        scale = jnp.sum(jnp.where(hit, weight, 0.0), axis=1, keepdims=True)
        cot_ref[span, :] = (dot(pick, packs[k][count : 2 * count, :]) * scale).astype(BF16)
    for copy in copies:
        copy.wait()
    gate, up = dot(in_ref[...], gw[...]), dot(in_ref[...], uw[...])
    back = dot(cot_ref[...], dw[...], ((1,), (1,)))
    store_parts(outs, [x.astype(BF16) for x in (gate, up, back)])


def more_kernel(n, expert, deps, *refs):
    in_ref, cot_ref, *refs = refs[deps:]
    weights, outs, (token, gw, uw, dw, sems) = refs[:3], refs[3 : 3 + n], refs[3 + n :]
    copies = weight_copies(expert, 1, weights, (gw, uw, dw), sems)
    token[...] = jnp.zeros_like(token)
    for copy in copies:
        copy.wait()
    gate, up = dot(in_ref[...], gw[...]), dot(in_ref[...], uw[...])
    back = dot(cot_ref[...], dw[...], ((1,), (1,)))
    store_parts(outs, [x.astype(BF16) for x in (gate, up, back)])


def thirds(value):
    high = value.astype(BF16)
    rest = value - high.astype(F32)
    middle = rest.astype(BF16)
    return high, middle, (rest - middle.astype(F32)).astype(BF16)


def mid_kernel(deps, others, *refs):
    own, right, left, *rest = refs[deps:]
    earlier, (out, product) = rest[:others], rest[others:]
    rows, tile = own.shape[0] // 3, own.shape[1]
    total = own[...].astype(F32) + right[...].astype(F32) + left[...].astype(F32)
    gate, up, back = (total[k * rows : (k + 1) * rows] for k in range(3))
    sig = jax.nn.sigmoid(gate)
    hidden = (gate * sig * up).astype(BF16)
    delta = back.astype(BF16).astype(F32)
    out[0:rows, :] = hidden
    out[rows : 2 * rows, :] = (delta * up * sig * (1.0 + gate * (1.0 - sig))).astype(BF16)
    out[2 * rows : 3 * rows, :] = (delta * (gate * sig)).astype(BF16)
    prod = hidden.astype(F32) * back
    lanes = product.shape[1]
    acc = prod[:, 0:lanes]
    for k in range(1, tile // lanes):
        acc = acc + prod[:, k * lanes : (k + 1) * lanes]
    product[...] = acc
    if others:
        partial = [ref[...] for ref in earlier] + [acc]
        ones, fill = jnp.ones((8, lanes), BF16), jnp.zeros((lanes - rows, lanes), F32)
        lines = []
        for e in range(len(partial) // 2):
            wide = jnp.concatenate([partial[2 * e] + partial[2 * e + 1], fill], axis=0)
            total = sum(dot(ones, part, ((1,), (1,))) for part in thirds(wide))[0:1]
            lines += [part.astype(F32) for part in thirds(total)]
        extra = out.shape[0] - 3 * rows
        lines.append(jnp.zeros((extra - len(lines), lanes), F32))
        out[3 * rows :, :] = jnp.zeros((extra, tile), BF16)
        out[3 * rows :, 0:lanes] = jnp.concatenate(lines, axis=0).astype(BF16)


def add_kernel(deps, *refs):
    a, b, out = refs[deps:]
    out[...] = (a[...].astype(F32) + b[...].astype(F32)).astype(out.dtype)


def relay_kernel(deps, *refs):
    value, out = refs[deps:]
    out[...] = value[...]


def part_of(scal, n, q, group, start, size):
    span = pl.ds(start, size)
    if len(group) == 1:
        return group[0][span, :]
    return jnp.where(scal[n + q] > 0, group[0][span, :], group[1][span, :])


def load_rows(scal, n, which, pieces):
    rows = pieces[0][0].shape[0] // 48 * 16
    return jnp.concatenate(
        [part_of(scal, n, q, group, which * rows, rows) for q, group in enumerate(pieces)], axis=0
    )


def split_pieces(refs, sizes):
    pieces, at = [refs[0:1]], 1
    for size in sizes:
        pieces.append(refs[at : at + size])
        at += size
    return pieces, refs[at:]


def terms(scal, n, pieces, copies, gw, uw, dw):
    hidden, gate, up = (load_rows(scal, n, k, pieces) for k in range(3))
    for copy in copies:
        copy.wait()
    back = dot(gate, gw[...], ((1,), (1,))) + dot(up, uw[...], ((1,), (1,)))
    return dot(hidden, dw[...]), back


def half_kernel(n, expert, sizes, deps, scal, *refs):
    pieces, refs = split_pieces(refs[deps:], sizes)
    weights, (eo, idl, token, gw, uw, dw, sems) = refs[:3], refs[3:]
    copies = weight_copies(expert, 0, weights, (gw, uw, dw), sems)
    token[...] = jnp.zeros_like(token)
    eo[...], idl[...] = terms(scal, n, pieces, copies, gw, uw, dw)


def out_kernel(n, expert, has_prev, sizes, deps, scal, *refs):
    refs = refs[deps:]
    routes, eo, idl, refs = refs[0], refs[1], refs[2], refs[3:]
    routes = [routes.at[k] for k in range(n)]
    if has_prev:
        prev, refs = refs[:2], refs[2:]
    pieces, refs = split_pieces(refs, sizes)
    weights, (near, far, token, *refs) = refs[:3], refs[3:]
    gw, uw, dw, sems, eo_ref, idl_ref = refs
    copies = weight_copies(expert, 1, weights, (gw, uw, dw), sems)
    token[...] = jnp.zeros_like(token)
    rows = eo.shape[0] // n
    spots = routing(scal, routes, expert, rows)
    layer, back = terms(scal, n, pieces, copies, gw, uw, dw)
    eo_ref[...], idl_ref[...] = (eo[...] + layer).astype(BF16), (idl[...] + back).astype(BF16)
    for k, (position, weight, hit) in enumerate(spots):
        pick = hit.astype(F32)
        scaled = (pick * weight).astype(BF16)
        span = span_of(position, rows)
        layer = dot(scaled, eo_ref[span, :], ((0,), (0,)))
        back = dot(pick.astype(BF16), idl_ref[span, :], ((0,), (0,)))
        which, place = (near, k) if k < n // 2 else (far, k - n // 2)
        if has_prev:
            before = prev[0 if k < n // 2 else 1]
            layer, back = layer + before[place, 0], back + before[place, 1]
        which[place, 0] = layer.astype(which.dtype)
        which[place, 1] = back.astype(which.dtype)


def grad_kernel(n, has_prev, sizes, deps, scal, in_ref, cot_ref, *refs):
    pieces, refs = split_pieces(refs[deps:], sizes)
    if has_prev:
        refs = refs[3:]
    gg, ug, dg, token = refs
    token[...] = jnp.zeros_like(token)
    gg[0] = dot(in_ref[...], load_rows(scal, n, 1, pieces), ((0,), (0,))).astype(BF16)
    ug[0] = dot(in_ref[...], load_rows(scal, n, 2, pieces), ((0,), (0,))).astype(BF16)
    dg[0] = dot(load_rows(scal, n, 0, pieces), cot_ref[...], ((0,), (0,))).astype(BF16)


def product_kernel(n, local, sizes, deps, scal, routes, *refs):
    pieces, (near, far, held) = split_pieces(refs[deps:], sizes)
    routes = [routes.at[k] for k in range(n)]
    _, extra, lanes = held.shape
    first = pieces[0][0].shape[0] - extra
    for q, group in enumerate(pieces):
        held[q] = part_of(scal, n, q, group, first, extra)[:, 0:lanes]
    experts_all, tokens = near.shape[1:]
    ids = lax.broadcasted_iota(jnp.int32, (experts_all, tokens), 0)
    sums = [jnp.zeros((experts_all, tokens), F32) for _ in range(n)]
    for e in range(local):
        for k, (position, _, hit) in enumerate(routing(scal, routes, e, lanes)):
            found = dot(held[position], hit.astype(F32).astype(BF16))
            value = found[3 * e : 3 * e + 1] + found[3 * e + 1 : 3 * e + 2] + found[3 * e + 2 : 3 * e + 3]
            sums[k] = sums[k] + jnp.where(ids == scal[2 * n] + e, value, 0.0)
    for k in range(n):
        if k < n // 2:
            near[k] = sums[k]
        else:
            far[k - n // 2] = sums[k]


def in_hbm(array):
    return pltpu.with_memory_space_constraint(array, pltpu.HBM)


def whole_spec(shape):
    return pl.BlockSpec(tuple(shape), lambda g: (0,) * len(shape))


def spec_of(array):
    return whole_spec(array.shape)


def like(shape, dtype=BF16):
    return jax.ShapeDtypeStruct(tuple(shape), dtype)


SMEM_SPEC = pl.BlockSpec(memory_space=pltpu.SMEM)
ANY_SPEC = pl.BlockSpec(memory_space=pl.ANY)
HBM_SPEC = pl.BlockSpec(memory_space=pltpu.HBM)
TOKEN = (8, 128)


def call(kernel, grid, in_specs, out_specs, out_shape, flops, moved, **rest):
    return pl.pallas_call(
        kernel,
        grid=(grid,),
        in_specs=in_specs,
        out_specs=out_specs,
        out_shape=out_shape,
        compiler_params=pltpu.CompilerParams(vmem_limit_bytes=VMEM_BYTES),
        cost_estimate=pl.CostEstimate(flops=flops, bytes_accessed=moved, transcendentals=0),
        **rest,
    )


def body(tokens, expert_ids, combine, gate_weight, up_weight, down_weight, out_grad):
    peers, n = lax.axis_size("expert"), lax.axis_size("dp")
    assert peers == n
    chips = peers // 2
    local, width, hidden = gate_weight.shape
    count, choose = expert_ids.shape
    experts_all = peers * local
    capacity = count * choose * 5 // (4 * experts_all)
    rows = -(-capacity // 16) * 16
    all_rows = n * rows
    tile = hidden // 2
    swaps = n == 4

    me, here = lax.axis_index("expert"), lax.axis_index("dp")
    at_end = (here == 0) | (here == n - 1)
    table = []
    for place in range(n):
        block = 2 * lax.rem(me // 2 - place % chips + chips, chips) + lax.rem(
            lax.rem(me, 2) + place // chips, 2
        )
        if swaps:
            across_middle = jnp.where((block == 0) | (block == 3), 3, 2)
            position = jnp.where(
                block == here, 0, jnp.where(block // 2 == here // 2, 1, across_middle)
            )
        else:
            position = lax.rem(here - block + n, n)
        table.append(position)
    flags = [at_end if swaps else here >= q for q in range(n)]
    scal = jnp.stack(
        [jnp.asarray(v).astype(jnp.int32) for v in table + flags + [me * local, at_end]]
    )

    ids_t, combine_t = expert_ids.T, combine.T
    named = ids_t[:, None, :] == jnp.arange(experts_all, dtype=jnp.int32)[None, :, None]

    along_x, across = Line("expert", chips, 2), Line("expert", peers, 1)
    swap = [(2 * x + c, 2 * x + 1 - c) for x in range(chips) for c in range(2)]

    def gather_blocks(own):
        found = [own] + [
            right if right is left else jnp.where(me // 2 >= q, right, left)
            for q, (right, left) in enumerate(along_x.gather(own), 1)
        ]
        return found + [across.send(piece, swap) for piece in found]

    route_rows = 16 + max(row for row, _ in route_blocks(choose, count, width))
    pack_shape = (2 * count + route_rows, width)
    pack = call(
        pack_kernel,
        1,
        [spec_of(ids_t), spec_of(combine_t), spec_of(tokens), spec_of(out_grad)],
        whole_spec(pack_shape),
        like(pack_shape),
        count * width,
        8 * count * width,
    )(*(in_hbm(x) for x in (ids_t, combine_t, tokens, out_grad)))
    packs = gather_blocks(pack)
    route_shape = (n, 2 * choose, count)

    mac = all_rows * width * hidden
    weight_bytes = 2 * width * hidden
    piece_shape = (3 * rows, tile)
    extra = -(-3 * local // 16) * 16
    wide_shape = (3 * rows + extra, tile)
    piece_bytes = 2 * 3 * rows * tile
    slot_shape = (all_rows, width)

    weights = [in_hbm(w) for w in (gate_weight, up_weight, down_weight)]
    held_weights = [pltpu.VMEM(shape, BF16) for shape in ((width, tile), (width, tile), (tile, width))]
    held_weights += [pltpu.SemaphoreType.DMA((3,))]

    def fill(e, deps):
        inputs, cot, *parts, token, routes = call(
            functools.partial(fill_kernel, n, e, choose, len(deps)),
            1,
            [SMEM_SPEC] + [ANY_SPEC] * len(deps) + [spec_of(x) for x in packs] + [HBM_SPEC] * 3,
            [whole_spec(slot_shape)] * 2
            + [whole_spec(piece_shape)] * n
            + [whole_spec(TOKEN), whole_spec(route_shape)],
            [like(slot_shape)] * 2
            + [like(piece_shape)] * n
            + [like(TOKEN, F32), like(route_shape, F32)],
            3 * mac,
            2 * weight_bytes + n * piece_bytes,
            scratch_shapes=held_weights,
        )(scal, *deps, *packs, *weights)
        return (inputs, cot), parts, token, routes

    def more(e, slots, deps):
        *parts, token = call(
            functools.partial(more_kernel, n, e, len(deps)),
            1,
            [ANY_SPEC] * len(deps) + [whole_spec(slot_shape)] * 2 + [HBM_SPEC] * 3,
            [whole_spec(piece_shape)] * n + [whole_spec(TOKEN)],
            [like(piece_shape)] * n + [like(TOKEN, F32)],
            3 * mac,
            2 * weight_bytes + n * piece_bytes,
            scratch_shapes=held_weights,
        )(*deps, *slots, *weights)
        return parts, token

    def mid(e, h, totals, products, deps=()):
        others = products if e == local - 1 and h == 1 else []
        shape = wide_shape if others else piece_shape
        return call(
            functools.partial(mid_kernel, len(deps), len(others)),
            1,
            [ANY_SPEC] * len(deps)
            + [whole_spec(piece_shape)] * 3
            + [whole_spec((rows, 128))] * len(others),
            [whole_spec(shape), whole_spec((rows, 128))],
            [like(shape), like((rows, 128), F32)],
            20 * rows * tile,
            4 * piece_bytes,
        )(*deps, *totals, *others)

    def add(a, b, deps):
        return call(
            functools.partial(add_kernel, len(deps)),
            1,
            [ANY_SPEC] * len(deps) + [spec_of(a)] * 2,
            spec_of(a),
            like(a.shape, a.dtype),
            a.size,
            3 * a.size * a.dtype.itemsize,
        )(*deps, a, b)

    def half(e, pieces, deps):
        flat = [x for group in pieces for x in group]
        return call(
            functools.partial(half_kernel, n, e, [len(g) for g in pieces[1:]], len(deps)),
            1,
            [SMEM_SPEC] + [ANY_SPEC] * len(deps) + [spec_of(x) for x in flat] + [HBM_SPEC] * 3,
            [whole_spec(slot_shape)] * 2 + [whole_spec(TOKEN)],
            [like(slot_shape, F32)] * 2 + [like(TOKEN, F32)],
            3 * mac,
            2 * weight_bytes + len(flat) * piece_bytes,
            scratch_shapes=held_weights,
        )(scal, *deps, *flat, *weights)

    def out(e, begun, pieces, prev, deps):
        flat = [x for group in pieces for x in group]
        last = e == local - 1
        sum_shape = (chips, 2, count, width)
        return call(
            functools.partial(out_kernel, n, e, e > 0, [len(g) for g in pieces[1:]], len(deps)),
            1,
            [SMEM_SPEC]
            + [ANY_SPEC] * len(deps)
            + [whole_spec(route_shape)]
            + [whole_spec(slot_shape)] * 2
            + ([whole_spec(sum_shape)] * 2 if e > 0 else [])
            + [spec_of(x) for x in flat]
            + [HBM_SPEC] * 3,
            [whole_spec(sum_shape)] * 2 + [whole_spec(TOKEN)],
            [like(sum_shape, BF16 if last else F32)] * 2 + [like(TOKEN, F32)],
            3 * mac,
            2 * weight_bytes + len(flat) * piece_bytes,
            scratch_shapes=held_weights + [pltpu.VMEM(slot_shape, BF16)] * 2,
        )(scal, *deps, routes, *begun, *prev, *flat, *weights)

    def grad(e, h, slots, pieces, prev, deps):
        flat = [x for group in pieces for x in group]
        base = 3 + len(deps) + len(flat)
        wide = pl.BlockSpec((1, width, tile), lambda g: (e, 0, h))
        return call(
            functools.partial(
                grad_kernel, n, len(prev) > 0, [len(g) for g in pieces[1:]], len(deps)
            ),
            1,
            [SMEM_SPEC]
            + [whole_spec(slot_shape)] * 2
            + [ANY_SPEC] * len(deps)
            + [spec_of(x) for x in flat]
            + [ANY_SPEC] * len(prev),
            [wide, wide, pl.BlockSpec((1, tile, width), lambda g: (e, h, 0)), whole_spec(TOKEN)],
            [like(w.shape) for w in weights] + [like(TOKEN, F32)],
            3 * mac,
            2 * weight_bytes + len(flat) * piece_bytes,
            input_output_aliases={base + k: k for k in range(len(prev))},
        )(scal, *slots, *deps, *flat, *prev)

    def product_sums(pieces, deps):
        flat = [x for group in pieces for x in group]
        dense_shape = (chips, experts_all, count)
        return call(
            functools.partial(product_kernel, n, local, [len(g) for g in pieces[1:]], len(deps)),
            1,
            [SMEM_SPEC, whole_spec(route_shape)]
            + [ANY_SPEC] * len(deps)
            + [spec_of(x) for x in flat],
            [whole_spec(dense_shape)] * 2,
            [like(dense_shape, F32)] * 2,
            local * all_rows * count * 16,
            len(flat) * piece_bytes,
            scratch_shapes=[pltpu.VMEM((n, extra, 128), BF16)],
        )(scal, routes, *deps, *flat)

    def relay(value, deps):
        return call(
            functools.partial(relay_kernel, len(deps)),
            1,
            [ANY_SPEC] * len(deps) + [spec_of(value)],
            spec_of(value),
            like(value.shape, value.dtype),
            0,
            2 * value.size * value.dtype.itemsize,
        )(*deps, value)

    along_z = Line("dp", n, 1)

    def outer(value):
        return along_z.send(value, [(0, 1), (1, 0), (2, 3), (3, 2)])

    def inner(value):
        pairs = []
        for p in range(peers):
            pairs += [(p * n + 1, p * n + 2), (p * n + 2, p * n + 1)]
            pairs += [(p * n + end, (p ^ 1) * n + end) for end in (0, n - 1)]
        return lax.ppermute(value, ("expert", "dp"), pairs)

    def unless_end(value):
        return jnp.where(at_end, jnp.zeros_like(value), value)

    products, sums, grads = [], [], []

    def send_home(near, far, add):
        near = add(near, across.send(far, swap))
        right, left = along_x.scatter([near[q] for q in range(chips)], add)
        home = near[0].astype(F32) + right.astype(F32)
        return near, home if left is None else home + left.astype(F32)

    if swaps:
        flight, arrived = [None, None], None
        slots, x0, _, routes = fill(0, [])
        parts, grad_token = [x0, more(0, slots, [])[0]], None
        for e in range(local):
            first, second, totals, halves = [], [], [], []
            following, seen = e < local - 1, [[], []]
            if following:
                next_slots, next0, token_0, _ = fill(e + 1, [] if e == 0 else [flight[0][2]])
            for h in range(2):
                x = parts[h]
                if e == 0:
                    first.append((outer(x[3]), None))
                else:
                    y, got_a, got_b = flight[h]
                    if h == 1 and following:
                        x[3] = relay(x[3], [token_0])
                    first.append((outer(jnp.where(at_end, x[3], got_b)), inner(got_a)))
            if grad_token is not None:
                seen[0].append(grad_token)
            if following and e == 0:
                seen[0].append(token_0)
            for h in range(2):
                x, (a1, b1) = parts[h], first[h]
                send_a2 = x[2] if e == 0 else jnp.where(at_end, x[2], b1)
                send_b2 = add(x[3], a1, seen[h])
                second.append((outer(send_a2), inner(send_b2)))
                if h == 0 and following:
                    next1, token_1 = more(e + 1, next_slots, [send_b2])
                    seen[1].append(token_1)
                if e > 0:
                    y, got_a, got_b = flight[h]
                    halves.append([(y,), (got_a,), (a1, got_b), (second[h][0], b1)])
            waits = [[], []]
            if e > 0:
                *begun, half_token = half(e - 1, halves[0], [])
                *sums, out_token = out(e - 1, begun, halves[1], sums, [])
                waits[0] = [out_token]
            for h in range(2):
                x, (a2, b2) = parts[h], second[h]
                both = add(x[1], b2, [half_token]) if e > 0 and h == 1 else add_rounded(x[1], b2)
                a3 = outer(jnp.where(at_end, x[1], both))
                b3 = inner(unless_end(add_rounded(x[2], a2)))
                totals.append((x[0], a3, b3))
            for h in range(2):
                y, product = mid(e, h, totals[h], products, waits[h])
                products.append(product)
                flight[h] = (y, outer(y), inner(y))
                if e > 0 and following:
                    *grads, grad_token = grad(e - 1, h, arrived, halves[h], grads, [y])
                    if h == 0:
                        waits[1] = [grad_token]
            late = (arrived, halves)
            arrived = slots
            if following:
                slots, parts = next_slots, [next0, next1]
        halves = []
        for h in range(2):
            y, got_a, got_b = flight[h]
            a1, b1 = outer(got_b), inner(got_a)
            a2 = outer(b1)
            halves.append([(y,), (got_a,), (a1, got_b), (a2, b1)])
        *grads, grad_token = grad(local - 2, 0, late[0], late[1][0], grads, [flight[0][1]])
        wait = [grad_token]
    else:
        late, started = None, []
        for e in range(local):
            slots, x0, _, routes = fill(e, [])
            parts = [x0, more(e, slots, [])[0]]
            started.append((slots, [(x[0], *along_z.scatter(x, add_rounded)) for x in parts]))
        for e in range(local):
            halves, arrived, wait = [], started[e][0], []
            for h in range(2):
                y, product = mid(e, h, started[e][1][h], products)
                products.append(product)
                halves.append([(y,)] + along_z.gather(y))
            if e < local - 1:
                *begun, _ = half(e, halves[0], [])
                *sums, _ = out(e, begun, halves[1], sums, [])
                for h in range(2):
                    *grads, _ = grad(e, h, arrived, halves[h], grads, [])

    *begun, _ = half(local - 1, halves[0], wait)
    near, far, _ = out(local - 1, begun, halves[1], sums, [])
    near_p, far_p = product_sums(halves[1], [near])
    hop, home = send_home(near, far, add_rounded)
    _, per_expert = send_home(near_p, far_p, lambda a, b: add(a, b, [hop]))
    if late is not None:
        *grads, _ = grad(local - 2, 1, late[0], late[1][1], grads, [hop])
    for h in range(2):
        *grads, _ = grad(local - 1, h, arrived, halves[h], grads, [hop])
    combine_grad = jnp.sum(jnp.where(named, per_expert[None], 0.0), axis=1) / combine_t
    return (home[0].astype(BF16), home[1].astype(BF16), *grads, combine_grad.T)


def solution(mesh):
    return jax.shard_map(
        body,
        mesh=mesh,
        in_specs=(
            P(("group", "expert"), "dp"),
            P(("group", "expert"), None),
            P(("group", "expert"), None),
            P("expert", "dp", None),
            P("expert", "dp", None),
            P("expert", None, "dp"),
            P(("group", "expert"), "dp"),
        ),
        out_specs=(
            P(("group", "expert"), "dp"),
            P(("group", "expert"), "dp"),
            P(("group", "expert"), "dp", None),
            P(("group", "expert"), "dp", None),
            P(("group", "expert"), None, "dp"),
            P(("group", "expert"), None),
        ),
        check_vma=False,
    )
```

```python
import functools

import jax
import jax.numpy as jnp
from jax import lax
from jax.experimental import pallas as pl
from jax.experimental.pallas import tpu as pltpu
from jax.sharding import PartitionSpec as P

F32, BF16 = jnp.float32, jnp.bfloat16
VMEM_BYTES = 20 << 20
STREAMS = 3


def line_pairs(n, gather, step):
    if gather:
        senders = [i for i in range(step - 1, n - 1)]
    else:
        senders = [i for i in range(0, min(step, n - 1))]
    right = [(i, i + 1) for i in senders]
    left = [(n - 1 - i, n - 2 - i) for i in senders]
    return right, left


class Line:
    def __init__(self, axis, n, stride):
        self.axis, self.n, self.stride = axis, n, stride

    def send(self, value, pairs):
        wide = [
            (a * self.stride + c, b * self.stride + c) for a, b in pairs for c in range(self.stride)
        ]
        return lax.ppermute(value, self.axis, wide)

    def gather(self, own):
        n = self.n
        if n == 2:
            both = self.send(own, [(0, 1), (1, 0)])
            return [(both, both)]
        right, left, rights, lefts = own, own, [], []
        for step in range(1, n):
            pairs_r, pairs_l = line_pairs(n, True, step)
            right, left = self.send(right, pairs_r), self.send(left, pairs_l)
            rights.append(right)
            lefts.append(left)
        return [(rights[q - 1], lefts[n - q - 1]) for q in range(1, n)]

    def scatter(self, parts, add):
        n = self.n
        if n == 2:
            return self.send(parts[1], [(0, 1), (1, 0)]), None
        right, left = parts[1], parts[n - 1]
        for step in range(1, n):
            pairs_r, pairs_l = line_pairs(n, False, step)
            right, left = self.send(right, pairs_r), self.send(left, pairs_l)
            if step < n - 1:
                right, left = add(parts[step + 1], right), add(parts[n - 1 - step], left)
        return right, left


def add_rounded(a, b):
    return (a.astype(F32) + b.astype(F32)).astype(BF16)


def dot(a, b, dims=((1,), (0,))):
    return lax.dot_general(a, b, (dims, ((), ())), preferred_element_type=F32)


def routing(scal, routes, expert, rows):
    n = len(routes)
    choose, tokens = routes[0].shape[0] // 2, routes[0].shape[1]
    which = (scal[2 * n] + expert).astype(F32)
    routes = [route[...] for route in routes]
    hits = [route[0:choose] == which for route in routes]
    weights = [
        jnp.sum(jnp.where(hit, route[choose:], 0.0), axis=0, keepdims=True)
        for hit, route in zip(hits, routes)
    ]
    chosen = jnp.concatenate(
        [jnp.sum(jnp.where(hit, 1.0, 0.0), axis=0, keepdims=True) for hit in hits], axis=0
    )
    earlier = lax.broadcasted_iota(jnp.int32, (tokens, tokens), 0) < lax.broadcasted_iota(
        jnp.int32, (tokens, tokens), 1
    )
    slots = dot(chosen.astype(BF16), earlier.astype(F32).astype(BF16))
    slots = jnp.where(chosen > 0.0, slots, -1.0).astype(jnp.int32)
    row = lax.broadcasted_iota(jnp.int32, (rows, tokens), 0)
    return [(scal[k], weights[k], row == slots[k : k + 1]) for k in range(n)]


def span_of(position, rows):
    return pl.ds(pl.multiple_of(position * rows, rows), rows)


def weight_copies(expert, weights, held, sems):
    halves = []
    for h in range(STREAMS):
        copies = []
        for k, (source, target) in enumerate(zip(weights, held)):
            size = target.shape[0 if k == 2 else 1] // STREAMS
            span = pl.ds(h * size, size)
            src, dst = (
                (source.at[expert, span, :], target.at[span, :])
                if k == 2
                else (source.at[expert, :, span], target.at[:, span])
            )
            copies.append(pltpu.make_async_copy(src, dst, sems.at[h, k]))
        halves.append(copies)
    return halves


def route_blocks(choose, count, width):
    wide = max(1, width // count)
    return [(16 * (b // wide), count * (b % wide)) for b in range(4 * choose // 16)]


def pack_kernel(ids, combine, tokens, grads, pack):
    count, width = tokens.shape
    choose = ids.shape[0]
    pack[0:count, :] = tokens[...]
    pack[count : 2 * count, :] = grads[...]
    lines = [ids[...].astype(F32)] + [part.astype(F32) for part in thirds(combine[...])]
    lines = jnp.concatenate(lines, axis=0).astype(BF16)
    blocks = route_blocks(choose, count, width)
    pack[2 * count :, :] = jnp.zeros((pack.shape[0] - 2 * count, width), BF16)
    for b, (row, lane) in enumerate(blocks):
        pack[2 * count + row : 2 * count + row + 16, lane : lane + count] = lines[16 * b : 16 * b + 16]


def unpack_route(pack, choose, count):
    lines = [
        pack[2 * count + row : 2 * count + row + 16, lane : lane + count]
        for row, lane in route_blocks(choose, count, pack.shape[1])
    ]
    lines = jnp.concatenate(lines, axis=0).astype(F32)
    ids, high, middle, low = (lines[k * choose : (k + 1) * choose] for k in range(4))
    return jnp.concatenate([ids, (high + middle) + low], axis=0)


def pre_kernel(n, expert, choose, deps, scal, *refs):
    refs = refs[deps:]
    packs, weights, (in_ref, cot_ref, *refs) = refs[:n], refs[n : n + 3], refs[n + 3 :]
    outs, (token, routes, gw, uw, dw, sems) = refs[: STREAMS * n], refs[STREAMS * n :]
    rows, tile, count = in_ref.shape[0] // n, gw.shape[1] // STREAMS, routes.shape[2]
    copies = weight_copies(expert, weights, (gw, uw, dw), sems)
    for group in copies:
        for copy in group:
            copy.start()
    token[...] = jnp.zeros_like(token)
    found = [unpack_route(pack, choose, count) for pack in packs]
    for k in range(n):
        routes[k] = found[k]
    for k, (position, weight, hit) in enumerate(routing(scal, found, expert, rows)):
        pick = hit.astype(F32).astype(BF16)
        span = span_of(position, rows)
        in_ref[span, :] = dot(pick, packs[k][0:count, :]).astype(BF16)
        scale = jnp.sum(jnp.where(hit, weight, 0.0), axis=1, keepdims=True)
        cot_ref[span, :] = (dot(pick, packs[k][count : 2 * count, :]) * scale).astype(BF16)
    for h in range(STREAMS):
        for copy in copies[h]:
            copy.wait()
        part = slice(h * tile, (h + 1) * tile)
        gate = dot(in_ref[...], gw[:, part]).astype(BF16)
        up = dot(in_ref[...], uw[:, part]).astype(BF16)
        back = dot(cot_ref[...], dw[part, :], ((1,), (1,))).astype(BF16)
        for p in range(n):
            for k, value in enumerate((gate, up, back)):
                outs[h * n + p][pl.ds(k * rows, rows), :] = value[p * rows : (p + 1) * rows]


def thirds(value):
    high = value.astype(BF16)
    rest = value - high.astype(F32)
    middle = rest.astype(BF16)
    return high, middle, (rest - middle.astype(F32)).astype(BF16)


def mid_kernel(deps, others, *refs):
    own, right, left, *rest = refs[deps:]
    earlier, (out, product) = rest[:others], rest[others:]
    rows, tile = own.shape[0] // 3, own.shape[1]
    total = own[...].astype(F32) + right[...].astype(F32) + left[...].astype(F32)
    gate, up, back = (total[k * rows : (k + 1) * rows] for k in range(3))
    sig = jax.nn.sigmoid(gate)
    hidden = (gate * sig * up).astype(BF16)
    delta = back.astype(BF16).astype(F32)
    out[0:rows, :] = hidden
    out[rows : 2 * rows, :] = (delta * up * sig * (1.0 + gate * (1.0 - sig))).astype(BF16)
    out[2 * rows : 3 * rows, :] = (delta * (gate * sig)).astype(BF16)
    prod = hidden.astype(F32) * back
    lanes = product.shape[1]
    acc = prod[:, 0:lanes]
    for k in range(1, tile // lanes):
        acc = acc + prod[:, k * lanes : (k + 1) * lanes]
    product[...] = acc
    if others:
        partial = [ref[...] for ref in earlier] + [acc]
        ones, fill = jnp.ones((8, lanes), BF16), jnp.zeros((lanes - rows, lanes), F32)
        lines = []
        for e in range(len(partial) // STREAMS):
            wide = jnp.concatenate([sum(partial[STREAMS * e : STREAMS * (e + 1)]), fill], axis=0)
            total = sum(dot(ones, part, ((1,), (1,))) for part in thirds(wide))[0:1]
            lines += [part.astype(F32) for part in thirds(total)]
        extra = out.shape[0] - 3 * rows
        lines.append(jnp.zeros((extra - len(lines), lanes), F32))
        out[3 * rows :, :] = jnp.zeros((extra, tile), BF16)
        out[3 * rows :, 0:lanes] = jnp.concatenate(lines, axis=0).astype(BF16)


def add_kernel(deps, *refs):
    a, b, out = refs[deps:]
    out[...] = (a[...].astype(F32) + b[...].astype(F32)).astype(out.dtype)


def part_of(scal, n, q, group, start, size):
    span = pl.ds(start, size)
    if len(group) == 1:
        return group[0][span, :]
    return jnp.where(scal[n + q] > 0, group[0][span, :], group[1][span, :])


def load_rows(scal, n, which, pieces):
    rows = pieces[0][0].shape[0] // 48 * 16
    return jnp.concatenate(
        [part_of(scal, n, q, group, which * rows, rows) for q, group in enumerate(pieces)], axis=0
    )


def split_pieces(refs, sizes):
    halves, at = [], 0
    for _ in range(STREAMS):
        pieces = [refs[at : at + 1]]
        at += 1
        for size in sizes:
            pieces.append(refs[at : at + size])
            at += size
        halves.append(pieces)
    return halves, refs[at:]


def out_kernel(n, expert, has_prev, last, sizes, deps, scal, *refs):
    refs = refs[deps:]
    routes, refs = [refs[0].at[k] for k in range(n)], refs[1:]
    if has_prev:
        prev, refs = refs[:2], refs[2:]
    halves, refs = split_pieces(refs, sizes)
    weights, (near, far, token, *refs) = refs[:3], refs[3:]
    if last:
        near_p, far_p, *refs, held = refs
    gw, uw, dw, sems, eo_ref, idl_ref = refs
    copies = weight_copies(expert, weights, (gw, uw, dw), sems)
    for group in copies:
        for copy in group:
            copy.start()
    token[...] = jnp.zeros_like(token)
    spots = routing(scal, routes, expert, halves[0][0][0].shape[0] // 48 * 16)
    if last:
        send_products(scal, routes, expert + 1, halves[-1], held, near_p, far_p)
    tile = gw.shape[1] // STREAMS
    eo, idl = 0.0, 0.0
    for h in range(STREAMS):
        for copy in copies[h]:
            copy.wait()
        part = slice(h * tile, (h + 1) * tile)
        eo = eo + dot(load_rows(scal, n, 0, halves[h]), dw[part, :])
        idl = idl + dot(load_rows(scal, n, 1, halves[h]), gw[:, part], ((1,), (1,)))
        idl = idl + dot(load_rows(scal, n, 2, halves[h]), uw[:, part], ((1,), (1,)))
    rows = eo.shape[0] // n
    eo_ref[...], idl_ref[...] = eo.astype(BF16), idl.astype(BF16)
    for k, (position, weight, hit) in enumerate(spots):
        pick = hit.astype(F32)
        scaled = (pick * weight).astype(BF16)
        span = span_of(position, rows)
        layer = dot(scaled, eo_ref[span, :], ((0,), (0,)))
        back = dot(pick.astype(BF16), idl_ref[span, :], ((0,), (0,)))
        which, place = (near, k) if k < n // 2 else (far, k - n // 2)
        if has_prev:
            before = prev[0 if k < n // 2 else 1]
            layer, back = layer + before[place, 0], back + before[place, 1]
        which[place, 0] = layer.astype(which.dtype)
        which[place, 1] = back.astype(which.dtype)


def grad_kernel(n, has_prev, sizes, deps, scal, in_ref, cot_ref, *refs):
    refs = refs[deps:]
    halves, refs = split_pieces(refs, sizes)
    if has_prev:
        refs = refs[3:]
    gg, ug, dg, token = refs
    step = pl.program_id(0)
    token[...] = jnp.zeros_like(token)
    for h in range(STREAMS):

        @pl.when(step == h)
        def _():
            gg[0] = dot(in_ref[...], load_rows(scal, n, 1, halves[h]), ((0,), (0,))).astype(BF16)
            ug[0] = dot(in_ref[...], load_rows(scal, n, 2, halves[h]), ((0,), (0,))).astype(BF16)
            dg[0] = dot(load_rows(scal, n, 0, halves[h]), cot_ref[...], ((0,), (0,))).astype(BF16)


def send_products(scal, routes, local, pieces, held, near, far):
    n, (_, extra, lanes) = len(routes), held.shape
    first = pieces[0][0].shape[0] - extra
    for q, group in enumerate(pieces):
        held[q] = part_of(scal, n, q, group, first, extra)[:, 0:lanes]
    experts_all, tokens = near.shape[1:]
    ids = lax.broadcasted_iota(jnp.int32, (experts_all, tokens), 0)
    sums = [jnp.zeros((experts_all, tokens), F32) for _ in range(n)]
    for e in range(local):
        for k, (position, _, hit) in enumerate(routing(scal, routes, e, lanes)):
            found = dot(held[position], hit.astype(F32).astype(BF16))
            value = found[3 * e : 3 * e + 1] + found[3 * e + 1 : 3 * e + 2] + found[3 * e + 2 : 3 * e + 3]
            sums[k] = sums[k] + jnp.where(ids == scal[2 * n] + e, value, 0.0)
    for k in range(n):
        if k < n // 2:
            near[k] = sums[k]
        else:
            far[k - n // 2] = sums[k]


def in_hbm(array):
    return pltpu.with_memory_space_constraint(array, pltpu.HBM)


def whole_spec(shape):
    return pl.BlockSpec(tuple(shape), lambda g: (0,) * len(shape))


def spec_of(array):
    return whole_spec(array.shape)


def like(shape, dtype=BF16):
    return jax.ShapeDtypeStruct(tuple(shape), dtype)


SMEM_SPEC = pl.BlockSpec(memory_space=pltpu.SMEM)
ANY_SPEC = pl.BlockSpec(memory_space=pl.ANY)
HBM_SPEC = pl.BlockSpec(memory_space=pltpu.HBM)
TOKEN = (8, 128)


def call(kernel, grid, in_specs, out_specs, out_shape, flops, moved, **rest):
    return pl.pallas_call(
        kernel,
        grid=(grid,),
        in_specs=in_specs,
        out_specs=out_specs,
        out_shape=out_shape,
        compiler_params=pltpu.CompilerParams(vmem_limit_bytes=VMEM_BYTES),
        cost_estimate=pl.CostEstimate(flops=flops, bytes_accessed=moved, transcendentals=0),
        **rest,
    )


def body(tokens, expert_ids, combine, gate_weight, up_weight, down_weight, out_grad):
    peers, n = lax.axis_size("expert"), lax.axis_size("dp")
    assert peers == n
    chips = peers // 2
    local, width, hidden = gate_weight.shape
    count, choose = expert_ids.shape
    experts_all = peers * local
    capacity = count * choose * 5 // (4 * experts_all)
    rows = -(-capacity // 16) * 16
    all_rows = n * rows
    tile = hidden // STREAMS
    swaps = n == 4

    me, here = lax.axis_index("expert"), lax.axis_index("dp")
    at_end = (here == 0) | (here == n - 1)
    table = []
    for place in range(n):
        block = 2 * lax.rem(me // 2 - place % chips + chips, chips) + lax.rem(
            lax.rem(me, 2) + place // chips, 2
        )
        if swaps:
            across_middle = jnp.where((block == 0) | (block == 3), 3, 2)
            position = jnp.where(
                block == here, 0, jnp.where(block // 2 == here // 2, 1, across_middle)
            )
        else:
            position = lax.rem(here - block + n, n)
        table.append(position)
    flags = [at_end if swaps else here >= q for q in range(n)]
    scal = jnp.stack(
        [jnp.asarray(v).astype(jnp.int32) for v in table + flags + [me * local, at_end]]
    )

    ids_t, combine_t = expert_ids.T, combine.T
    named = ids_t[:, None, :] == jnp.arange(experts_all, dtype=jnp.int32)[None, :, None]

    along_x, across = Line("expert", chips, 2), Line("expert", peers, 1)
    swap = [(2 * x + c, 2 * x + 1 - c) for x in range(chips) for c in range(2)]

    def gather_blocks(own):
        found = [own] + [
            right if right is left else jnp.where(me // 2 >= q, right, left)
            for q, (right, left) in enumerate(along_x.gather(own), 1)
        ]
        return found + [across.send(piece, swap) for piece in found]

    route_rows = 16 + max(row for row, _ in route_blocks(choose, count, width))
    pack_shape = (2 * count + route_rows, width)
    pack = call(
        pack_kernel,
        1,
        [spec_of(ids_t), spec_of(combine_t), spec_of(tokens), spec_of(out_grad)],
        whole_spec(pack_shape),
        like(pack_shape),
        count * width,
        8 * count * width,
    )(*(in_hbm(x) for x in (ids_t, combine_t, tokens, out_grad)))
    packs = gather_blocks(pack)
    route_shape = (n, 2 * choose, count)

    mac = all_rows * width * hidden
    weight_bytes = 2 * width * hidden
    piece_shape = (3 * rows, tile)
    extra = -(-3 * local // 16) * 16
    wide_shape = (3 * rows + extra, tile)
    piece_bytes = 2 * 3 * rows * tile
    slot_shape = (all_rows, width)

    weights = [in_hbm(w) for w in (gate_weight, up_weight, down_weight)]
    held_weights = [pltpu.VMEM(w.shape[1:], BF16) for w in weights] + [
        pltpu.SemaphoreType.DMA((STREAMS, 3))
    ]

    def grad_specs(e):
        wide = pl.BlockSpec((1, width, tile), lambda g: (e, 0, g))
        return [wide, wide, pl.BlockSpec((1, tile, width), lambda g: (e, g, 0))]

    def pre(e, deps):
        inputs, cot, *parts, token, found = call(
            functools.partial(pre_kernel, n, e, choose, len(deps)),
            1,
            [SMEM_SPEC] + [ANY_SPEC] * len(deps) + [spec_of(x) for x in packs] + [HBM_SPEC] * 3,
            [whole_spec(slot_shape)] * 2
            + [whole_spec(piece_shape)] * (STREAMS * n)
            + [whole_spec(TOKEN), whole_spec(route_shape)],
            [like(slot_shape)] * 2
            + [like(piece_shape)] * (STREAMS * n)
            + [like(TOKEN, F32), like(route_shape, F32)],
            6 * mac,
            3 * weight_bytes + STREAMS * n * piece_bytes,
            scratch_shapes=held_weights,
        )(scal, *deps, *packs, *weights)
        parts = [parts[h * n : (h + 1) * n] for h in range(STREAMS)]
        return (inputs, cot), parts, token, found

    def mid(e, h, totals, products, deps=()):
        others = products if e == local - 1 and h == STREAMS - 1 else []
        shape = wide_shape if others else piece_shape
        return call(
            functools.partial(mid_kernel, len(deps), len(others)),
            1,
            [ANY_SPEC] * len(deps)
            + [whole_spec(piece_shape)] * 3
            + [whole_spec((rows, 128))] * len(others),
            [whole_spec(shape), whole_spec((rows, 128))],
            [like(shape), like((rows, 128), F32)],
            20 * rows * tile,
            4 * piece_bytes,
        )(*deps, *totals, *others)

    def add(a, b, deps):
        return call(
            functools.partial(add_kernel, len(deps)),
            1,
            [ANY_SPEC] * len(deps) + [spec_of(a)] * 2,
            spec_of(a),
            like(a.shape, a.dtype),
            a.size,
            3 * a.size * a.dtype.itemsize,
        )(*deps, a, b)

    def flatten(halves):
        return [x for pieces in halves for group in pieces for x in group]

    def sizes_of(pieces):
        return [len(group) for group in pieces[1:]]

    def out(e, halves, prev, deps):
        flat = flatten(halves)
        last = e == local - 1
        dense_shape = (chips, experts_all, count)
        sum_shape = (chips, 2, count, width)
        return call(
            functools.partial(out_kernel, n, e, e > 0, last, sizes_of(halves[0]), len(deps)),
            1,
            [SMEM_SPEC]
            + [ANY_SPEC] * len(deps)
            + [whole_spec(route_shape)]
            + ([whole_spec(sum_shape)] * 2 if e > 0 else [])
            + [spec_of(x) for x in flat]
            + [HBM_SPEC] * 3,
            [whole_spec(sum_shape)] * 2
            + [whole_spec(TOKEN)]
            + ([whole_spec(dense_shape)] * 2 if last else []),
            [like(sum_shape, BF16 if last else F32)] * 2
            + [like(TOKEN, F32)]
            + ([like(dense_shape, F32)] * 2 if last else []),
            6 * mac,
            3 * weight_bytes + len(flat) * piece_bytes,
            scratch_shapes=held_weights
            + [pltpu.VMEM(slot_shape, BF16)] * 2
            + ([pltpu.VMEM((n, extra, 128), BF16)] if last else []),
        )(scal, *deps, routes, *prev, *flat, *weights)

    def grad(e, slots, halves, prev, deps):
        flat = flatten(halves)
        base = 3 + len(deps) + len(flat)
        return call(
            functools.partial(grad_kernel, n, e > 0, sizes_of(halves[0]), len(deps)),
            STREAMS,
            [SMEM_SPEC]
            + [whole_spec(slot_shape)] * 2
            + [ANY_SPEC] * len(deps)
            + [spec_of(x) for x in flat]
            + ([ANY_SPEC] * 3 if e > 0 else []),
            grad_specs(e) + [whole_spec(TOKEN)],
            [like(w.shape) for w in weights] + [like(TOKEN, F32)],
            6 * mac,
            3 * weight_bytes + len(flat) * piece_bytes,
            input_output_aliases={base + k: k for k in range(3)} if e > 0 else {},
        )(scal, *slots, *deps, *flat, *prev)

    along_z = Line("dp", n, 1)

    def outer(value):
        return along_z.send(value, [(0, 1), (1, 0), (2, 3), (3, 2)])

    def inner(value):
        pairs = []
        for p in range(peers):
            pairs += [(p * n + 1, p * n + 2), (p * n + 2, p * n + 1)]
            pairs += [(p * n + end, (p ^ 1) * n + end) for end in (0, n - 1)]
        return lax.ppermute(value, ("expert", "dp"), pairs)

    def unless_end(value):
        return jnp.where(at_end, jnp.zeros_like(value), value)

    products, sums, grads = [], [], []

    def send_home(near, far, add):
        near = add(near, across.send(far, swap))
        right, left = along_x.scatter([near[q] for q in range(chips)], add)
        home = near[0].astype(F32) + right.astype(F32)
        return near, home if left is None else home + left.astype(F32)

    if swaps:
        flight, arrived, streams = [None] * STREAMS, None, range(STREAMS)
        slots, parts, _, routes = pre(0, [])
        grad_token = None
        for e in range(local):
            following = e < local - 1
            first, second, totals, halves = [], [], [], []
            for h in streams:
                x = parts[h]
                if e == 0:
                    first.append((outer(x[3]), None))
                else:
                    y, got_a, got_b = flight[h]
                    first.append((outer(jnp.where(at_end, x[3], got_b)), inner(got_a)))
            seen = [[] for _ in streams]
            if following:
                next_slots, next_parts, token, _ = pre(e + 1, [] if e == 0 else [flight[1][2]])
                seen[0 if e == 0 else STREAMS - 1].append(token)
            if grad_token is not None:
                seen[0].append(grad_token)
            for h in streams:
                x, (a1, b1) = parts[h], first[h]
                send_a2 = x[2] if e == 0 else jnp.where(at_end, x[2], b1)
                second.append((outer(send_a2), inner(add(x[3], a1, seen[h]))))
                if e > 0:
                    y, got_a, got_b = flight[h]
                    halves.append([(y,), (got_a,), (a1, got_b), (second[h][0], b1)])
            for h in streams:
                x, (a2, b2) = parts[h], second[h]
                a3 = outer(jnp.where(at_end, x[1], add_rounded(x[1], b2)))
                b3 = inner(unless_end(add_rounded(x[2], a2)))
                totals.append((x[0], a3, b3))
            wait = []
            if e > 0:
                *sums, out_token = out(e - 1, halves, sums, [])
                wait = [out_token]
            for h in streams:
                y, product = mid(e, h, totals[h], products, wait if h == 0 else [])
                products.append(product)
                flight[h] = (y, outer(y), inner(y))
            if e > 0:
                *grads, grad_token = grad(e - 1, arrived, halves, grads, [flight[-1][0]])
            arrived = slots
            if following:
                slots, parts = next_slots, next_parts
        halves = []
        for h in streams:
            y, got_a, got_b = flight[h]
            a1, b1 = outer(got_b), inner(got_a)
            a2 = outer(b1)
            halves.append([(y,), (got_a,), (a1, got_b), (a2, b1)])
        wait = [grad_token]
    else:
        begun = []
        for e in range(local):
            slots, parts, _, routes = pre(e, [])
            begun.append((slots, [(x[0], *along_z.scatter(x, add_rounded)) for x in parts]))
        for e in range(local):
            halves, arrived, wait = [], begun[e][0], []
            for h in range(STREAMS):
                y, product = mid(e, h, begun[e][1][h], products)
                products.append(product)
                halves.append([(y,)] + along_z.gather(y))
            if e < local - 1:
                *sums, _ = out(e, halves, sums, [])
                *grads, _ = grad(e, arrived, halves, grads, [])

    near, far, _, near_p, far_p = out(local - 1, halves, sums, wait)
    hop, home = send_home(near, far, add_rounded)
    *grads, token = grad(local - 1, arrived, halves, grads, [hop])
    _, per_expert = send_home(near_p, far_p, lambda a, b: add(a, b, [token]))
    combine_grad = jnp.sum(jnp.where(named, per_expert[None], 0.0), axis=1) / combine_t
    return (home[0].astype(BF16), home[1].astype(BF16), *grads, combine_grad.T)


def solution(mesh):
    return jax.shard_map(
        body,
        mesh=mesh,
        in_specs=(
            P(("group", "expert"), "dp"),
            P(("group", "expert"), None),
            P(("group", "expert"), None),
            P("expert", "dp", None),
            P("expert", "dp", None),
            P("expert", None, "dp"),
            P(("group", "expert"), "dp"),
        ),
        out_specs=(
            P(("group", "expert"), "dp"),
            P(("group", "expert"), "dp"),
            P(("group", "expert"), "dp", None),
            P(("group", "expert"), "dp", None),
            P(("group", "expert"), None, "dp"),
            P(("group", "expert"), None),
        ),
        check_vma=False,
    )
```

```python
import functools

import jax
import jax.numpy as jnp
from jax import lax
from jax.experimental import pallas as pl
from jax.experimental.pallas import tpu as pltpu
from jax.sharding import PartitionSpec as P

F32, BF16 = jnp.float32, jnp.bfloat16
VMEM_BYTES = 20 << 20
STREAMS = 2


def line_pairs(n, gather, step):
    if gather:
        senders = [i for i in range(step - 1, n - 1)]
    else:
        senders = [i for i in range(0, min(step, n - 1))]
    right = [(i, i + 1) for i in senders]
    left = [(n - 1 - i, n - 2 - i) for i in senders]
    return right, left


class Line:
    def __init__(self, axis, n, stride):
        self.axis, self.n, self.stride = axis, n, stride

    def send(self, value, pairs):
        wide = [
            (a * self.stride + c, b * self.stride + c) for a, b in pairs for c in range(self.stride)
        ]
        return lax.ppermute(value, self.axis, wide)

    def gather(self, own):
        n = self.n
        if n == 2:
            both = self.send(own, [(0, 1), (1, 0)])
            return [(both, both)]
        right, left, rights, lefts = own, own, [], []
        for step in range(1, n):
            pairs_r, pairs_l = line_pairs(n, True, step)
            right, left = self.send(right, pairs_r), self.send(left, pairs_l)
            rights.append(right)
            lefts.append(left)
        return [(rights[q - 1], lefts[n - q - 1]) for q in range(1, n)]

    def scatter(self, parts, add):
        n = self.n
        if n == 2:
            return self.send(parts[1], [(0, 1), (1, 0)]), None
        right, left = parts[1], parts[n - 1]
        for step in range(1, n):
            pairs_r, pairs_l = line_pairs(n, False, step)
            right, left = self.send(right, pairs_r), self.send(left, pairs_l)
            if step < n - 1:
                right, left = add(parts[step + 1], right), add(parts[n - 1 - step], left)
        return right, left


def add_rounded(a, b):
    return (a.astype(F32) + b.astype(F32)).astype(BF16)


def dot(a, b, dims=((1,), (0,))):
    return lax.dot_general(a, b, (dims, ((), ())), preferred_element_type=F32)


def routing(scal, routes, expert, rows):
    n = len(routes)
    choose, tokens = routes[0].shape[0] // 2, routes[0].shape[1]
    which = (scal[2 * n] + expert).astype(F32)
    routes = [route[...] for route in routes]
    hits = [route[0:choose] == which for route in routes]
    weights = [
        jnp.sum(jnp.where(hit, route[choose:], 0.0), axis=0, keepdims=True)
        for hit, route in zip(hits, routes)
    ]
    chosen = jnp.concatenate(
        [jnp.sum(jnp.where(hit, 1.0, 0.0), axis=0, keepdims=True) for hit in hits], axis=0
    )
    earlier = lax.broadcasted_iota(jnp.int32, (tokens, tokens), 0) < lax.broadcasted_iota(
        jnp.int32, (tokens, tokens), 1
    )
    slots = dot(chosen.astype(BF16), earlier.astype(F32).astype(BF16))
    slots = jnp.where(chosen > 0.0, slots, -1.0).astype(jnp.int32)
    row = lax.broadcasted_iota(jnp.int32, (rows, tokens), 0)
    return [(scal[k], weights[k], row == slots[k : k + 1]) for k in range(n)]


def span_of(position, rows):
    return pl.ds(pl.multiple_of(position * rows, rows), rows)


def weight_copies(expert, weights, held, sems):
    halves = []
    for h in range(STREAMS):
        copies = []
        for k, (source, target) in enumerate(zip(weights, held)):
            size = target.shape[0 if k == 2 else 1] // STREAMS
            span = pl.ds(h * size, size)
            src, dst = (
                (source.at[expert, span, :], target.at[span, :])
                if k == 2
                else (source.at[expert, :, span], target.at[:, span])
            )
            copies.append(pltpu.make_async_copy(src, dst, sems.at[h, k]))
        halves.append(copies)
    return halves


def route_blocks(choose, count, width):
    wide = max(1, width // count)
    return [(16 * (b // wide), count * (b % wide)) for b in range(4 * choose // 16)]


def pack_kernel(ids, combine, tokens, grads, pack):
    count, width = tokens.shape
    choose = ids.shape[0]
    pack[0:count, :] = tokens[...]
    pack[count : 2 * count, :] = grads[...]
    lines = [ids[...].astype(F32)] + [part.astype(F32) for part in thirds(combine[...])]
    lines = jnp.concatenate(lines, axis=0).astype(BF16)
    blocks = route_blocks(choose, count, width)
    pack[2 * count :, :] = jnp.zeros((pack.shape[0] - 2 * count, width), BF16)
    for b, (row, lane) in enumerate(blocks):
        pack[2 * count + row : 2 * count + row + 16, lane : lane + count] = lines[16 * b : 16 * b + 16]


def unpack_route(pack, choose, count):
    lines = [
        pack[2 * count + row : 2 * count + row + 16, lane : lane + count]
        for row, lane in route_blocks(choose, count, pack.shape[1])
    ]
    lines = jnp.concatenate(lines, axis=0).astype(F32)
    ids, high, middle, low = (lines[k * choose : (k + 1) * choose] for k in range(4))
    return jnp.concatenate([ids, (high + middle) + low], axis=0)


def pre_kernel(n, expert, choose, deps, scal, *refs):
    refs = refs[deps:]
    packs, weights, (in_ref, cot_ref, *refs) = refs[:n], refs[n : n + 3], refs[n + 3 :]
    outs, (token, routes, gw, uw, dw, sems) = refs[: STREAMS * n], refs[STREAMS * n :]
    rows, tile, count = in_ref.shape[0] // n, gw.shape[1] // STREAMS, routes.shape[2]
    copies = weight_copies(expert, weights, (gw, uw, dw), sems)
    for group in copies:
        for copy in group:
            copy.start()
    token[...] = jnp.zeros_like(token)
    found = [unpack_route(pack, choose, count) for pack in packs]
    for k in range(n):
        routes[k] = found[k]
    for k, (position, weight, hit) in enumerate(routing(scal, found, expert, rows)):
        pick = hit.astype(F32).astype(BF16)
        span = span_of(position, rows)
        in_ref[span, :] = dot(pick, packs[k][0:count, :]).astype(BF16)
        scale = jnp.sum(jnp.where(hit, weight, 0.0), axis=1, keepdims=True)
        cot_ref[span, :] = (dot(pick, packs[k][count : 2 * count, :]) * scale).astype(BF16)
    for h in range(STREAMS):
        for copy in copies[h]:
            copy.wait()
        part = slice(h * tile, (h + 1) * tile)
        gate = dot(in_ref[...], gw[:, part]).astype(BF16)
        up = dot(in_ref[...], uw[:, part]).astype(BF16)
        back = dot(cot_ref[...], dw[part, :], ((1,), (1,))).astype(BF16)
        for p in range(n):
            for k, value in enumerate((gate, up, back)):
                outs[h * n + p][pl.ds(k * rows, rows), :] = value[p * rows : (p + 1) * rows]


def thirds(value):
    high = value.astype(BF16)
    rest = value - high.astype(F32)
    middle = rest.astype(BF16)
    return high, middle, (rest - middle.astype(F32)).astype(BF16)


def mid_kernel(deps, others, *refs):
    own, right, left, *rest = refs[deps:]
    earlier, (out, product) = rest[:others], rest[others:]
    rows, tile = own.shape[0] // 3, own.shape[1]
    total = own[...].astype(F32) + right[...].astype(F32) + left[...].astype(F32)
    gate, up, back = (total[k * rows : (k + 1) * rows] for k in range(3))
    sig = jax.nn.sigmoid(gate)
    hidden = (gate * sig * up).astype(BF16)
    delta = back.astype(BF16).astype(F32)
    out[0:rows, :] = hidden
    out[rows : 2 * rows, :] = (delta * up * sig * (1.0 + gate * (1.0 - sig))).astype(BF16)
    out[2 * rows : 3 * rows, :] = (delta * (gate * sig)).astype(BF16)
    prod = hidden.astype(F32) * back
    lanes = product.shape[1]
    acc = prod[:, 0:lanes]
    for k in range(1, tile // lanes):
        acc = acc + prod[:, k * lanes : (k + 1) * lanes]
    product[...] = acc
    if others:
        partial = [ref[...] for ref in earlier] + [acc]
        ones, fill = jnp.ones((8, lanes), BF16), jnp.zeros((lanes - rows, lanes), F32)
        lines = []
        for e in range(len(partial) // STREAMS):
            wide = jnp.concatenate([sum(partial[STREAMS * e : STREAMS * (e + 1)]), fill], axis=0)
            total = sum(dot(ones, part, ((1,), (1,))) for part in thirds(wide))[0:1]
            lines += [part.astype(F32) for part in thirds(total)]
        extra = out.shape[0] - 3 * rows
        lines.append(jnp.zeros((extra - len(lines), lanes), F32))
        out[3 * rows :, :] = jnp.zeros((extra, tile), BF16)
        out[3 * rows :, 0:lanes] = jnp.concatenate(lines, axis=0).astype(BF16)


def add_kernel(deps, *refs):
    a, b, out = refs[deps:]
    out[...] = (a[...].astype(F32) + b[...].astype(F32)).astype(out.dtype)


def part_of(scal, n, q, group, start, size):
    span = pl.ds(start, size)
    if len(group) == 1:
        return group[0][span, :]
    return jnp.where(scal[n + q] > 0, group[0][span, :], group[1][span, :])


def load_rows(scal, n, which, pieces):
    rows = pieces[0][0].shape[0] // 48 * 16
    return jnp.concatenate(
        [part_of(scal, n, q, group, which * rows, rows) for q, group in enumerate(pieces)], axis=0
    )


def split_pieces(refs, sizes):
    halves, at = [], 0
    for _ in range(STREAMS):
        pieces = [refs[at : at + 1]]
        at += 1
        for size in sizes:
            pieces.append(refs[at : at + size])
            at += size
        halves.append(pieces)
    return halves, refs[at:]


def out_kernel(n, expert, has_prev, last, sizes, deps, scal, *refs):
    refs = refs[deps:]
    routes, refs = [refs[0].at[k] for k in range(n)], refs[1:]
    if has_prev:
        prev, refs = refs[:2], refs[2:]
    halves, refs = split_pieces(refs, sizes)
    (gw, uw, dw), (near, far, token, *refs) = refs[:3], refs[3:]
    if last:
        near_p, far_p, *refs, held = refs
    eo_ref, idl_ref = refs
    token[...] = jnp.zeros_like(token)
    spots = routing(scal, routes, expert, halves[0][0][0].shape[0] // 48 * 16)
    if last:
        send_products(scal, routes, expert + 1, halves[-1], held, near_p, far_p)
    tile = gw.shape[1] // STREAMS
    eo, idl = 0.0, 0.0
    for h in range(STREAMS):
        part = slice(h * tile, (h + 1) * tile)
        eo = eo + dot(load_rows(scal, n, 0, halves[h]), dw[part, :])
        idl = idl + dot(load_rows(scal, n, 1, halves[h]), gw[:, part], ((1,), (1,)))
        idl = idl + dot(load_rows(scal, n, 2, halves[h]), uw[:, part], ((1,), (1,)))
    rows = eo.shape[0] // n
    eo_ref[...], idl_ref[...] = eo.astype(BF16), idl.astype(BF16)
    for k, (position, weight, hit) in enumerate(spots):
        pick = hit.astype(F32)
        scaled = (pick * weight).astype(BF16)
        span = span_of(position, rows)
        layer = dot(scaled, eo_ref[span, :], ((0,), (0,)))
        back = dot(pick.astype(BF16), idl_ref[span, :], ((0,), (0,)))
        which, place = (near, k) if k < n // 2 else (far, k - n // 2)
        if has_prev:
            before = prev[0 if k < n // 2 else 1]
            layer, back = layer + before[place, 0], back + before[place, 1]
        which[place, 0] = layer.astype(which.dtype)
        which[place, 1] = back.astype(which.dtype)


def grad_kernel(n, has_prev, sizes, deps, scal, in_ref, cot_ref, *refs):
    refs = refs[deps:]
    halves, refs = split_pieces(refs, sizes)
    if has_prev:
        refs = refs[3:]
    gg, ug, dg, token = refs
    step = pl.program_id(0)
    token[...] = jnp.zeros_like(token)
    for h in range(STREAMS):

        @pl.when(step == h)
        def _():
            deltas = [load_rows(scal, n, k, halves[h]) for k in (1, 2)]
            both = dot(in_ref[...], jnp.concatenate(deltas, axis=1), ((0,), (0,))).astype(BF16)
            gg[0], ug[0] = both[:, : gg.shape[2]], both[:, gg.shape[2] :]
            dg[0] = dot(load_rows(scal, n, 0, halves[h]), cot_ref[...], ((0,), (0,))).astype(BF16)


def send_products(scal, routes, local, pieces, held, near, far):
    n, (_, extra, lanes) = len(routes), held.shape
    first = pieces[0][0].shape[0] - extra
    for q, group in enumerate(pieces):
        held[q] = part_of(scal, n, q, group, first, extra)[:, 0:lanes]
    experts_all, tokens = near.shape[1:]
    ids = lax.broadcasted_iota(jnp.int32, (experts_all, tokens), 0)
    sums = [jnp.zeros((experts_all, tokens), F32) for _ in range(n)]
    for e in range(local):
        for k, (position, _, hit) in enumerate(routing(scal, routes, e, lanes)):
            found = dot(held[position], hit.astype(F32).astype(BF16))
            value = found[3 * e : 3 * e + 1] + found[3 * e + 1 : 3 * e + 2] + found[3 * e + 2 : 3 * e + 3]
            sums[k] = sums[k] + jnp.where(ids == scal[2 * n] + e, value, 0.0)
    for k in range(n):
        if k < n // 2:
            near[k] = sums[k]
        else:
            far[k - n // 2] = sums[k]


def in_hbm(array):
    return pltpu.with_memory_space_constraint(array, pltpu.HBM)


def whole_spec(shape):
    return pl.BlockSpec(tuple(shape), lambda g: (0,) * len(shape))


def spec_of(array):
    return whole_spec(array.shape)


def like(shape, dtype=BF16):
    return jax.ShapeDtypeStruct(tuple(shape), dtype)


SMEM_SPEC = pl.BlockSpec(memory_space=pltpu.SMEM)
ANY_SPEC = pl.BlockSpec(memory_space=pl.ANY)
HBM_SPEC = pl.BlockSpec(memory_space=pltpu.HBM)
TOKEN = (8, 128)


def call(kernel, grid, in_specs, out_specs, out_shape, flops, moved, **rest):
    return pl.pallas_call(
        kernel,
        grid=(grid,),
        in_specs=in_specs,
        out_specs=out_specs,
        out_shape=out_shape,
        compiler_params=pltpu.CompilerParams(vmem_limit_bytes=VMEM_BYTES),
        cost_estimate=pl.CostEstimate(flops=flops, bytes_accessed=moved, transcendentals=0),
        **rest,
    )


def body(tokens, expert_ids, combine, gate_weight, up_weight, down_weight, out_grad):
    peers, n = lax.axis_size("expert"), lax.axis_size("dp")
    assert peers == n
    chips = peers // 2
    local, width, hidden = gate_weight.shape
    count, choose = expert_ids.shape
    experts_all = peers * local
    capacity = count * choose * 5 // (4 * experts_all)
    rows = -(-capacity // 16) * 16
    all_rows = n * rows
    tile = hidden // STREAMS
    swaps = n == 4

    me, here = lax.axis_index("expert"), lax.axis_index("dp")
    at_end = (here == 0) | (here == n - 1)
    table = []
    for place in range(n):
        block = 2 * lax.rem(me // 2 - place % chips + chips, chips) + lax.rem(
            lax.rem(me, 2) + place // chips, 2
        )
        if swaps:
            across_middle = jnp.where((block == 0) | (block == 3), 3, 2)
            position = jnp.where(
                block == here, 0, jnp.where(block // 2 == here // 2, 1, across_middle)
            )
        else:
            position = lax.rem(here - block + n, n)
        table.append(position)
    flags = [at_end if swaps else here >= q for q in range(n)]
    scal = jnp.stack(
        [jnp.asarray(v).astype(jnp.int32) for v in table + flags + [me * local, at_end]]
    )

    ids_t, combine_t = expert_ids.T, combine.T
    named = ids_t[:, None, :] == jnp.arange(experts_all, dtype=jnp.int32)[None, :, None]

    along_x, across = Line("expert", chips, 2), Line("expert", peers, 1)
    swap = [(2 * x + c, 2 * x + 1 - c) for x in range(chips) for c in range(2)]

    def gather_blocks(own):
        found = [own] + [
            right if right is left else jnp.where(me // 2 >= q, right, left)
            for q, (right, left) in enumerate(along_x.gather(own), 1)
        ]
        return found + [across.send(piece, swap) for piece in found]

    route_rows = 16 + max(row for row, _ in route_blocks(choose, count, width))
    pack_shape = (2 * count + route_rows, width)
    pack = call(
        pack_kernel,
        1,
        [spec_of(ids_t), spec_of(combine_t), spec_of(tokens), spec_of(out_grad)],
        whole_spec(pack_shape),
        like(pack_shape),
        count * width,
        8 * count * width,
    )(*(in_hbm(x) for x in (ids_t, combine_t, tokens, out_grad)))
    packs = gather_blocks(pack)
    route_shape = (n, 2 * choose, count)

    mac = all_rows * width * hidden
    weight_bytes = 2 * width * hidden
    piece_shape = (3 * rows, tile)
    extra = -(-3 * local // 16) * 16
    wide_shape = (3 * rows + extra, tile)
    piece_bytes = 2 * 3 * rows * tile
    slot_shape = (all_rows, width)

    weights = [in_hbm(w) for w in (gate_weight, up_weight, down_weight)]
    def grad_specs(e):
        wide = pl.BlockSpec((1, width, tile), lambda g: (e, 0, g))
        return [wide, wide, pl.BlockSpec((1, tile, width), lambda g: (e, g, 0))]

    own_weights = []

    def pre(e, deps):
        inputs, cot, *parts, token, found, gw, uw, dw = call(
            functools.partial(pre_kernel, n, e, choose, len(deps)),
            1,
            [SMEM_SPEC] + [ANY_SPEC] * len(deps) + [spec_of(x) for x in packs] + [HBM_SPEC] * 3,
            [whole_spec(slot_shape)] * 2
            + [whole_spec(piece_shape)] * (STREAMS * n)
            + [whole_spec(TOKEN), whole_spec(route_shape)]
            + [whole_spec(w.shape[1:]) for w in weights],
            [like(slot_shape)] * 2
            + [like(piece_shape)] * (STREAMS * n)
            + [like(TOKEN, F32), like(route_shape, F32)]
            + [like(w.shape[1:]) for w in weights],
            6 * mac,
            3 * weight_bytes + STREAMS * n * piece_bytes,
            scratch_shapes=[pltpu.SemaphoreType.DMA((STREAMS, 3))],
        )(scal, *deps, *packs, *weights)
        parts = [parts[h * n : (h + 1) * n] for h in range(STREAMS)]
        own_weights.append((gw, uw, dw))
        return (inputs, cot), parts, token, found

    def mid(e, h, totals, products, deps=()):
        others = products if e == local - 1 and h == STREAMS - 1 else []
        shape = wide_shape if others else piece_shape
        return call(
            functools.partial(mid_kernel, len(deps), len(others)),
            1,
            [ANY_SPEC] * len(deps)
            + [whole_spec(piece_shape)] * 3
            + [whole_spec((rows, 128))] * len(others),
            [whole_spec(shape), whole_spec((rows, 128))],
            [like(shape), like((rows, 128), F32)],
            20 * rows * tile,
            4 * piece_bytes,
        )(*deps, *totals, *others)

    def add(a, b, deps):
        return call(
            functools.partial(add_kernel, len(deps)),
            1,
            [ANY_SPEC] * len(deps) + [spec_of(a)] * 2,
            spec_of(a),
            like(a.shape, a.dtype),
            a.size,
            3 * a.size * a.dtype.itemsize,
        )(*deps, a, b)

    def flatten(halves):
        return [x for pieces in halves for group in pieces for x in group]

    def sizes_of(pieces):
        return [len(group) for group in pieces[1:]]

    def out(e, halves, prev, deps):
        flat = flatten(halves)
        last = e == local - 1
        dense_shape = (chips, experts_all, count)
        sum_shape = (chips, 2, count, width)
        return call(
            functools.partial(out_kernel, n, e, e > 0, last, sizes_of(halves[0]), len(deps)),
            1,
            [SMEM_SPEC]
            + [ANY_SPEC] * len(deps)
            + [whole_spec(route_shape)]
            + ([whole_spec(sum_shape)] * 2 if e > 0 else [])
            + [spec_of(x) for x in flat]
            + [whole_spec(w.shape[1:]) for w in weights],
            [whole_spec(sum_shape)] * 2
            + [whole_spec(TOKEN)]
            + ([whole_spec(dense_shape)] * 2 if last else []),
            [like(sum_shape, BF16 if last else F32)] * 2
            + [like(TOKEN, F32)]
            + ([like(dense_shape, F32)] * 2 if last else []),
            6 * mac,
            3 * weight_bytes + len(flat) * piece_bytes,
            scratch_shapes=[pltpu.VMEM(slot_shape, BF16)] * 2
            + ([pltpu.VMEM((n, extra, 128), BF16)] if last else []),
        )(scal, *deps, routes, *prev, *flat, *own_weights[e])

    def grad(e, slots, halves, prev, deps):
        flat = flatten(halves)
        base = 3 + len(deps) + len(flat)
        return call(
            functools.partial(grad_kernel, n, e > 0, sizes_of(halves[0]), len(deps)),
            STREAMS,
            [SMEM_SPEC]
            + [whole_spec(slot_shape)] * 2
            + [ANY_SPEC] * len(deps)
            + [spec_of(x) for x in flat]
            + ([ANY_SPEC] * 3 if e > 0 else []),
            grad_specs(e) + [whole_spec(TOKEN)],
            [like(w.shape) for w in weights] + [like(TOKEN, F32)],
            6 * mac,
            3 * weight_bytes + len(flat) * piece_bytes,
            input_output_aliases={base + k: k for k in range(3)} if e > 0 else {},
        )(scal, *slots, *deps, *flat, *prev)

    along_z = Line("dp", n, 1)

    def outer(value):
        return along_z.send(value, [(0, 1), (1, 0), (2, 3), (3, 2)])

    def inner(value):
        pairs = []
        for p in range(peers):
            pairs += [(p * n + 1, p * n + 2), (p * n + 2, p * n + 1)]
            pairs += [(p * n + end, (p ^ 1) * n + end) for end in (0, n - 1)]
        return lax.ppermute(value, ("expert", "dp"), pairs)

    def unless_end(value):
        return jnp.where(at_end, jnp.zeros_like(value), value)

    products, sums, grads = [], [], []

    def send_home(near, far, add):
        near = add(near, across.send(far, swap))
        right, left = along_x.scatter([near[q] for q in range(chips)], add)
        home = near[0].astype(F32) + right.astype(F32)
        return near, home if left is None else home + left.astype(F32)

    if swaps:
        flight, arrived, streams = [None] * STREAMS, None, range(STREAMS)
        slots, parts, _, routes = pre(0, [])
        grad_token = None
        for e in range(local):
            following = e < local - 1
            first, second, totals, halves = [], [], [], []
            for h in streams:
                x = parts[h]
                if e == 0:
                    first.append((outer(x[3]), None))
                else:
                    y, got_a, got_b = flight[h]
                    first.append((outer(jnp.where(at_end, x[3], got_b)), inner(got_a)))
            seen = [[] for _ in streams]
            if following:
                next_slots, next_parts, token, _ = pre(e + 1, [] if e == 0 else [flight[1][2]])
                seen[0 if e == 0 else STREAMS - 1].append(token)
            if grad_token is not None:
                seen[0].append(grad_token)
            for h in streams:
                x, (a1, b1) = parts[h], first[h]
                send_a2 = x[2] if e == 0 else jnp.where(at_end, x[2], b1)
                second.append((outer(send_a2), inner(add(x[3], a1, seen[h]))))
                if e > 0:
                    y, got_a, got_b = flight[h]
                    halves.append([(y,), (got_a,), (a1, got_b), (second[h][0], b1)])
            for h in streams:
                x, (a2, b2) = parts[h], second[h]
                a3 = outer(jnp.where(at_end, x[1], add_rounded(x[1], b2)))
                b3 = inner(unless_end(add_rounded(x[2], a2)))
                totals.append((x[0], a3, b3))
            wait = []
            if e > 0:
                *sums, out_token = out(e - 1, halves, sums, [])
                wait = [out_token]
            for h in streams:
                y, product = mid(e, h, totals[h], products, wait if h == 0 else [])
                products.append(product)
                flight[h] = (y, outer(y), inner(y))
            if e > 0:
                *grads, grad_token = grad(e - 1, arrived, halves, grads, [flight[-1][0]])
            arrived = slots
            if following:
                slots, parts = next_slots, next_parts
        halves = []
        for h in streams:
            y, got_a, got_b = flight[h]
            a1, b1 = outer(got_b), inner(got_a)
            a2 = outer(b1)
            halves.append([(y,), (got_a,), (a1, got_b), (a2, b1)])
        wait = [grad_token]
    else:
        begun = []
        for e in range(local):
            slots, parts, _, routes = pre(e, [])
            begun.append((slots, [(x[0], *along_z.scatter(x, add_rounded)) for x in parts]))
        for e in range(local):
            halves, arrived, wait = [], begun[e][0], []
            for h in range(STREAMS):
                y, product = mid(e, h, begun[e][1][h], products)
                products.append(product)
                halves.append([(y,)] + along_z.gather(y))
            if e < local - 1:
                *sums, _ = out(e, halves, sums, [])
                *grads, _ = grad(e, arrived, halves, grads, [])

    near, far, _, near_p, far_p = out(local - 1, halves, sums, wait)
    hop, home = send_home(near, far, add_rounded)
    _, per_expert = send_home(near_p, far_p, lambda a, b: add(a, b, [hop]))
    *grads, _ = grad(local - 1, arrived, halves, grads, [hop])
    combine_grad = jnp.sum(jnp.where(named, per_expert[None], 0.0), axis=1) / combine_t
    return (home[0].astype(BF16), home[1].astype(BF16), *grads, combine_grad.T)


def solution(mesh):
    return jax.shard_map(
        body,
        mesh=mesh,
        in_specs=(
            P(("group", "expert"), "dp"),
            P(("group", "expert"), None),
            P(("group", "expert"), None),
            P("expert", "dp", None),
            P("expert", "dp", None),
            P("expert", None, "dp"),
            P(("group", "expert"), "dp"),
        ),
        out_specs=(
            P(("group", "expert"), "dp"),
            P(("group", "expert"), "dp"),
            P(("group", "expert"), "dp", None),
            P(("group", "expert"), "dp", None),
            P(("group", "expert"), None, "dp"),
            P(("group", "expert"), None),
        ),
        check_vma=False,
    )
```

```python
import functools

import jax
import jax.numpy as jnp
from jax import lax
from jax.experimental import pallas as pl
from jax.experimental.pallas import tpu as pltpu
from jax.sharding import PartitionSpec as P

F32, BF16 = jnp.float32, jnp.bfloat16
VMEM_BYTES = 20 << 20
STREAMS = 2


def line_pairs(n, gather, step):
    if gather:
        senders = [i for i in range(step - 1, n - 1)]
    else:
        senders = [i for i in range(0, min(step, n - 1))]
    right = [(i, i + 1) for i in senders]
    left = [(n - 1 - i, n - 2 - i) for i in senders]
    return right, left


class Line:
    def __init__(self, axis, n, stride):
        self.axis, self.n, self.stride = axis, n, stride

    def send(self, value, pairs):
        wide = [
            (a * self.stride + c, b * self.stride + c) for a, b in pairs for c in range(self.stride)
        ]
        return lax.ppermute(value, self.axis, wide)

    def gather(self, own):
        n = self.n
        if n == 2:
            both = self.send(own, [(0, 1), (1, 0)])
            return [(both, both)]
        right, left, rights, lefts = own, own, [], []
        for step in range(1, n):
            pairs_r, pairs_l = line_pairs(n, True, step)
            right, left = self.send(right, pairs_r), self.send(left, pairs_l)
            rights.append(right)
            lefts.append(left)
        return [(rights[q - 1], lefts[n - q - 1]) for q in range(1, n)]

    def scatter(self, parts, add):
        n = self.n
        if n == 2:
            return self.send(parts[1], [(0, 1), (1, 0)]), None
        right, left = parts[1], parts[n - 1]
        for step in range(1, n):
            pairs_r, pairs_l = line_pairs(n, False, step)
            right, left = self.send(right, pairs_r), self.send(left, pairs_l)
            if step < n - 1:
                right, left = add(parts[step + 1], right), add(parts[n - 1 - step], left)
        return right, left


def add_rounded(a, b):
    return (a.astype(F32) + b.astype(F32)).astype(BF16)


def dot(a, b, dims=((1,), (0,))):
    return lax.dot_general(a, b, (dims, ((), ())), preferred_element_type=F32)


def routing(scal, routes, expert, rows):
    n = len(routes)
    choose, tokens = routes[0].shape[0] // 2, routes[0].shape[1]
    which = (scal[2 * n] + expert).astype(F32)
    routes = [route[...] for route in routes]
    hits = [route[0:choose] == which for route in routes]
    weights = [
        jnp.sum(jnp.where(hit, route[choose:], 0.0), axis=0, keepdims=True)
        for hit, route in zip(hits, routes)
    ]
    chosen = jnp.concatenate(
        [jnp.sum(jnp.where(hit, 1.0, 0.0), axis=0, keepdims=True) for hit in hits], axis=0
    )
    earlier = lax.broadcasted_iota(jnp.int32, (tokens, tokens), 0) < lax.broadcasted_iota(
        jnp.int32, (tokens, tokens), 1
    )
    slots = dot(chosen.astype(BF16), earlier.astype(F32).astype(BF16))
    slots = jnp.where(chosen > 0.0, slots, -1.0).astype(jnp.int32)
    row = lax.broadcasted_iota(jnp.int32, (rows, tokens), 0)
    return [(scal[k], weights[k], row == slots[k : k + 1]) for k in range(n)]


def span_of(position, rows):
    return pl.ds(pl.multiple_of(position * rows, rows), rows)


def weight_copies(expert, weights, held, sems):
    halves = []
    for h in range(STREAMS):
        copies = []
        for k, (source, target) in enumerate(zip(weights, held)):
            size = target.shape[0 if k == 2 else 1] // STREAMS
            span = pl.ds(h * size, size)
            src, dst = (
                (source.at[expert, span, :], target.at[span, :])
                if k == 2
                else (source.at[expert, :, span], target.at[:, span])
            )
            copies.append(pltpu.make_async_copy(src, dst, sems.at[h, k]))
        halves.append(copies)
    return halves


def route_blocks(choose, count, width):
    wide = max(1, width // count)
    return [(16 * (b // wide), count * (b % wide)) for b in range(4 * choose // 16)]


def pack_kernel(ids, combine, tokens, grads, pack):
    count, width = tokens.shape
    choose = ids.shape[0]
    pack[0:count, :] = tokens[...]
    pack[count : 2 * count, :] = grads[...]
    lines = [ids[...].astype(F32)] + [part.astype(F32) for part in thirds(combine[...])]
    lines = jnp.concatenate(lines, axis=0).astype(BF16)
    blocks = route_blocks(choose, count, width)
    pack[2 * count :, :] = jnp.zeros((pack.shape[0] - 2 * count, width), BF16)
    for b, (row, lane) in enumerate(blocks):
        pack[2 * count + row : 2 * count + row + 16, lane : lane + count] = lines[16 * b : 16 * b + 16]


def unpack_route(pack, choose, count):
    lines = [
        pack[2 * count + row : 2 * count + row + 16, lane : lane + count]
        for row, lane in route_blocks(choose, count, pack.shape[1])
    ]
    lines = jnp.concatenate(lines, axis=0).astype(F32)
    ids, high, middle, low = (lines[k * choose : (k + 1) * choose] for k in range(4))
    return jnp.concatenate([ids, (high + middle) + low], axis=0)


def pre_kernel(n, expert, choose, handed, deps, scal, *refs):
    refs = refs[deps:]
    packs, weights, (in_ref, cot_ref, *refs) = refs[:n], refs[n : n + 3], refs[n + 3 :]
    outs, (token, routes, *refs) = refs[: STREAMS * n], refs[STREAMS * n :]
    gw, uw, dw, *sems = weights if handed else refs
    rows, tile, count = in_ref.shape[0] // n, gw.shape[1] // STREAMS, routes.shape[2]
    copies = [] if handed else weight_copies(expert, weights, (gw, uw, dw), sems[0])
    for group in copies:
        for copy in group:
            copy.start()
    token[...] = jnp.zeros_like(token)
    found = [unpack_route(pack, choose, count) for pack in packs]
    for k in range(n):
        routes[k] = found[k]
    for k, (position, weight, hit) in enumerate(routing(scal, found, expert, rows)):
        pick = hit.astype(F32).astype(BF16)
        span = span_of(position, rows)
        in_ref[span, :] = dot(pick, packs[k][0:count, :]).astype(BF16)
        scale = jnp.sum(jnp.where(hit, weight, 0.0), axis=1, keepdims=True)
        cot_ref[span, :] = (dot(pick, packs[k][count : 2 * count, :]) * scale).astype(BF16)
    for h in range(STREAMS):
        for copy in copies[h] if copies else []:
            copy.wait()
        part = slice(h * tile, (h + 1) * tile)
        gate = dot(in_ref[...], gw[:, part]).astype(BF16)
        up = dot(in_ref[...], uw[:, part]).astype(BF16)
        back = dot(cot_ref[...], dw[part, :], ((1,), (1,))).astype(BF16)
        for p in range(n):
            for k, value in enumerate((gate, up, back)):
                outs[h * n + p][pl.ds(k * rows, rows), :] = value[p * rows : (p + 1) * rows]


def thirds(value):
    high = value.astype(BF16)
    rest = value - high.astype(F32)
    middle = rest.astype(BF16)
    return high, middle, (rest - middle.astype(F32)).astype(BF16)


def mid_kernel(deps, others, *refs):
    own, right, left, *rest = refs[deps:]
    earlier, (out, product) = rest[:others], rest[others:]
    rows, tile = own.shape[0] // 3, own.shape[1]
    total = own[...].astype(F32) + right[...].astype(F32) + left[...].astype(F32)
    gate, up, back = (total[k * rows : (k + 1) * rows] for k in range(3))
    sig = jax.nn.sigmoid(gate)
    hidden = (gate * sig * up).astype(BF16)
    delta = back.astype(BF16).astype(F32)
    out[0:rows, :] = hidden
    out[rows : 2 * rows, :] = (delta * up * sig * (1.0 + gate * (1.0 - sig))).astype(BF16)
    out[2 * rows : 3 * rows, :] = (delta * (gate * sig)).astype(BF16)
    prod = hidden.astype(F32) * back
    lanes = product.shape[1]
    acc = prod[:, 0:lanes]
    for k in range(1, tile // lanes):
        acc = acc + prod[:, k * lanes : (k + 1) * lanes]
    product[...] = acc
    if others:
        partial = [ref[...] for ref in earlier] + [acc]
        ones, fill = jnp.ones((8, lanes), BF16), jnp.zeros((lanes - rows, lanes), F32)
        lines = []
        for e in range(len(partial) // STREAMS):
            wide = jnp.concatenate([sum(partial[STREAMS * e : STREAMS * (e + 1)]), fill], axis=0)
            total = sum(dot(ones, part, ((1,), (1,))) for part in thirds(wide))[0:1]
            lines += [part.astype(F32) for part in thirds(total)]
        extra = out.shape[0] - 3 * rows
        lines.append(jnp.zeros((extra - len(lines), lanes), F32))
        out[3 * rows :, :] = jnp.zeros((extra, tile), BF16)
        out[3 * rows :, 0:lanes] = jnp.concatenate(lines, axis=0).astype(BF16)


def add_kernel(deps, *refs):
    a, b, out = refs[deps:]
    out[...] = (a[...].astype(F32) + b[...].astype(F32)).astype(out.dtype)


def part_of(scal, n, q, group, start, size):
    span = pl.ds(start, size)
    if len(group) == 1:
        return group[0][span, :]
    return jnp.where(scal[n + q] > 0, group[0][span, :], group[1][span, :])


def load_rows(scal, n, which, pieces):
    rows = pieces[0][0].shape[0] // 48 * 16
    return jnp.concatenate(
        [part_of(scal, n, q, group, which * rows, rows) for q, group in enumerate(pieces)], axis=0
    )


def split_pieces(refs, sizes):
    halves, at = [], 0
    for _ in range(STREAMS):
        pieces = [refs[at : at + 1]]
        at += 1
        for size in sizes:
            pieces.append(refs[at : at + size])
            at += size
        halves.append(pieces)
    return halves, refs[at:]


def out_kernel(n, expert, local, fetch, sizes, deps, scal, *refs):
    has_prev, last = expert > 0, expert == local - 1
    refs = refs[deps:]
    routes, refs = [refs[0].at[k] for k in range(n)], refs[1:]
    if has_prev:
        prev, refs = refs[:2], refs[2:]
    halves, refs = split_pieces(refs, sizes)
    (gw, uw, dw), refs = refs[:3], refs[3:]
    copies = []
    if fetch:
        sources, (near, far, token, *held), refs = refs[:3], refs[3:9], refs[9:]
        copies = weight_copies(expert + 2, sources, held, refs[0])
    else:
        (near, far, token), refs = refs[:3], refs[3:]
    eo_ref, idl_ref = refs[-2:]
    for group in copies:
        for copy in group:
            copy.start()
    token[...] = jnp.zeros_like(token)
    spots = routing(scal, routes, expert, halves[0][0][0].shape[0] // 48 * 16)
    if last:
        send_products(scal, routes, local, halves[-1], refs[0], near, far)
    tile = gw.shape[1] // STREAMS
    eo, idl = 0.0, 0.0
    for h in range(STREAMS):
        part = slice(h * tile, (h + 1) * tile)
        eo = eo + dot(load_rows(scal, n, 0, halves[h]), dw[part, :])
        idl = idl + dot(load_rows(scal, n, 1, halves[h]), gw[:, part], ((1,), (1,)))
        idl = idl + dot(load_rows(scal, n, 2, halves[h]), uw[:, part], ((1,), (1,)))
    rows, count = eo.shape[0] // n, routes[0].shape[1]
    eo_ref[...], idl_ref[...] = eo.astype(BF16), idl.astype(BF16)
    for k, (position, weight, hit) in enumerate(spots):
        pick = hit.astype(F32)
        scaled = (pick * weight).astype(BF16)
        span = span_of(position, rows)
        layer = dot(scaled, eo_ref[span, :], ((0,), (0,)))
        back = dot(pick.astype(BF16), idl_ref[span, :], ((0,), (0,)))
        which, place = (near, k) if k < n // 2 else (far, k - n // 2)
        if has_prev:
            before = prev[0 if k < n // 2 else 1]
            layer, back = layer + before[place, 0:count], back + before[place, count : 2 * count]
        which[place, 0:count] = layer.astype(which.dtype)
        which[place, count : 2 * count] = back.astype(which.dtype)
    for group in copies:
        for copy in group:
            copy.wait()


def grad_kernel(n, has_prev, sizes, deps, scal, in_ref, cot_ref, *refs):
    refs = refs[deps:]
    halves, refs = split_pieces(refs, sizes)
    if has_prev:
        refs = refs[3:]
    gg, ug, dg, token = refs
    step = pl.program_id(0)
    token[...] = jnp.zeros_like(token)
    for h in range(STREAMS):

        @pl.when(step == h)
        def _():
            deltas = [load_rows(scal, n, k, halves[h]) for k in (1, 2)]
            both = dot(in_ref[...], jnp.concatenate(deltas, axis=1), ((0,), (0,))).astype(BF16)
            gg[0], ug[0] = both[:, : gg.shape[2]], both[:, gg.shape[2] :]
            dg[0] = dot(load_rows(scal, n, 0, halves[h]), cot_ref[...], ((0,), (0,))).astype(BF16)


def product_rows(peers, extra, count, width):
    wide = width // count
    return [(extra * (p // wide), count * (p % wide)) for p in range(peers)], extra * -(-peers // wide)


def send_products(scal, routes, local, pieces, held, near, far):
    n, (_, extra, lanes) = len(routes), held.shape
    first = pieces[0][0].shape[0] - extra
    for q, group in enumerate(pieces):
        held[q] = part_of(scal, n, q, group, first, extra)[:, 0:lanes]
    tokens = routes[0].shape[1]
    line = lax.broadcasted_iota(jnp.int32, (extra, tokens), 0)
    blocks = [jnp.zeros((extra, tokens), F32) for _ in range(n)]
    for e in range(local):
        for k, (position, _, hit) in enumerate(routing(scal, routes, e, lanes)):
            found = dot(held[position], hit.astype(F32).astype(BF16))
            blocks[k] = jnp.where((line >= 3 * e) & (line < 3 * e + 3), found, blocks[k])
    spots, _ = product_rows(n, extra, tokens, near.shape[2])
    for k in range(n):
        which, place = (near, k) if k < n // 2 else (far, k - n // 2)
        for p, (row, lane) in enumerate(spots):
            value = jnp.where(scal[2 * n] == p * local, blocks[k], 0.0).astype(BF16)
            start = 2 * tokens + row
            which[place, start : start + extra, lane : lane + tokens] = value


def in_hbm(array):
    return pltpu.with_memory_space_constraint(array, pltpu.HBM)


def whole_spec(shape):
    return pl.BlockSpec(tuple(shape), lambda g: (0,) * len(shape))


def spec_of(array):
    return whole_spec(array.shape)


def like(shape, dtype=BF16):
    return jax.ShapeDtypeStruct(tuple(shape), dtype)


SMEM_SPEC = pl.BlockSpec(memory_space=pltpu.SMEM)
ANY_SPEC = pl.BlockSpec(memory_space=pl.ANY)
HBM_SPEC = pl.BlockSpec(memory_space=pltpu.HBM)
TOKEN = (8, 128)


def call(kernel, grid, in_specs, out_specs, out_shape, flops, moved, **rest):
    return pl.pallas_call(
        kernel,
        grid=(grid,),
        in_specs=in_specs,
        out_specs=out_specs,
        out_shape=out_shape,
        compiler_params=pltpu.CompilerParams(vmem_limit_bytes=VMEM_BYTES),
        cost_estimate=pl.CostEstimate(flops=flops, bytes_accessed=moved, transcendentals=0),
        **rest,
    )


def body(tokens, expert_ids, combine, gate_weight, up_weight, down_weight, out_grad):
    peers, n = lax.axis_size("expert"), lax.axis_size("dp")
    assert peers == n
    chips = peers // 2
    local, width, hidden = gate_weight.shape
    count, choose = expert_ids.shape
    experts_all = peers * local
    capacity = count * choose * 5 // (4 * experts_all)
    rows = -(-capacity // 16) * 16
    all_rows = n * rows
    tile = hidden // STREAMS
    swaps = n == 4

    me, here = lax.axis_index("expert"), lax.axis_index("dp")
    at_end = (here == 0) | (here == n - 1)
    table = []
    for place in range(n):
        block = 2 * lax.rem(me // 2 - place % chips + chips, chips) + lax.rem(
            lax.rem(me, 2) + place // chips, 2
        )
        if swaps:
            across_middle = jnp.where((block == 0) | (block == 3), 3, 2)
            position = jnp.where(
                block == here, 0, jnp.where(block // 2 == here // 2, 1, across_middle)
            )
        else:
            position = lax.rem(here - block + n, n)
        table.append(position)
    flags = [at_end if swaps else here >= q for q in range(n)]
    scal = jnp.stack(
        [jnp.asarray(v).astype(jnp.int32) for v in table + flags + [me * local, at_end]]
    )

    ids_t, combine_t = expert_ids.T, combine.T
    named = ids_t[:, None, :] == jnp.arange(experts_all, dtype=jnp.int32)[None, :, None]

    along_x, across = Line("expert", chips, 2), Line("expert", peers, 1)
    swap = [(2 * x + c, 2 * x + 1 - c) for x in range(chips) for c in range(2)]

    def gather_blocks(own):
        found = [own] + [
            right if right is left else jnp.where(me // 2 >= q, right, left)
            for q, (right, left) in enumerate(along_x.gather(own), 1)
        ]
        return found + [across.send(piece, swap) for piece in found]

    route_rows = 16 + max(row for row, _ in route_blocks(choose, count, width))
    pack_shape = (2 * count + route_rows, width)
    pack = call(
        pack_kernel,
        1,
        [spec_of(ids_t), spec_of(combine_t), spec_of(tokens), spec_of(out_grad)],
        whole_spec(pack_shape),
        like(pack_shape),
        count * width,
        8 * count * width,
    )(*(in_hbm(x) for x in (ids_t, combine_t, tokens, out_grad)))
    packs = gather_blocks(pack)
    route_shape = (n, 2 * choose, count)

    mac = all_rows * width * hidden
    weight_bytes = 2 * width * hidden
    piece_shape = (3 * rows, tile)
    extra = -(-3 * local // 16) * 16
    wide_shape = (3 * rows + extra, tile)
    spots, below = product_rows(peers, extra, count, width)
    piece_bytes = 2 * 3 * rows * tile
    slot_shape = (all_rows, width)

    weights = [in_hbm(w) for w in (gate_weight, up_weight, down_weight)]
    def grad_specs(e):
        wide = pl.BlockSpec((1, width, tile), lambda g: (e, 0, g))
        return [wide, wide, pl.BlockSpec((1, tile, width), lambda g: (e, g, 0))]

    own_weights = {}

    def pre(e, deps):
        handed = e in own_weights
        weight_shapes = [w.shape[1:] for w in weights]
        inputs, cot, *parts = call(
            functools.partial(pre_kernel, n, e, choose, handed, len(deps)),
            1,
            [SMEM_SPEC]
            + [ANY_SPEC] * len(deps)
            + [spec_of(x) for x in packs]
            + ([whole_spec(shape) for shape in weight_shapes] if handed else [HBM_SPEC] * 3),
            [whole_spec(slot_shape)] * 2
            + [whole_spec(piece_shape)] * (STREAMS * n)
            + [whole_spec(TOKEN), whole_spec(route_shape)]
            + ([] if handed else [whole_spec(shape) for shape in weight_shapes]),
            [like(slot_shape)] * 2
            + [like(piece_shape)] * (STREAMS * n)
            + [like(TOKEN, F32), like(route_shape, F32)]
            + ([] if handed else [like(shape) for shape in weight_shapes]),
            6 * mac,
            3 * weight_bytes + STREAMS * n * piece_bytes,
            scratch_shapes=[] if handed else [pltpu.SemaphoreType.DMA((STREAMS, 3))],
        )(scal, *deps, *packs, *(own_weights[e] if handed else weights))
        parts, (token, found, *held) = parts[: STREAMS * n], parts[STREAMS * n :]
        if not handed:
            own_weights[e] = held
        return (inputs, cot), [parts[h * n : (h + 1) * n] for h in range(STREAMS)], token, found

    def mid(e, h, totals, products, deps=()):
        others = products if e == local - 1 and h == STREAMS - 1 else []
        shape = wide_shape if others else piece_shape
        return call(
            functools.partial(mid_kernel, len(deps), len(others)),
            1,
            [ANY_SPEC] * len(deps)
            + [whole_spec(piece_shape)] * 3
            + [whole_spec((rows, 128))] * len(others),
            [whole_spec(shape), whole_spec((rows, 128))],
            [like(shape), like((rows, 128), F32)],
            20 * rows * tile,
            4 * piece_bytes,
        )(*deps, *totals, *others)

    def add(a, b, deps):
        return call(
            functools.partial(add_kernel, len(deps)),
            1,
            [ANY_SPEC] * len(deps) + [spec_of(a)] * 2,
            spec_of(a),
            like(a.shape, a.dtype),
            a.size,
            3 * a.size * a.dtype.itemsize,
        )(*deps, a, b)

    def flatten(halves):
        return [x for pieces in halves for group in pieces for x in group]

    def sizes_of(pieces):
        return [len(group) for group in pieces[1:]]

    def out(e, halves, prev, deps):
        flat = flatten(halves)
        last, fetch = e == local - 1, swaps and e + 2 < local
        sum_shape = (chips, 2 * count, width)
        out_shape = (chips, 2 * count + below, width) if last else sum_shape
        weight_specs = [whole_spec(w.shape[1:]) for w in weights]
        near, far, token, *held = call(
            functools.partial(out_kernel, n, e, local, fetch, sizes_of(halves[0]), len(deps)),
            1,
            [SMEM_SPEC]
            + [ANY_SPEC] * len(deps)
            + [whole_spec(route_shape)]
            + ([whole_spec(sum_shape)] * 2 if e > 0 else [])
            + [spec_of(x) for x in flat]
            + weight_specs
            + ([HBM_SPEC] * 3 if fetch else []),
            [whole_spec(out_shape)] * 2 + [whole_spec(TOKEN)] + (weight_specs if fetch else []),
            [like(out_shape, BF16 if last else F32)] * 2
            + [like(TOKEN, F32)]
            + ([like(w.shape[1:]) for w in weights] if fetch else []),
            6 * mac,
            3 * weight_bytes + len(flat) * piece_bytes,
            scratch_shapes=([pltpu.SemaphoreType.DMA((STREAMS, 3))] if fetch else [])
            + ([pltpu.VMEM((n, extra, 128), BF16)] if last else [])
            + [pltpu.VMEM(slot_shape, BF16)] * 2,
        )(
            scal,
            *deps,
            routes,
            *prev,
            *flat,
            *own_weights[e],
            *(weights if fetch else []),
        )
        if fetch:
            own_weights[e + 2] = held
        return near, far, token

    def grad(e, slots, halves, prev, deps):
        flat = flatten(halves)
        base = 3 + len(deps) + len(flat)
        return call(
            functools.partial(grad_kernel, n, e > 0, sizes_of(halves[0]), len(deps)),
            STREAMS,
            [SMEM_SPEC]
            + [whole_spec(slot_shape)] * 2
            + [ANY_SPEC] * len(deps)
            + [spec_of(x) for x in flat]
            + ([ANY_SPEC] * 3 if e > 0 else []),
            grad_specs(e) + [whole_spec(TOKEN)],
            [like(w.shape) for w in weights] + [like(TOKEN, F32)],
            6 * mac,
            3 * weight_bytes + len(flat) * piece_bytes,
            input_output_aliases={base + k: k for k in range(3)} if e > 0 else {},
        )(scal, *slots, *deps, *flat, *prev)

    along_z = Line("dp", n, 1)

    def outer(value):
        return along_z.send(value, [(0, 1), (1, 0), (2, 3), (3, 2)])

    def inner(value):
        pairs = []
        for p in range(peers):
            pairs += [(p * n + 1, p * n + 2), (p * n + 2, p * n + 1)]
            pairs += [(p * n + end, (p ^ 1) * n + end) for end in (0, n - 1)]
        return lax.ppermute(value, ("expert", "dp"), pairs)

    def unless_end(value):
        return jnp.where(at_end, jnp.zeros_like(value), value)

    products, sums, grads = [], [], []

    def send_home(near, far, add):
        near = add(near, across.send(far, swap))
        right, left = along_x.scatter([near[q] for q in range(chips)], add)
        home = near[0].astype(F32) + right.astype(F32)
        return near, home if left is None else home + left.astype(F32)

    if swaps:
        flight, arrived, streams = [None] * STREAMS, None, range(STREAMS)
        slots, parts, _, routes = pre(0, [])
        grad_token = None
        for e in range(local):
            following = e < local - 1
            first, second, totals, halves = [], [], [], []
            for h in streams:
                x = parts[h]
                if e == 0:
                    first.append((outer(x[3]), None))
                else:
                    y, got_a, got_b = flight[h]
                    first.append((outer(jnp.where(at_end, x[3], got_b)), inner(got_a)))
            seen = [[] for _ in streams]
            if following:
                next_slots, next_parts, token, _ = pre(e + 1, [] if e == 0 else [flight[1][2]])
                seen[0 if e == 0 else STREAMS - 1].append(token)
            if grad_token is not None:
                seen[0].append(grad_token)
            for h in streams:
                x, (a1, b1) = parts[h], first[h]
                send_a2 = x[2] if e == 0 else jnp.where(at_end, x[2], b1)
                second.append((outer(send_a2), inner(add(x[3], a1, seen[h]))))
                if e > 0:
                    y, got_a, got_b = flight[h]
                    halves.append([(y,), (got_a,), (a1, got_b), (second[h][0], b1)])
            for h in streams:
                x, (a2, b2) = parts[h], second[h]
                a3 = outer(jnp.where(at_end, x[1], add_rounded(x[1], b2)))
                b3 = inner(unless_end(add_rounded(x[2], a2)))
                totals.append((x[0], a3, b3))
            wait = []
            if e > 0:
                *sums, out_token = out(e - 1, halves, sums, [])
                wait = [out_token]
            for h in streams:
                y, product = mid(e, h, totals[h], products, wait if h == 0 else [])
                products.append(product)
                flight[h] = (y, outer(y), inner(y))
            if e > 0:
                *grads, grad_token = grad(e - 1, arrived, halves, grads, [flight[-1][0]])
            arrived = slots
            if following:
                slots, parts = next_slots, next_parts
        halves = []
        for h in streams:
            y, got_a, got_b = flight[h]
            a1, b1 = outer(got_b), inner(got_a)
            a2 = outer(b1)
            halves.append([(y,), (got_a,), (a1, got_b), (a2, b1)])
        wait = [grad_token]
    else:
        begun = []
        for e in range(local):
            slots, parts, _, routes = pre(e, [])
            begun.append((slots, [(x[0], *along_z.scatter(x, add_rounded)) for x in parts]))
        for e in range(local):
            halves, arrived, wait = [], begun[e][0], []
            for h in range(STREAMS):
                y, product = mid(e, h, begun[e][1][h], products)
                products.append(product)
                halves.append([(y,)] + along_z.gather(y))
            if e < local - 1:
                *sums, _ = out(e, halves, sums, [])
                *grads, _ = grad(e, arrived, halves, grads, [])

    near, far, _ = out(local - 1, halves, sums, wait)
    hop, home = send_home(near, far, add_rounded)
    *grads, _ = grad(local - 1, arrived, halves, grads, [hop])
    per_expert = jnp.concatenate(
        [
            home[2 * count + row : 2 * count + row + 3 * local, lane : lane + count]
            .reshape(local, 3, count)
            .sum(axis=1)
            for row, lane in spots
        ]
    )
    combine_grad = jnp.sum(jnp.where(named, per_expert[None], 0.0), axis=1) / combine_t
    layer_out, token_grad = home[:count].astype(BF16), home[count : 2 * count].astype(BF16)
    return (layer_out, token_grad, *grads, combine_grad.T)


def solution(mesh):
    return jax.shard_map(
        body,
        mesh=mesh,
        in_specs=(
            P(("group", "expert"), "dp"),
            P(("group", "expert"), None),
            P(("group", "expert"), None),
            P("expert", "dp", None),
            P("expert", "dp", None),
            P("expert", None, "dp"),
            P(("group", "expert"), "dp"),
        ),
        out_specs=(
            P(("group", "expert"), "dp"),
            P(("group", "expert"), "dp"),
            P(("group", "expert"), "dp", None),
            P(("group", "expert"), "dp", None),
            P(("group", "expert"), None, "dp"),
            P(("group", "expert"), None),
        ),
        check_vma=False,
    )
```

```python
import functools

import jax
import jax.numpy as jnp
from jax import lax
from jax.experimental import pallas as pl
from jax.experimental.pallas import tpu as pltpu
from jax.sharding import PartitionSpec as P

F32, BF16 = jnp.float32, jnp.bfloat16
VMEM_BYTES = 20 << 20
STREAMS = 2


def line_pairs(n, gather, step):
    if gather:
        senders = [i for i in range(step - 1, n - 1)]
    else:
        senders = [i for i in range(0, min(step, n - 1))]
    right = [(i, i + 1) for i in senders]
    left = [(n - 1 - i, n - 2 - i) for i in senders]
    return right, left


class Line:
    def __init__(self, axis, n, stride):
        self.axis, self.n, self.stride = axis, n, stride

    def send(self, value, pairs):
        wide = [
            (a * self.stride + c, b * self.stride + c) for a, b in pairs for c in range(self.stride)
        ]
        return lax.ppermute(value, self.axis, wide)

    def gather(self, own):
        n = self.n
        if n == 2:
            both = self.send(own, [(0, 1), (1, 0)])
            return [(both, both)]
        right, left, rights, lefts = own, own, [], []
        for step in range(1, n):
            pairs_r, pairs_l = line_pairs(n, True, step)
            right, left = self.send(right, pairs_r), self.send(left, pairs_l)
            rights.append(right)
            lefts.append(left)
        return [(rights[q - 1], lefts[n - q - 1]) for q in range(1, n)]

    def scatter(self, parts, add):
        n = self.n
        if n == 2:
            return self.send(parts[1], [(0, 1), (1, 0)]), None
        right, left = parts[1], parts[n - 1]
        for step in range(1, n):
            pairs_r, pairs_l = line_pairs(n, False, step)
            right, left = self.send(right, pairs_r), self.send(left, pairs_l)
            if step < n - 1:
                right, left = add(parts[step + 1], right), add(parts[n - 1 - step], left)
        return right, left


def add_rounded(a, b):
    return (a.astype(F32) + b.astype(F32)).astype(BF16)


def dot(a, b, dims=((1,), (0,))):
    return lax.dot_general(a, b, (dims, ((), ())), preferred_element_type=F32)


def routing(scal, routes, expert, rows):
    n = len(routes)
    choose, tokens = routes[0].shape[0] // 2, routes[0].shape[1]
    which = (scal[2 * n] + expert).astype(F32)
    routes = [route[...] for route in routes]
    hits = [route[0:choose] == which for route in routes]
    weights = [
        jnp.sum(jnp.where(hit, route[choose:], 0.0), axis=0, keepdims=True)
        for hit, route in zip(hits, routes)
    ]
    chosen = jnp.concatenate(
        [jnp.sum(jnp.where(hit, 1.0, 0.0), axis=0, keepdims=True) for hit in hits], axis=0
    )
    earlier = lax.broadcasted_iota(jnp.int32, (tokens, tokens), 0) < lax.broadcasted_iota(
        jnp.int32, (tokens, tokens), 1
    )
    slots = dot(chosen.astype(BF16), earlier.astype(F32).astype(BF16))
    slots = jnp.where(chosen > 0.0, slots, -1.0).astype(jnp.int32)
    row = lax.broadcasted_iota(jnp.int32, (rows, tokens), 0)
    return [(scal[k], weights[k], row == slots[k : k + 1]) for k in range(n)]


def span_of(position, rows):
    return pl.ds(pl.multiple_of(position * rows, rows), rows)


def weight_copies(expert, weights, held, sems):
    halves = []
    for h in range(STREAMS):
        copies = []
        for k, (source, target) in enumerate(zip(weights, held)):
            size = target.shape[0 if k == 2 else 1] // STREAMS
            span = pl.ds(h * size, size)
            src, dst = (
                (source.at[expert, span, :], target.at[span, :])
                if k == 2
                else (source.at[expert, :, span], target.at[:, span])
            )
            copies.append(pltpu.make_async_copy(src, dst, sems.at[h, k]))
        halves.append(copies)
    return halves


def route_blocks(choose, count, width):
    wide = max(1, width // count)
    return [(16 * (b // wide), count * (b % wide)) for b in range(4 * choose // 16)]


def pack_kernel(ids, combine, tokens, grads, pack):
    count, width = tokens.shape
    choose = ids.shape[0]
    pack[0:count, :] = tokens[...]
    pack[count : 2 * count, :] = grads[...]
    lines = [ids[...].astype(F32)] + [part.astype(F32) for part in thirds(combine[...])]
    lines = jnp.concatenate(lines, axis=0).astype(BF16)
    blocks = route_blocks(choose, count, width)
    pack[2 * count :, :] = jnp.zeros((pack.shape[0] - 2 * count, width), BF16)
    for b, (row, lane) in enumerate(blocks):
        pack[2 * count + row : 2 * count + row + 16, lane : lane + count] = lines[16 * b : 16 * b + 16]


def unpack_route(pack, choose, count):
    lines = [
        pack[2 * count + row : 2 * count + row + 16, lane : lane + count]
        for row, lane in route_blocks(choose, count, pack.shape[1])
    ]
    lines = jnp.concatenate(lines, axis=0).astype(F32)
    ids, high, middle, low = (lines[k * choose : (k + 1) * choose] for k in range(4))
    return jnp.concatenate([ids, (high + middle) + low], axis=0)


def pre_kernel(n, expert, choose, deps, scal, *refs):
    refs = refs[deps:]
    packs, weights, (in_ref, cot_ref, *refs) = refs[:n], refs[n : n + 3], refs[n + 3 :]
    outs, (token, routes, gw, uw, dw, sems) = refs[: STREAMS * n], refs[STREAMS * n :]
    rows, tile, count = in_ref.shape[0] // n, gw.shape[1] // STREAMS, routes.shape[2]
    copies = weight_copies(expert, weights, (gw, uw, dw), sems)
    for group in copies:
        for copy in group:
            copy.start()
    token[...] = jnp.zeros_like(token)
    found = [unpack_route(pack, choose, count) for pack in packs]
    for k in range(n):
        routes[k] = found[k]
    for k, (position, weight, hit) in enumerate(routing(scal, found, expert, rows)):
        pick = hit.astype(F32).astype(BF16)
        span = span_of(position, rows)
        in_ref[span, :] = dot(pick, packs[k][0:count, :]).astype(BF16)
        scale = jnp.sum(jnp.where(hit, weight, 0.0), axis=1, keepdims=True)
        cot_ref[span, :] = (dot(pick, packs[k][count : 2 * count, :]) * scale).astype(BF16)
    for h in range(STREAMS):
        for copy in copies[h]:
            copy.wait()
        part = slice(h * tile, (h + 1) * tile)
        gate = dot(in_ref[...], gw[:, part]).astype(BF16)
        up = dot(in_ref[...], uw[:, part]).astype(BF16)
        back = dot(cot_ref[...], dw[part, :], ((1,), (1,))).astype(BF16)
        for p in range(n):
            for k, value in enumerate((gate, up, back)):
                outs[h * n + p][pl.ds(k * rows, rows), :] = value[p * rows : (p + 1) * rows]


def thirds(value):
    high = value.astype(BF16)
    rest = value - high.astype(F32)
    middle = rest.astype(BF16)
    return high, middle, (rest - middle.astype(F32)).astype(BF16)


def mid_kernel(deps, others, *refs):
    own, right, left, *rest = refs[deps:]
    earlier, (out, product) = rest[:others], rest[others:]
    rows, tile = own.shape[0] // 3, own.shape[1]
    total = own[...].astype(F32) + right[...].astype(F32) + left[...].astype(F32)
    gate, up, back = (total[k * rows : (k + 1) * rows] for k in range(3))
    sig = jax.nn.sigmoid(gate)
    hidden = (gate * sig * up).astype(BF16)
    delta = back.astype(BF16).astype(F32)
    out[0:rows, :] = hidden
    out[rows : 2 * rows, :] = (delta * up * sig * (1.0 + gate * (1.0 - sig))).astype(BF16)
    out[2 * rows : 3 * rows, :] = (delta * (gate * sig)).astype(BF16)
    prod = hidden.astype(F32) * back
    lanes = product.shape[1]
    acc = prod[:, 0:lanes]
    for k in range(1, tile // lanes):
        acc = acc + prod[:, k * lanes : (k + 1) * lanes]
    product[...] = acc
    if others:
        partial = [ref[...] for ref in earlier] + [acc]
        ones, fill = jnp.ones((8, lanes), BF16), jnp.zeros((lanes - rows, lanes), F32)
        lines = []
        for e in range(len(partial) // STREAMS):
            wide = jnp.concatenate([sum(partial[STREAMS * e : STREAMS * (e + 1)]), fill], axis=0)
            total = sum(dot(ones, part, ((1,), (1,))) for part in thirds(wide))[0:1]
            lines += [part.astype(F32) for part in thirds(total)]
        extra = out.shape[0] - 3 * rows
        lines.append(jnp.zeros((extra - len(lines), lanes), F32))
        out[3 * rows :, :] = jnp.zeros((extra, tile), BF16)
        out[3 * rows :, 0:lanes] = jnp.concatenate(lines, axis=0).astype(BF16)


def add_kernel(deps, *refs):
    a, b, out = refs[deps:]
    out[...] = (a[...].astype(F32) + b[...].astype(F32)).astype(out.dtype)


def part_of(scal, n, q, group, start, size):
    span = pl.ds(start, size)
    if len(group) == 1:
        return group[0][span, :]
    return jnp.where(scal[n + q] > 0, group[0][span, :], group[1][span, :])


def load_rows(scal, n, which, pieces):
    rows = pieces[0][0].shape[0] // 48 * 16
    return jnp.concatenate(
        [part_of(scal, n, q, group, which * rows, rows) for q, group in enumerate(pieces)], axis=0
    )


def split_pieces(refs, sizes):
    halves, at = [], 0
    for _ in range(STREAMS):
        pieces = [refs[at : at + 1]]
        at += 1
        for size in sizes:
            pieces.append(refs[at : at + size])
            at += size
        halves.append(pieces)
    return halves, refs[at:]


def out_kernel(n, expert, has_prev, last, sizes, deps, scal, *refs):
    refs = refs[deps:]
    routes, refs = [refs[0].at[k] for k in range(n)], refs[1:]
    if has_prev:
        prev, refs = refs[:2], refs[2:]
    halves, refs = split_pieces(refs, sizes)
    (gw, uw, dw), (near, far, token, *refs) = refs[:3], refs[3:]
    if last:
        near_p, far_p, *refs, held = refs
    eo_ref, idl_ref = refs
    token[...] = jnp.zeros_like(token)
    spots = routing(scal, routes, expert, halves[0][0][0].shape[0] // 48 * 16)
    if last:
        send_products(scal, routes, expert + 1, halves[-1], held, near_p, far_p)
    tile = gw.shape[1] // STREAMS
    eo, idl = 0.0, 0.0
    for h in range(STREAMS):
        part = slice(h * tile, (h + 1) * tile)
        eo = eo + dot(load_rows(scal, n, 0, halves[h]), dw[part, :])
        idl = idl + dot(load_rows(scal, n, 1, halves[h]), gw[:, part], ((1,), (1,)))
        idl = idl + dot(load_rows(scal, n, 2, halves[h]), uw[:, part], ((1,), (1,)))
    rows = eo.shape[0] // n
    eo_ref[...], idl_ref[...] = eo.astype(BF16), idl.astype(BF16)
    for k, (position, weight, hit) in enumerate(spots):
        pick = hit.astype(F32)
        scaled = (pick * weight).astype(BF16)
        span = span_of(position, rows)
        layer = dot(scaled, eo_ref[span, :], ((0,), (0,)))
        back = dot(pick.astype(BF16), idl_ref[span, :], ((0,), (0,)))
        which, place = (near, k) if k < n // 2 else (far, k - n // 2)
        if has_prev:
            before = prev[0 if k < n // 2 else 1]
            layer, back = layer + before[place, 0], back + before[place, 1]
        which[place, 0] = layer.astype(which.dtype)
        which[place, 1] = back.astype(which.dtype)


def grad_kernel(n, has_prev, sizes, deps, scal, in_ref, cot_ref, *refs):
    refs = refs[deps:]
    halves, refs = split_pieces(refs, sizes)
    if has_prev:
        refs = refs[3:]
    gg, ug, dg, token = refs
    step = pl.program_id(0)
    token[...] = jnp.zeros_like(token)
    for h in range(STREAMS):

        @pl.when(step == h)
        def _():
            deltas = [load_rows(scal, n, k, halves[h]) for k in (1, 2)]
            both = dot(in_ref[...], jnp.concatenate(deltas, axis=1), ((0,), (0,))).astype(BF16)
            gg[0], ug[0] = both[:, : gg.shape[2]], both[:, gg.shape[2] :]
            dg[0] = dot(load_rows(scal, n, 0, halves[h]), cot_ref[...], ((0,), (0,))).astype(BF16)


def send_products(scal, routes, local, pieces, held, near, far):
    n, (_, extra, lanes) = len(routes), held.shape
    first = pieces[0][0].shape[0] - extra
    for q, group in enumerate(pieces):
        held[q] = part_of(scal, n, q, group, first, extra)[:, 0:lanes]
    experts_all, tokens = near.shape[1:]
    ids = lax.broadcasted_iota(jnp.int32, (experts_all, tokens), 0)
    sums = [jnp.zeros((experts_all, tokens), F32) for _ in range(n)]
    for e in range(local):
        for k, (position, _, hit) in enumerate(routing(scal, routes, e, lanes)):
            found = dot(held[position], hit.astype(F32).astype(BF16))
            value = found[3 * e : 3 * e + 1] + found[3 * e + 1 : 3 * e + 2] + found[3 * e + 2 : 3 * e + 3]
            sums[k] = sums[k] + jnp.where(ids == scal[2 * n] + e, value, 0.0)
    for k in range(n):
        if k < n // 2:
            near[k] = sums[k]
        else:
            far[k - n // 2] = sums[k]


def in_hbm(array):
    return pltpu.with_memory_space_constraint(array, pltpu.HBM)


def whole_spec(shape):
    return pl.BlockSpec(tuple(shape), lambda g: (0,) * len(shape))


def spec_of(array):
    return whole_spec(array.shape)


def like(shape, dtype=BF16):
    return jax.ShapeDtypeStruct(tuple(shape), dtype)


SMEM_SPEC = pl.BlockSpec(memory_space=pltpu.SMEM)
ANY_SPEC = pl.BlockSpec(memory_space=pl.ANY)
HBM_SPEC = pl.BlockSpec(memory_space=pltpu.HBM)
TOKEN = (8, 128)


def call(kernel, grid, in_specs, out_specs, out_shape, flops, moved, **rest):
    return pl.pallas_call(
        kernel,
        grid=(grid,),
        in_specs=in_specs,
        out_specs=out_specs,
        out_shape=out_shape,
        compiler_params=pltpu.CompilerParams(vmem_limit_bytes=VMEM_BYTES),
        cost_estimate=pl.CostEstimate(flops=flops, bytes_accessed=moved, transcendentals=0),
        **rest,
    )


def body(tokens, expert_ids, combine, gate_weight, up_weight, down_weight, out_grad):
    peers, n = lax.axis_size("expert"), lax.axis_size("dp")
    assert peers == n
    chips = peers // 2
    local, width, hidden = gate_weight.shape
    count, choose = expert_ids.shape
    experts_all = peers * local
    capacity = count * choose * 5 // (4 * experts_all)
    rows = -(-capacity // 16) * 16
    all_rows = n * rows
    tile = hidden // STREAMS
    swaps = n == 4

    me, here = lax.axis_index("expert"), lax.axis_index("dp")
    at_end = (here == 0) | (here == n - 1)
    table = []
    for place in range(n):
        block = 2 * lax.rem(me // 2 - place % chips + chips, chips) + lax.rem(
            lax.rem(me, 2) + place // chips, 2
        )
        if swaps:
            across_middle = jnp.where((block == 0) | (block == 3), 3, 2)
            position = jnp.where(
                block == here, 0, jnp.where(block // 2 == here // 2, 1, across_middle)
            )
        else:
            position = lax.rem(here - block + n, n)
        table.append(position)
    flags = [at_end if swaps else here >= q for q in range(n)]
    scal = jnp.stack(
        [jnp.asarray(v).astype(jnp.int32) for v in table + flags + [me * local, at_end]]
    )

    ids_t, combine_t = expert_ids.T, combine.T
    named = ids_t[:, None, :] == jnp.arange(experts_all, dtype=jnp.int32)[None, :, None]

    along_x, across = Line("expert", chips, 2), Line("expert", peers, 1)
    swap = [(2 * x + c, 2 * x + 1 - c) for x in range(chips) for c in range(2)]

    def gather_blocks(own):
        found = [own] + [
            right if right is left else jnp.where(me // 2 >= q, right, left)
            for q, (right, left) in enumerate(along_x.gather(own), 1)
        ]
        return found + [across.send(piece, swap) for piece in found]

    route_rows = 16 + max(row for row, _ in route_blocks(choose, count, width))
    pack_shape = (2 * count + route_rows, width)
    pack = call(
        pack_kernel,
        1,
        [spec_of(ids_t), spec_of(combine_t), spec_of(tokens), spec_of(out_grad)],
        whole_spec(pack_shape),
        like(pack_shape),
        count * width,
        8 * count * width,
    )(*(in_hbm(x) for x in (ids_t, combine_t, tokens, out_grad)))
    packs = gather_blocks(pack)
    route_shape = (n, 2 * choose, count)

    mac = all_rows * width * hidden
    weight_bytes = 2 * width * hidden
    piece_shape = (3 * rows, tile)
    extra = -(-3 * local // 16) * 16
    wide_shape = (3 * rows + extra, tile)
    piece_bytes = 2 * 3 * rows * tile
    slot_shape = (all_rows, width)

    weights = [in_hbm(w) for w in (gate_weight, up_weight, down_weight)]
    def grad_specs(e):
        wide = pl.BlockSpec((1, width, tile), lambda g: (e, 0, g))
        return [wide, wide, pl.BlockSpec((1, tile, width), lambda g: (e, g, 0))]

    own_weights = []

    def pre(e, deps):
        inputs, cot, *parts, token, found, gw, uw, dw = call(
            functools.partial(pre_kernel, n, e, choose, len(deps)),
            1,
            [SMEM_SPEC] + [ANY_SPEC] * len(deps) + [spec_of(x) for x in packs] + [HBM_SPEC] * 3,
            [whole_spec(slot_shape)] * 2
            + [whole_spec(piece_shape)] * (STREAMS * n)
            + [whole_spec(TOKEN), whole_spec(route_shape)]
            + [whole_spec(w.shape[1:]) for w in weights],
            [like(slot_shape)] * 2
            + [like(piece_shape)] * (STREAMS * n)
            + [like(TOKEN, F32), like(route_shape, F32)]
            + [like(w.shape[1:]) for w in weights],
            6 * mac,
            3 * weight_bytes + STREAMS * n * piece_bytes,
            scratch_shapes=[pltpu.SemaphoreType.DMA((STREAMS, 3))],
        )(scal, *deps, *packs, *weights)
        parts = [parts[h * n : (h + 1) * n] for h in range(STREAMS)]
        own_weights.append((gw, uw, dw))
        return (inputs, cot), parts, token, found

    def mid(e, h, totals, products, deps=()):
        others = products if e == local - 1 and h == STREAMS - 1 else []
        shape = wide_shape if others else piece_shape
        return call(
            functools.partial(mid_kernel, len(deps), len(others)),
            1,
            [ANY_SPEC] * len(deps)
            + [whole_spec(piece_shape)] * 3
            + [whole_spec((rows, 128))] * len(others),
            [whole_spec(shape), whole_spec((rows, 128))],
            [like(shape), like((rows, 128), F32)],
            20 * rows * tile,
            4 * piece_bytes,
        )(*deps, *totals, *others)

    def add(a, b, deps):
        return call(
            functools.partial(add_kernel, len(deps)),
            1,
            [ANY_SPEC] * len(deps) + [spec_of(a)] * 2,
            spec_of(a),
            like(a.shape, a.dtype),
            a.size,
            3 * a.size * a.dtype.itemsize,
        )(*deps, a, b)

    def flatten(halves):
        return [x for pieces in halves for group in pieces for x in group]

    def sizes_of(pieces):
        return [len(group) for group in pieces[1:]]

    def out(e, halves, prev, deps):
        flat = flatten(halves)
        last = e == local - 1
        dense_shape = (chips, experts_all, count)
        sum_shape = (chips, 2, count, width)
        return call(
            functools.partial(out_kernel, n, e, e > 0, last, sizes_of(halves[0]), len(deps)),
            1,
            [SMEM_SPEC]
            + [ANY_SPEC] * len(deps)
            + [whole_spec(route_shape)]
            + ([whole_spec(sum_shape)] * 2 if e > 0 else [])
            + [spec_of(x) for x in flat]
            + [whole_spec(w.shape[1:]) for w in weights],
            [whole_spec(sum_shape)] * 2
            + [whole_spec(TOKEN)]
            + ([whole_spec(dense_shape)] * 2 if last else []),
            [like(sum_shape, BF16 if last else F32)] * 2
            + [like(TOKEN, F32)]
            + ([like(dense_shape, F32)] * 2 if last else []),
            6 * mac,
            3 * weight_bytes + len(flat) * piece_bytes,
            scratch_shapes=[pltpu.VMEM(slot_shape, BF16)] * 2
            + ([pltpu.VMEM((n, extra, 128), BF16)] if last else []),
        )(scal, *deps, routes, *prev, *flat, *own_weights[e])

    def grad(e, slots, halves, prev, deps):
        flat = flatten(halves)
        base = 3 + len(deps) + len(flat)
        return call(
            functools.partial(grad_kernel, n, e > 0, sizes_of(halves[0]), len(deps)),
            STREAMS,
            [SMEM_SPEC]
            + [whole_spec(slot_shape)] * 2
            + [ANY_SPEC] * len(deps)
            + [spec_of(x) for x in flat]
            + ([ANY_SPEC] * 3 if e > 0 else []),
            grad_specs(e) + [whole_spec(TOKEN)],
            [like(w.shape) for w in weights] + [like(TOKEN, F32)],
            6 * mac,
            3 * weight_bytes + len(flat) * piece_bytes,
            input_output_aliases={base + k: k for k in range(3)} if e > 0 else {},
        )(scal, *slots, *deps, *flat, *prev)

    along_z = Line("dp", n, 1)

    def outer(value):
        return along_z.send(value, [(0, 1), (1, 0), (2, 3), (3, 2)])

    def inner(value):
        pairs = []
        for p in range(peers):
            pairs += [(p * n + 1, p * n + 2), (p * n + 2, p * n + 1)]
            pairs += [(p * n + end, (p ^ 1) * n + end) for end in (0, n - 1)]
        return lax.ppermute(value, ("expert", "dp"), pairs)

    def mirror(value):
        return along_z.send(value, [(0, 3), (3, 0), (1, 2), (2, 1)])

    def unless_end(value):
        return jnp.where(at_end, jnp.zeros_like(value), value)

    products, sums, grads = [], [], []

    def send_home(near, far, add):
        near = add(near, across.send(far, swap))
        right, left = along_x.scatter([near[q] for q in range(chips)], add)
        home = near[0].astype(F32) + right.astype(F32)
        return near, home if left is None else home + left.astype(F32)

    if swaps:
        flight, arrived, streams = [None] * STREAMS, None, range(STREAMS)
        slots, parts, _, routes = pre(0, [])
        grad_token = None
        for e in range(local):
            following = e < local - 1
            first, second, totals, halves = [], [], [], []
            for h in streams:
                x = parts[h]
                if e == 0:
                    first.append((outer(x[3]), None))
                else:
                    y, got_a, got_b = flight[h]
                    first.append((outer(jnp.where(at_end, x[3], got_b)), inner(got_a)))
            seen = [[] for _ in streams]
            if following:
                next_slots, next_parts, token, _ = pre(e + 1, [] if e == 0 else [flight[1][2]])
                seen[0 if e == 0 else STREAMS - 1].append(token)
            if grad_token is not None:
                seen[0].append(grad_token)
            for h in streams:
                x, (a1, b1) = parts[h], first[h]
                send_a2 = x[2] if e == 0 else jnp.where(at_end, x[2], b1)
                second.append((outer(send_a2), inner(add(x[3], a1, seen[h]))))
                if e > 0:
                    y, got_a, got_b = flight[h]
                    halves.append([(y,), (got_a,), (a1, got_b), (second[h][0], b1)])
            for h in streams:
                x, (a2, b2) = parts[h], second[h]
                a3 = outer(jnp.where(at_end, x[1], add_rounded(x[1], b2)))
                b3 = inner(unless_end(add_rounded(x[2], a2)))
                totals.append((x[0], a3, b3))
            wait = []
            if e > 0:
                *sums, out_token = out(e - 1, halves, sums, [])
                wait = [out_token]
            for h in streams:
                y, product = mid(e, h, totals[h], products, wait if h == 0 else [])
                products.append(product)
                flight[h] = (y, outer(y), inner(y))
            if e > 0:
                *grads, grad_token = grad(e - 1, arrived, halves, grads, [flight[-1][0]])
            arrived = slots
            if following:
                slots, parts = next_slots, next_parts
        halves = []
        for h in streams:
            y, got_a, got_b = flight[h]
            a1, far_end = outer(got_b), mirror(jnp.where(at_end, y, got_a))
            halves.append([(y,), (got_a,), (a1, got_b), (far_end,)])
        wait = [grad_token]
    else:
        begun = []
        for e in range(local):
            slots, parts, _, routes = pre(e, [])
            begun.append((slots, [(x[0], *along_z.scatter(x, add_rounded)) for x in parts]))
        for e in range(local):
            halves, arrived, wait = [], begun[e][0], []
            for h in range(STREAMS):
                y, product = mid(e, h, begun[e][1][h], products)
                products.append(product)
                halves.append([(y,)] + along_z.gather(y))
            if e < local - 1:
                *sums, _ = out(e, halves, sums, [])
                *grads, _ = grad(e, arrived, halves, grads, [])

    near, far, _, near_p, far_p = out(local - 1, halves, sums, wait)
    hop, home = send_home(near, far, add_rounded)
    _, per_expert = send_home(near_p, far_p, lambda a, b: add(a, b, [hop]))
    *grads, _ = grad(local - 1, arrived, halves, grads, [hop])
    combine_grad = jnp.sum(jnp.where(named, per_expert[None], 0.0), axis=1) / combine_t
    return (home[0].astype(BF16), home[1].astype(BF16), *grads, combine_grad.T)


def solution(mesh):
    return jax.shard_map(
        body,
        mesh=mesh,
        in_specs=(
            P(("group", "expert"), "dp"),
            P(("group", "expert"), None),
            P(("group", "expert"), None),
            P("expert", "dp", None),
            P("expert", "dp", None),
            P("expert", None, "dp"),
            P(("group", "expert"), "dp"),
        ),
        out_specs=(
            P(("group", "expert"), "dp"),
            P(("group", "expert"), "dp"),
            P(("group", "expert"), "dp", None),
            P(("group", "expert"), "dp", None),
            P(("group", "expert"), None, "dp"),
            P(("group", "expert"), None),
        ),
        check_vma=False,
    )
```
